128 devices in a mesh: node: 16 (over x, z), local: 8 (over y, core).
Axes of the slice: x: 4, y: 4, z: 4, core: 2. Of those that a mesh axis runs over, the one named last changes fastest.
Arguments:
- tokens: bfloat16 [2048, 7168], P(('node', 'local')), may hold values from -6 to 6
- out_grads: bfloat16 [2048, 7168], P(('node', 'local')), may hold values from -0.59765625 to 0.59765625
- routes: int32 [2048, 8], P(('node', 'local')), may hold values from 0 to 63, as said below
- gate_values: float32 [2048, 8], P(('node', 'local')), may hold values from 0.1 to 1
- gate_weight: bfloat16 [128, 7168, 512], P(('node', 'local')), may hold values from -0.0625 to 0.0625
- up_weight: bfloat16 [128, 7168, 512], P(('node', 'local')), may hold values from -0.0625 to 0.0625
- down_weight: bfloat16 [128, 512, 7168], P(('node', 'local')), may hold values from -0.1875 to 0.1875
Outputs:
- input_grads: bfloat16 [2048, 7168], P(('node', 'local'))
- gate_grads: float32 [2048, 8], P(('node', 'local'))
The draws below stay inside these ranges and needn't reach their ends.
Inputs may be any that keep to these rules, and one draw needn't show every extreme that they name: `routes`: each row names 8 different experts, 2 from each of 4 different groups (group of e is e // 4). Among the 16 rows of one device, at most 5 rows use a given group and at most 3 rows name a given expert; in every draw some group and some expert reach these bounds from every device.
All inputs are finite; a program needn't handle non-finite values.
Results may differ from the reference program's by a relative error of at most 0.012.
Values may be sent and summed in bfloat16 or wider, within the bound.
No kernel may reach another device: no remote copies, remote signals or barrier semaphores. Data moves between devices by JAX's collectives and lax.ppermute only.
A program may use at most 128 MiB of HBM per device.

```python
import math
import jax
import jax.numpy as jnp
from jax import lax

D = 7168
HID = 1024
HALF = 512
TOPK = 8
NODE_LIMIT = 4
PER_NODE = 2
TOK_DEV = 16
TOKENS = 2048
EXP_NODE = 4
EXPERTS = 64
CAP_NODE = 5
CAP_EXP = 3
N_NODE = 16
N_LOCAL = 8


def draw_routes(key, part):
    key = jax.random.fold_in(key, 7)
    hot_key, dev_base = jax.random.split(key)
    favored_node_index = jax.random.randint(hot_key, (), 0, N_NODE)
    favored_local_expert = jax.random.randint(jax.random.fold_in(hot_key, 1), (), 0, EXP_NODE)
    node_ids = jnp.arange(N_NODE, dtype=jnp.int32)
    local_expert_index = jnp.arange(EXP_NODE, dtype=jnp.int32)

    def one_device(dev_key):
        node_key, local_key = jax.random.split(dev_key)
        node_noise = jax.random.randint(node_key, (TOK_DEV, N_NODE), 0, 4096)
        local_noise = jax.random.randint(local_key, (TOK_DEV, N_NODE, EXP_NODE), 0, 4096)

        def choose(counters, noise_pair):
            node_count, local_count = counters
            node_row, local_row = noise_pair
            node_score = node_row * N_NODE + node_ids + jnp.where(node_ids == favored_node_index, 1 << 24, 0)
            node_score = jnp.where(node_count < CAP_NODE, node_score, -1 - node_ids)
            _, selected_experts = lax.top_k(node_score, NODE_LIMIT)
            local_expert_affinity = local_row[selected_experts] * EXP_NODE + local_expert_index[None, :]
            favored_score_boost = (selected_experts[:, None] == favored_node_index) & (local_expert_index[None, :] == favored_local_expert)
            local_expert_affinity = local_expert_affinity + jnp.where(favored_score_boost, 1 << 24, 0)
            has_room = local_count[selected_experts] < CAP_EXP
            local_expert_affinity = jnp.where(has_room, local_expert_affinity, -1 - local_expert_index[None, :])
            _, pick_ids = lax.top_k(local_expert_affinity, PER_NODE)
            node_mark = (node_ids[None, :] == selected_experts[:, None]).astype(jnp.int32)
            local_mark = jnp.sum((local_expert_index[None, None, :] == pick_ids[:, :, None]).astype(jnp.int32), axis=1)
            node_count = node_count + jnp.sum(node_mark, axis=0)
            local_count = local_count + jnp.sum(node_mark[:, :, None] * local_mark[:, None, :], axis=0)
            expert_row = (selected_experts[:, None] * EXP_NODE + pick_ids).reshape(TOPK)
            return ((node_count, local_count), expert_row)
        zero_state = (jnp.zeros((N_NODE,), jnp.int32), jnp.zeros((N_NODE, EXP_NODE), jnp.int32))
        _, route_rows = lax.scan(choose, zero_state, (node_noise, local_noise))
        return route_rows
    dev_keys = jax.random.split(dev_base, TOKENS // TOK_DEV)
    return jax.vmap(one_device)(dev_keys).reshape(TOKENS, TOPK).astype(jnp.int32)


def block_levels(own_key, extent, shards, low, top_value):
    loudness = 1.0
    for axis_at, blocks in shards:
        draws = jax.random.uniform(jax.random.fold_in(jax.random.fold_in(own_key, 6), axis_at), (blocks,), jnp.float32, low / len(shards), top_value / len(shards))
        loudness = loudness * jnp.repeat(jnp.exp(draws), extent[axis_at] // blocks).reshape((-1,) + (1,) * (len(extent) - 1 - axis_at))
    return loudness


def noise(stream_key, dims, spread, bound, pieces=(), kind=jnp.bfloat16):
    values = jax.random.normal(stream_key, dims, jnp.float32) * spread
    if len(pieces) > 0:
        values = block_levels(stream_key, dims, pieces, -0.22, 0.18) * values
    return jnp.clip(values, min=-bound, max=bound).astype(kind)


def setup_inputs(seed: int = 0) -> dict:
    key_list = jax.random.split(jax.random.key(seed), 8)
    tokens = noise(key_list[0], (TOKENS, D), 1.0, 6.0, ((0, 128),))
    out_grads = noise(key_list[1], (TOKENS, D), 0.1, 0.59765625, ((0, 128),))
    routes = draw_routes(jax.random.fold_in(key_list[7], 71), 0)
    gate_values = jnp.clip(jnp.exp(math.log(1.0) - 2.3025851 * jax.random.uniform(key_list[3], (TOKENS, TOPK), jnp.float32) ** block_levels(key_list[3], (TOKENS, TOPK), ((0, 128),), -0.2, 0.2)), 0.1, 1.0)
    gate_weight = noise(key_list[4], (2 * EXPERTS, D, HALF), D ** -0.5, 0.0625, ((0, 128),))
    up_weight = noise(key_list[5], (2 * EXPERTS, D, HALF), D ** -0.5, 0.0625, ((0, 128),))
    down_weight = noise(key_list[6], (2 * EXPERTS, HALF, D), HID ** -0.5, 0.1875, ((0, 128),))
    return {"tokens": tokens, "out_grads": out_grads, "routes": routes, "gate_values": gate_values, "gate_weight": gate_weight, "up_weight": up_weight, "down_weight": down_weight}


def shard_terms(rows_x, rows_dy, w_gate, w_up, w_down):
    pre_gate = jnp.dot(rows_x, w_gate, preferred_element_type=jnp.float32)
    pre_up = jnp.dot(rows_x, w_up, preferred_element_type=jnp.float32)
    sigmoid_gate = jax.nn.sigmoid(pre_gate)
    activated = pre_gate * sigmoid_gate
    hidden = (activated * pre_up).astype(jnp.bfloat16)
    back_grad = lax.dot_general(rows_dy, w_down, (((1,), (1,)), ((), ())), preferred_element_type=jnp.float32)
    part_gate = jnp.sum(hidden.astype(jnp.float32) * back_grad, axis=1)
    d_gate = (back_grad * pre_up * sigmoid_gate * (1.0 + pre_gate * (1.0 - sigmoid_gate))).astype(jnp.bfloat16)
    d_up = (back_grad * activated).astype(jnp.bfloat16)
    part_dx = lax.dot_general(d_gate, w_gate, (((1,), (1,)), ((), ())), preferred_element_type=jnp.float32)
    part_dx = part_dx + lax.dot_general(d_up, w_up, (((1,), (1,)), ((), ())), preferred_element_type=jnp.float32)
    gate_high = part_gate.astype(jnp.bfloat16)
    gate_low = (part_gate - gate_high.astype(jnp.float32)).astype(jnp.bfloat16)
    return part_dx.astype(jnp.bfloat16), gate_high, gate_low


def reference(tokens, out_grads, routes, gate_values, gate_weight, up_weight, down_weight):
    capacity = N_NODE * N_LOCAL * CAP_EXP

    def one_shard(totals, shard_id):
        dx_sum, gate_sum = totals
        expert = shard_id // 2
        is_routed = routes == expert
        routed = jnp.any(is_routed, axis=1)
        row_index = jnp.nonzero(routed, size=capacity, fill_value=TOKENS)[0].astype(jnp.int32)
        rows_x = jnp.take(tokens, row_index, axis=0, mode="fill", fill_value=0)
        rows_dy = jnp.take(out_grads, row_index, axis=0, mode="fill", fill_value=0)
        w_gate = lax.dynamic_index_in_dim(gate_weight, shard_id, 0, keepdims=False)
        w_up = lax.dynamic_index_in_dim(up_weight, shard_id, 0, keepdims=False)
        w_down = lax.dynamic_index_in_dim(down_weight, shard_id, 0, keepdims=False)
        part_dx, gate_high, gate_low = shard_terms(rows_x, rows_dy, w_gate, w_up, w_down)
        carried = gate_high.astype(jnp.float32) + gate_low.astype(jnp.float32)
        token_gate = jnp.sum(jnp.where(is_routed, gate_values, 0.0), axis=1)
        row_gate = jnp.take(token_gate, row_index, axis=0, mode="fill", fill_value=0)
        dx_sum = dx_sum.at[row_index].add(part_dx.astype(jnp.float32) * row_gate[:, None], mode="drop")
        gate_term = jnp.zeros((TOKENS,), jnp.float32).at[row_index].add(carried, mode="drop")
        gate_sum = gate_sum + jnp.where(is_routed, gate_term[:, None], 0.0)
        return (dx_sum, gate_sum), None

    zero_state = (jnp.zeros((TOKENS, D), jnp.float32), jnp.zeros((TOKENS, TOPK), jnp.float32))
    (dx_sum, gate_sum), _ = lax.scan(one_shard, zero_state, jnp.arange(2 * EXPERTS, dtype=jnp.int32))
    return dx_sum.astype(jnp.bfloat16), gate_sum
```

```python
import functools

import jax
import jax.numpy as jnp
from jax import lax
from jax.experimental import pallas as pl
from jax.experimental.pallas import tpu as pltpu
from jax.sharding import PartitionSpec as P

BF = jnp.bfloat16
F32 = jnp.float32
I32 = jnp.int32

N_NODE = 16
N_Y = 4
TOK = 16
CAP_NODE = 5
CAP_EXP = 3
WIDTH = 7168
HALF = 512
ROWS_Y = N_NODE * CAP_EXP
SLOTS = N_Y * ROWS_Y
ROWS_N = N_NODE * 40
EXT = 128
VMEM_LIMIT = 48 * 1024 * 1024


def iota(shape, dim):
    return lax.broadcasted_iota(I32, shape, dim)


def div3(v):
    return (v * 171) >> 9


def div5(v):
    return (v * 205) >> 10


def div40(v):
    return div5(v >> 3)


def dot(a, b):
    return jnp.dot(a, b, preferred_element_type=F32)


def dot_nt(a, b):
    return lax.dot_general(a, b, (((1,), (1,)), ((), ())), preferred_element_type=F32)


def dot_tn(a, b):
    return lax.dot_general(a, b, (((0,), (0,)), ((), ())), preferred_element_type=F32)


def onehot(mask):
    return jnp.where(mask, 1.0, 0.0)


def route_tables(routes, width):
    lane = iota((TOK, width), 1) & 63
    hot = jnp.zeros((TOK, width), F32)
    for k in range(8):
        hot = hot + onehot(routes[:, k : k + 1] == lane)
    return hot


def node_codes(hot):
    width = hot.shape[1]
    row = iota((width, 128), 0)
    group = onehot((row < 64) & ((row >> 2) == iota((width, 128), 1))).astype(BF)
    used = jnp.minimum(dot(hot.astype(BF), group), 1.0)
    tri = onehot(iota((TOK, TOK), 1) < iota((TOK, TOK), 0)).astype(BF)
    return used * (dot(tri, used.astype(BF)) + 1.0)


def send_dy_kernel(routes_ref, gates_ref, dy_ref, out_ref):
    routes = routes_ref[...]
    gates = gates_ref[...]
    width = 256
    lane = iota((TOK, width), 1)
    hot = route_tables(routes, width)
    gate = jnp.zeros((TOK, width), F32)
    for k in range(8):
        gate = gate + jnp.where(routes[:, k : k + 1] == (lane & 63), gates[:, k : k + 1], 0.0)
    tri = onehot(iota((TOK, TOK), 1) < iota((TOK, TOK), 0)).astype(BF)
    code = hot * (dot(tri, hot.astype(BF)) + 1.0)
    section = lane >> 6
    meta = jnp.where(section == 0, code, jnp.where(section == 1, gate, 0.0)).astype(BF)
    meta = jnp.concatenate([meta, jnp.zeros((TOK, 1024 - width), BF)], axis=1)
    stack = jnp.concatenate([dy_ref[:, 1024 * q : 1024 * (q + 1)] for q in range(7)] + [meta], axis=0)
    ncode = node_codes(hot)
    spread = onehot((iota((TOK, 128), 1) & 15) == iota((TOK, 128), 0)).astype(BF)
    ncode_lane = dot_tn(ncode.astype(BF), spread)[:N_NODE]
    chunk = (iota((N_NODE, 128), 1) >> 4).astype(F32)
    key = jnp.where(ncode_lane > 0.0, 8.0 * chunk + ncode_lane, -1.0)
    row = iota((40, 128), 0)
    q = div5(row)
    row_key = (8 * q + (row - 5 * q) + 1).astype(F32)
    pick = jnp.concatenate([onehot(row_key == key[n : n + 1, :]) for n in range(N_NODE)], axis=0)
    out_ref[...] = dot(pick.astype(BF), stack).astype(BF)


def send_x_kernel(place_ref, x0_ref, x1_ref, x2_ref, x3_ref, out_ref):
    y = place_ref[1]
    xs = [x0_ref, x1_ref, x2_ref, x3_ref]
    routes = jnp.concatenate([r[:, WIDTH : WIDTH + EXT] for r in xs], axis=0).astype(F32)
    lane = iota((64, 128), 1)
    wanted = jnp.where(lane < N_NODE, 4 * lane + y, -1).astype(F32)
    hot = jnp.zeros((64, 128), F32)
    for k in range(8):
        hot = hot + onehot(routes[:, k : k + 1] == wanted)
    r64 = iota((64, 64), 0)
    c64 = iota((64, 64), 1)
    tri = onehot((c64 < r64) & ((c64 >> 4) == (r64 >> 4))).astype(BF)
    code = hot * (dot(tri, hot.astype(BF)) + 1.0)
    spread = onehot((lane & 63) == iota((64, 128), 0)).astype(BF)
    code_lane = dot_tn(code.astype(BF), spread)[:N_NODE]
    block = (iota((N_NODE, 128), 1) >> 4).astype(F32)
    key = jnp.where(code_lane > 0.0, 4.0 * block + code_lane, -1.0)
    row = iota((24, 128), 0)
    b = div3(row)
    row_key = (4 * b + (row - 3 * b) + 1).astype(F32)
    pick = jnp.concatenate([onehot(row_key == key[n : n + 1, :]) for n in range(N_NODE)], axis=0).astype(BF)
    for i in range(7):
        lo = 512 * i
        stack = jnp.concatenate(
            [r[:, lo : lo + 512] for r in xs] + [r[:, 3584 + lo : 3584 + lo + 512] for r in xs], axis=0
        )
        out_ref[:, lo : lo + 512] = dot(pick, stack).astype(BF)


def regroup_kernel(place_ref, rows_ref, out0_ref, out1_ref, out2_ref, out3_ref, table_ref):
    node = place_ref[0]
    y = place_ref[1]
    outs = [out0_ref, out1_ref, out2_ref, out3_ref]
    c = iota((256, 128), 1)
    want = ((c >> 2) << 6) + 4 * node + ((y + c) & 3)
    select = onehot((c < 8) & (iota((256, 128), 0) == want)).astype(BF)
    meta = rows_ref[:, :256]
    code = lax.dot_general(select, meta, (((0,), (1,)), ((), ())), preferred_element_type=F32)[:8]
    col = iota((8, ROWS_N), 1)
    n = div40(col)
    key = jnp.where((col - 40 * n >= 35) & (code > 0.0), 4.0 * n.astype(F32) + code, -1.0)
    row = iota((ROWS_Y, ROWS_N), 0)
    rn = div3(row)
    row_key = (4 * rn + (row - 3 * rn) + 1).astype(F32)
    for q in range(7):
        key_q = pltpu.roll(key, ROWS_N - (35 - 5 * q), 1)
        pick = jnp.concatenate([onehot(row_key == key_q[s : s + 1, :]) for s in range(N_Y)], axis=0)
        moved = dot(pick.astype(BF), rows_ref[...]).astype(BF)
        for s in range(N_Y):
            outs[s][:, 1024 * q : 1024 * (q + 1)] = moved[ROWS_Y * s : ROWS_Y * (s + 1)]
    picked = dot(meta, select).astype(BF)
    r = iota((ROWS_N, ROWS_N), 0)
    rn = div40(r)
    rp = r - 40 * rn
    source = 40 * rn + 35 + (rp - 5 * div5(rp))
    table_ref[...] = dot(onehot(iota((ROWS_N, ROWS_N), 1) == source).astype(BF), picked)


def back_kernel(*refs):
    pieces, down_ref, out_ref = refs[:8], refs[8], refs[9]

    @pl.when(pl.program_id(0) == 0)
    def _():
        out_ref[...] = jnp.zeros_like(out_ref)

    rows = jnp.concatenate([p[...] for p in pieces], axis=0)
    out_ref[...] += dot_nt(rows, down_ref[...])


def forward_kernel(own_ref, other_ref, gate_ref, up_ref, back_ref, dgate_ref, dup_ref, ext_ref, pg_ref, pu_ref):
    step = pl.program_id(0)

    @pl.when(step == 0)
    def _():
        pg_ref[...] = jnp.zeros_like(pg_ref)
        pu_ref[...] = jnp.zeros_like(pu_ref)

    h = jnp.where(step >= 7, 1, 0)
    row = iota((SLOTS, 384), 0)
    s = div3(row >> 4)
    rem = row - ROWS_Y * s
    n = div3(rem)
    r = rem - 3 * n
    perm = onehot(iota((SLOTS, 384), 1) == 24 * n + 12 * h + 3 * s + r).astype(BF)
    rows = jnp.concatenate(
        [dot(perm, own_ref[...]).astype(BF), dot(perm, other_ref[...]).astype(BF)], axis=0
    )
    pg_ref[...] += dot(rows, gate_ref[...])
    pu_ref[...] += dot(rows, up_ref[...])

    @pl.when(step == 13)
    def _():
        pre_gate = pg_ref[...]
        pre_up = pu_ref[...]
        back = back_ref[...]
        sig = jax.nn.sigmoid(pre_gate)
        act = pre_gate * sig
        hidden = (act * pre_up).astype(BF)
        part = jnp.sum(hidden.astype(F32) * back, axis=1, keepdims=True)
        dgate_ref[...] = (back * pre_up * sig * (1.0 + pre_gate * (1.0 - sig))).astype(BF)
        dup_ref[...] = (back * act).astype(BF)
        high = part.astype(BF).astype(F32)
        low = part - high
        slot = iota((2 * SLOTS, EXT), 0)
        slot = jnp.where(slot >= SLOTS, slot - SLOTS, slot)
        at = 2 * div3(slot >> 4)
        lane = iota((2 * SLOTS, EXT), 1)
        ext_ref[...] = jnp.where(lane == at, high, jnp.where(lane == at + 1, low, 0.0)).astype(BF)


def dx_kernel(dgate_ref, dup_ref, gate_ref, up_ref, ext_ref, own_ref, other_ref):
    step = pl.program_id(0)
    part = (dot_nt(dgate_ref[...], gate_ref[...]) + dot_nt(dup_ref[...], up_ref[...])).astype(BF)
    at = pl.multiple_of(step * 512, 512)
    own_ref[:, pl.ds(at, 512)] = part[:SLOTS]
    other_ref[:, pl.ds(at, 512)] = part[SLOTS:]

    @pl.when(step == 0)
    def _():
        own_ref[:, 3584:] = ext_ref[:SLOTS]
        other_ref[:, 3584:] = ext_ref[SLOTS:]


def add_kernel(own_ref, got_ref, *outs):
    lane = iota((ROWS_Y, EXT), 1)
    for s in range(N_Y):
        rows = slice(ROWS_Y * s, ROWS_Y * (s + 1))
        total = own_ref[rows, :3584].astype(F32) + got_ref[rows, :3584].astype(F32)
        outs[s][:, :3584] = total.astype(BF)
        term = jnp.sum(
            own_ref[rows, 3584:].astype(F32) + got_ref[rows, 3584:].astype(F32), axis=1, keepdims=True
        )
        high = term.astype(BF).astype(F32)
        low = term - high
        outs[s][:, 3584:] = jnp.where(
            lane == 2 * s, high, jnp.where(lane == 2 * s + 1, low, 0.0)
        ).astype(BF)


def combine_kernel(table_ref, p0_ref, p1_ref, p2_ref, p3_ref, out_ref):
    pieces = [p0_ref, p1_ref, p2_ref, p3_ref]
    lane = iota((ROWS_N, SLOTS), 1)
    ls = div3(lane >> 4)
    rem = lane - ROWS_Y * ls
    ln = div3(rem)
    lr = rem - 3 * ln
    row = iota((ROWS_N, SLOTS), 0)
    rn = div40(row)
    rq = div5(row - 40 * rn)
    table = table_ref[...]
    code = jnp.zeros((ROWS_N, SLOTS), F32)
    gate = jnp.zeros((ROWS_N, SLOTS), F32)
    for s in range(N_Y):
        code = jnp.where(ls == s, table[:, s : s + 1], code)
        gate = jnp.where(ls == s, table[:, 4 + s : 5 + s], gate)
    match = (rn == ln) & (code == (lr + 1).astype(F32))
    weight = jnp.where(match, gate, 0.0)
    total = jnp.zeros((ROWS_N, 512), F32)
    for q in range(7):
        rows = jnp.concatenate([p[:, 512 * q : 512 * (q + 1)] for p in pieces], axis=0)
        total = total + dot(jnp.where(rq == q, weight, 0.0).astype(BF), rows)
    ext = jnp.concatenate([p[:, 3584:] for p in pieces], axis=0)
    terms = dot(onehot(match & (rq == 7)).astype(BF), ext)
    out_ref[:, :EXT] = (total[:, :EXT] + terms).astype(BF)
    out_ref[:, EXT:] = total[:, EXT:].astype(BF)


def finish_kernel(place_ref, routes_ref, a_ref, b_ref, dx_ref, gg_ref):
    y = place_ref[1]
    routes = routes_ref[...]
    ncode = node_codes(route_tables(routes, 128))
    col = iota((128, ROWS_N), 1)
    spread = onehot(div40(col) == iota((128, ROWS_N), 0)).astype(BF)
    code = dot(ncode.astype(BF), spread)
    col = iota((TOK, ROWS_N), 1)
    cn = div40(col)
    cp = col - 40 * cn
    cq = div5(cp)
    match = code == (cp - 5 * cq + 1).astype(F32)
    for q in range(7):
        pick = onehot(match & (cq == q)).astype(BF)
        dx_ref[:, 512 * q : 512 * (q + 1)] = dot(pick, a_ref[...]).astype(BF)
        dx_ref[:, 3584 + 512 * q : 3584 + 512 * (q + 1)] = dot(pick, b_ref[...]).astype(BF)
    last = match & (cq == 7)
    masks = jnp.concatenate(
        [onehot(last & (cn == (routes[:, k : k + 1] >> 2))) for k in range(8)], axis=0
    ).astype(BF)
    terms = dot(masks, a_ref[:, :EXT])
    lane = iota((TOK, EXT), 1)
    result = jnp.zeros((TOK, EXT), F32)
    for k in range(8):
        s = ((routes[:, k : k + 1] & 3) - y) & 3
        mine = jnp.where((lane >> 1) == s, terms[TOK * k : TOK * (k + 1)], 0.0)
        result = jnp.where(lane == k, jnp.sum(mine, axis=1, keepdims=True), result)
    gg_ref[...] = result[:, :8]


SMEM = pl.BlockSpec(memory_space=pltpu.SMEM)
VM = pl.BlockSpec(memory_space=pltpu.VMEM)
PARAMS = pltpu.CompilerParams(vmem_limit_bytes=VMEM_LIMIT)


def sds(shape, dtype=BF):
    return jax.ShapeDtypeStruct(shape, dtype)


def whole(kernel, out_shape, in_specs, name):
    multi = isinstance(out_shape, (list, tuple))
    return pl.pallas_call(
        kernel,
        out_shape=out_shape,
        in_specs=in_specs,
        out_specs=[VM] * len(out_shape) if multi else VM,
        compiler_params=PARAMS,
        name=name,
    )


def shift_y(v, s):
    return lax.ppermute(v, "local", [(i, (i + 2 * s) % 8) for i in range(8)])


def swap_core(v):
    return lax.ppermute(v, "local", [(i, i ^ 1) for i in range(8)])


def node_exchange(v):
    shape = v.shape
    v = v.reshape(N_NODE, shape[0] // N_NODE, shape[1])
    return lax.all_to_all(v, "node", split_axis=0, concat_axis=0, tiled=True).reshape(shape)


def on_device(tokens, out_grads, routes, gate_values, gate_weight, up_weight, down_weight):
    w_gate = gate_weight[0]
    w_up = up_weight[0]
    w_down = down_weight[0]
    place = jnp.stack([lax.axis_index("node"), lax.axis_index("local") // 2]).astype(I32)

    x_own = jnp.concatenate([tokens, jnp.pad(routes.astype(BF), ((0, 0), (0, EXT - 8)))], axis=1)
    x_near = [x_own] + [shift_y(x_own, s) for s in (1, 2, 3)]

    dy_send = whole(send_dy_kernel, sds((ROWS_N, 1024)), [VM] * 3, "send_dy")(
        routes, gate_values, out_grads
    )
    dy_mid = node_exchange(dy_send)
    x_send = whole(send_x_kernel, sds((384, 3584)), [SMEM] + [VM] * 4, "send_x")(place, *x_near)
    x_mine = node_exchange(x_send)

    *dy_out, table = whole(
        regroup_kernel,
        [sds((ROWS_Y, WIDTH))] * 4 + [sds((ROWS_N, 128), F32)],
        [SMEM, VM],
        "regroup",
    )(place, dy_mid)
    dy_mine = [dy_out[0]] + [shift_y(dy_out[s], s) for s in (1, 2, 3)]
    dy_other = [swap_core(v) for v in dy_mine]
    x_other = swap_core(x_mine)

    back = pl.pallas_call(
        back_kernel,
        grid=(7,),
        out_shape=sds((2 * SLOTS, HALF), F32),
        in_specs=[pl.BlockSpec((ROWS_Y, 1024), lambda i: (0, i))] * 8
        + [pl.BlockSpec((HALF, 1024), lambda i: (0, i))],
        out_specs=pl.BlockSpec((2 * SLOTS, HALF), lambda i: (0, 0)),
        compiler_params=PARAMS,
        name="back",
    )(*dy_mine, *dy_other, w_down)

    full = lambda shape: pl.BlockSpec(shape, lambda i: (0, 0))
    d_gate, d_up, ext = pl.pallas_call(
        forward_kernel,
        grid=(14,),
        out_shape=[sds((2 * SLOTS, HALF)), sds((2 * SLOTS, HALF)), sds((2 * SLOTS, EXT))],
        in_specs=[pl.BlockSpec((384, 512), lambda i: (0, lax.rem(i, 7)))] * 2
        + [pl.BlockSpec((512, HALF), lambda i: (i, 0))] * 2
        + [full((2 * SLOTS, HALF))],
        out_specs=[full((2 * SLOTS, HALF)), full((2 * SLOTS, HALF)), full((2 * SLOTS, EXT))],
        scratch_shapes=[pltpu.VMEM((2 * SLOTS, HALF), F32)] * 2,
        compiler_params=PARAMS,
        name="forward",
    )(x_mine, x_other, w_gate, w_up, back)

    halves = []
    for part in range(2):
        rows = pl.BlockSpec((512, HALF), functools.partial(lambda p, i: (7 * p + i, 0), part))
        own, other = pl.pallas_call(
            dx_kernel,
            grid=(7,),
            out_shape=[sds((SLOTS, 3584 + EXT))] * 2,
            in_specs=[full((2 * SLOTS, HALF))] * 2 + [rows] * 2 + [full((2 * SLOTS, EXT))],
            out_specs=[full((SLOTS, 3584 + EXT))] * 2,
            compiler_params=PARAMS,
            name="dx",
        )(d_gate, d_up, w_gate, w_up, ext)
        got = swap_core(other)
        pieces = whole(add_kernel, [sds((ROWS_Y, 3584 + EXT))] * 4, [VM] * 2, "add_halves")(own, got)
        pieces = [pieces[0]] + [shift_y(pieces[s], -s) for s in (1, 2, 3)]
        mixed = whole(combine_kernel, sds((ROWS_N, 512)), [VM] * 5, "combine")(table, *pieces)
        halves.append(node_exchange(mixed))

    return tuple(
        whole(
            finish_kernel, [sds((TOK, WIDTH)), sds((TOK, 8), F32)], [SMEM] + [VM] * 3, "finish"
        )(place, routes, *halves)
    )


def solution(mesh):
    row = P(("node", "local"), None)
    weight = P(("node", "local"), None, None)
    return jax.shard_map(
        on_device,
        mesh=mesh,
        in_specs=(row, row, row, row, weight, weight, weight),
        out_specs=(row, row),
        check_vma=False,
    )
```

```python
import functools

import jax
import jax.numpy as jnp
from jax import lax
from jax.experimental import pallas as pl
from jax.experimental.pallas import tpu as pltpu
from jax.sharding import PartitionSpec as P

BF = jnp.bfloat16
F32 = jnp.float32
I32 = jnp.int32

N_NODE = 16
N_Y = 4
TOK = 16
CAP_NODE = 5
CAP_EXP = 3
WIDTH = 7168
HALF = 512
ROWS_Y = N_NODE * CAP_EXP
SLOTS = N_Y * ROWS_Y
ROWS_N = N_NODE * 40
EXT = 128
VMEM_LIMIT = 36 * 1024 * 1024


def iota(shape, dim):
    return lax.broadcasted_iota(I32, shape, dim)


def div3(v):
    return (v * 171) >> 9


def div5(v):
    return (v * 205) >> 10


def div40(v):
    return div5(v >> 3)


def dot(a, b):
    return jnp.dot(a, b, preferred_element_type=F32)


def dot_nt(a, b):
    return lax.dot_general(a, b, (((1,), (1,)), ((), ())), preferred_element_type=F32)


def dot_tn(a, b):
    return lax.dot_general(a, b, (((0,), (0,)), ((), ())), preferred_element_type=F32)


def onehot(mask):
    return jnp.where(mask, 1.0, 0.0)


def route_tables(routes, width):
    lane = iota((TOK, width), 1) & 63
    hot = jnp.zeros((TOK, width), F32)
    for k in range(8):
        hot = hot + onehot(routes[:, k : k + 1] == lane)
    return hot


def node_codes(hot):
    width = hot.shape[1]
    row = iota((width, 128), 0)
    group = onehot((row < 64) & ((row >> 2) == iota((width, 128), 1))).astype(BF)
    used = jnp.minimum(dot(hot.astype(BF), group), 1.0)
    tri = onehot(iota((TOK, TOK), 1) < iota((TOK, TOK), 0)).astype(BF)
    return used * (dot(tri, used.astype(BF)) + 1.0)


def send_dy_kernel(routes_ref, gates_ref, dy_ref, out_ref):
    routes = routes_ref[...]
    gates = gates_ref[...]
    width = 256
    lane = iota((TOK, width), 1)
    hot = route_tables(routes, width)
    gate = jnp.zeros((TOK, width), F32)
    for k in range(8):
        gate = gate + jnp.where(routes[:, k : k + 1] == (lane & 63), gates[:, k : k + 1], 0.0)
    tri = onehot(iota((TOK, TOK), 1) < iota((TOK, TOK), 0)).astype(BF)
    code = hot * (dot(tri, hot.astype(BF)) + 1.0)
    section = lane >> 6
    meta = jnp.where(section == 0, code, jnp.where(section == 1, gate, 0.0)).astype(BF)
    meta = jnp.concatenate([meta, jnp.zeros((TOK, 1024 - width), BF)], axis=1)
    stack = jnp.concatenate([dy_ref[:, 1024 * q : 1024 * (q + 1)] for q in range(7)] + [meta], axis=0)
    ncode = node_codes(hot)
    spread = onehot((iota((TOK, 128), 1) & 15) == iota((TOK, 128), 0)).astype(BF)
    ncode_lane = dot_tn(ncode.astype(BF), spread)[:N_NODE]
    chunk = (iota((N_NODE, 128), 1) >> 4).astype(F32)
    key = jnp.where(ncode_lane > 0.0, 8.0 * chunk + ncode_lane, -1.0)
    row = iota((40, 128), 0)
    q = div5(row)
    row_key = (8 * q + (row - 5 * q) + 1).astype(F32)
    pick = jnp.concatenate([onehot(row_key == key[n : n + 1, :]) for n in range(N_NODE)], axis=0)
    out_ref[...] = dot(pick.astype(BF), stack).astype(BF)


def send_x_kernel(place_ref, x0_ref, x1_ref, x2_ref, x3_ref, out_ref):
    y = place_ref[1]
    xs = [x0_ref, x1_ref, x2_ref, x3_ref]
    code, _ = near_tables(y, xs)
    lane = iota((64, 128), 1)
    spread = onehot((lane & 63) == iota((64, 128), 0)).astype(BF)
    code_lane = dot_tn(code.astype(BF), spread)[:N_NODE]
    block = (iota((N_NODE, 128), 1) >> 4).astype(F32)
    key = jnp.where(code_lane > 0.0, 4.0 * block + code_lane, -1.0)
    row = iota((24, 128), 0)
    b = div3(row)
    row_key = (4 * b + (row - 3 * b) + 1).astype(F32)
    pick = jnp.concatenate([onehot(row_key == key[n : n + 1, :]) for n in range(N_NODE)], axis=0).astype(BF)
    for i in range(7):
        lo = 512 * i
        stack = jnp.concatenate(
            [r[:, lo : lo + 512] for r in xs] + [r[:, 3584 + lo : 3584 + lo + 512] for r in xs], axis=0
        )
        out_ref[:, lo : lo + 512] = dot(pick, stack).astype(BF)


def regroup_kernel(place_ref, rows_ref, out0_ref, out1_ref, out2_ref, out3_ref, table_ref):
    node = place_ref[0]
    y = place_ref[1]
    outs = [out0_ref, out1_ref, out2_ref, out3_ref]
    c = iota((256, 128), 1)
    want = ((c >> 2) << 6) + 4 * node + ((y + c) & 3)
    select = onehot((c < 8) & (iota((256, 128), 0) == want)).astype(BF)
    meta = rows_ref[:, :256]
    code = lax.dot_general(select, meta, (((0,), (1,)), ((), ())), preferred_element_type=F32)[:8]
    col = iota((8, ROWS_N), 1)
    n = div40(col)
    key = jnp.where((col - 40 * n >= 35) & (code > 0.0), 4.0 * n.astype(F32) + code, -1.0)
    row = iota((ROWS_Y, ROWS_N), 0)
    rn = div3(row)
    row_key = (4 * rn + (row - 3 * rn) + 1).astype(F32)
    for q in range(7):
        key_q = pltpu.roll(key, ROWS_N - (35 - 5 * q), 1)
        pick = jnp.concatenate([onehot(row_key == key_q[s : s + 1, :]) for s in range(N_Y)], axis=0)
        moved = dot(pick.astype(BF), rows_ref[...]).astype(BF)
        for s in range(N_Y):
            outs[s][:, 1024 * q : 1024 * (q + 1)] = moved[ROWS_Y * s : ROWS_Y * (s + 1)]
    picked = dot(meta, select).astype(BF)
    r = iota((ROWS_N, ROWS_N), 0)
    rn = div40(r)
    rp = r - 40 * rn
    source = 40 * rn + 35 + (rp - 5 * div5(rp))
    table_ref[...] = dot(onehot(iota((ROWS_N, ROWS_N), 1) == source).astype(BF), picked)


def back_kernel(*refs):
    pieces, down_ref, out_ref = refs[:8], refs[8], refs[9]
    rows = jnp.concatenate([p[...] for p in pieces], axis=0)
    out_ref[...] = dot_nt(rows, down_ref[...])


def forward_kernel(own_ref, other_ref, gate_ref, up_ref, back_ref, dgate_ref, dup_ref, ext_ref, x_ref):
    row = iota((SLOTS, 384), 0)
    s = div3(row >> 4)
    rem = row - ROWS_Y * s
    n = div3(rem)
    r = rem - 3 * n
    for h in range(2):
        perm = onehot(iota((SLOTS, 384), 1) == 24 * n + 12 * h + 3 * s + r).astype(BF)
        x_ref[:SLOTS, 3584 * h : 3584 * (h + 1)] = dot(perm, own_ref[...]).astype(BF)
        x_ref[SLOTS:, 3584 * h : 3584 * (h + 1)] = dot(perm, other_ref[...]).astype(BF)
    pre_gate = dot(x_ref[...], gate_ref[...])
    pre_up = dot(x_ref[...], up_ref[...])
    back = back_ref[...]
    sig = jax.nn.sigmoid(pre_gate)
    act = pre_gate * sig
    hidden = (act * pre_up).astype(BF)
    part = jnp.sum(hidden.astype(F32) * back, axis=1, keepdims=True)
    dgate_ref[...] = (back * pre_up * sig * (1.0 + pre_gate * (1.0 - sig))).astype(BF)
    dup_ref[...] = (back * act).astype(BF)
    high = part.astype(BF).astype(F32)
    low = part - high
    slot = iota((2 * SLOTS, EXT), 0)
    slot = jnp.where(slot >= SLOTS, slot - SLOTS, slot)
    at = 2 * div3(slot >> 4)
    lane = iota((2 * SLOTS, EXT), 1)
    ext_ref[...] = jnp.where(lane == at, high, jnp.where(lane == at + 1, low, 0.0)).astype(BF)


def dx_kernel(part, dgate_ref, dup_ref, gate_ref, up_ref, ext_ref, own_ref, other_ref):
    cols = slice(3584 * part, 3584 * (part + 1))
    out = (dot_nt(dgate_ref[...], gate_ref[cols, :]) + dot_nt(dup_ref[...], up_ref[cols, :])).astype(BF)
    own_ref[:, :3584] = out[:SLOTS]
    other_ref[:, :3584] = out[SLOTS:]
    if part == 0:
        own_ref[:, 3584:] = ext_ref[:SLOTS]
        other_ref[:, 3584:] = ext_ref[SLOTS:]


def add_kernel(own_ref, got_ref, *outs):
    lane = iota((ROWS_Y, EXT), 1)
    for s in range(N_Y):
        rows = slice(ROWS_Y * s, ROWS_Y * (s + 1))
        total = own_ref[rows, :3584].astype(F32) + got_ref[rows, :3584].astype(F32)
        outs[s][:, :3584] = total.astype(BF)
        term = jnp.sum(
            own_ref[rows, 3584:].astype(F32) + got_ref[rows, 3584:].astype(F32), axis=1, keepdims=True
        )
        high = term.astype(BF).astype(F32)
        low = term - high
        outs[s][:, 3584:] = jnp.where(
            lane == 2 * s, high, jnp.where(lane == 2 * s + 1, low, 0.0)
        ).astype(BF)


def add_to_nodes_kernel(own_ref, got_ref, out_ref):
    row = iota((384, 384), 0)
    block = div3(row >> 3)
    rest = row - 24 * block
    h = jnp.where(rest >= 12, 1, 0)
    rest = rest - 12 * h
    s = div3(rest)
    source = SLOTS * h + ROWS_Y * s + 3 * block + (rest - 3 * s)
    perm = onehot(iota((384, 384), 1) == source).astype(BF)
    total = (own_ref[...].astype(F32) + got_ref[...].astype(F32)).astype(BF)
    out_ref[...] = dot(perm, jnp.concatenate([total[:, :1792], total[:, 1792:]], axis=0)).astype(BF)


def near_tables(y, xs):
    meta = jnp.concatenate([r[:, WIDTH : WIDTH + EXT] for r in xs], axis=0).astype(F32)
    lane = iota((64, 128), 1)
    wanted = jnp.where(lane < N_NODE, 4 * lane + y, -1).astype(F32)
    hot = jnp.zeros((64, 128), F32)
    gate = jnp.zeros((64, 128), F32)
    for k in range(8):
        here = meta[:, k : k + 1] == wanted
        hot = hot + onehot(here)
        gate = gate + jnp.where(here, meta[:, 8 + k : 9 + k], 0.0)
    r64 = iota((64, 64), 0)
    c64 = iota((64, 64), 1)
    tri = onehot((c64 < r64) & ((c64 >> 4) == (r64 >> 4))).astype(BF)
    return hot * (dot(tri, hot.astype(BF)) + 1.0), gate


def combine_near_kernel(place_ref, x0_ref, x1_ref, x2_ref, x3_ref, rows_ref, *outs):
    code, gate = near_tables(place_ref[1], [x0_ref, x1_ref, x2_ref, x3_ref])
    col = iota((128, 384), 1)
    spread = onehot(div3(col >> 3) == iota((128, 384), 0)).astype(BF)
    code = dot(code.astype(BF), spread)
    gate = dot(gate.astype(BF), spread)
    col = iota((64, 384), 1)
    rest = col - 24 * div3(col >> 3)
    half = jnp.where(rest >= 12, 1, 0)
    rest = rest - 12 * half
    s = div3(rest)
    match = (s == (iota((64, 384), 0) >> 4)) & (code == (rest - 3 * s + 1).astype(F32))
    for h in range(2):
        weight = jnp.where(match & (half == h), gate, 0.0).astype(BF)
        total = dot(weight, rows_ref[...]).astype(BF)
        for s in range(N_Y):
            outs[s][:, 1792 * h : 1792 * (h + 1)] = total[TOK * s : TOK * (s + 1)]


def combine_kernel(table_ref, p0_ref, p1_ref, p2_ref, p3_ref, out_ref):
    pieces = [p0_ref, p1_ref, p2_ref, p3_ref]
    lane = iota((ROWS_N, SLOTS), 1)
    ls = div3(lane >> 4)
    rem = lane - ROWS_Y * ls
    ln = div3(rem)
    lr = rem - 3 * ln
    row = iota((ROWS_N, SLOTS), 0)
    rn = div40(row)
    rq = div5(row - 40 * rn)
    table = table_ref[...]
    code = jnp.zeros((ROWS_N, SLOTS), F32)
    gate = jnp.zeros((ROWS_N, SLOTS), F32)
    for s in range(N_Y):
        code = jnp.where(ls == s, table[:, s : s + 1], code)
        gate = jnp.where(ls == s, table[:, 4 + s : 5 + s], gate)
    match = (rn == ln) & (code == (lr + 1).astype(F32))
    weight = jnp.where(match, gate, 0.0)
    total = jnp.zeros((ROWS_N, 512), F32)
    for q in range(7):
        rows = jnp.concatenate([p[:, 512 * q : 512 * (q + 1)] for p in pieces], axis=0)
        total = total + dot(jnp.where(rq == q, weight, 0.0).astype(BF), rows)
    ext = jnp.concatenate([p[:, 3584:] for p in pieces], axis=0)
    terms = dot(onehot(match & (rq == 7)).astype(BF), ext)
    out_ref[:, :EXT] = (total[:, :EXT] + terms).astype(BF)
    out_ref[:, EXT:] = total[:, EXT:].astype(BF)


def finish_kernel(place_ref, routes_ref, a_ref, b0_ref, b1_ref, b2_ref, b3_ref, dx_ref, gg_ref):
    y = place_ref[1]
    routes = routes_ref[...]
    ncode = node_codes(route_tables(routes, 128))
    col = iota((128, ROWS_N), 1)
    spread = onehot(div40(col) == iota((128, ROWS_N), 0)).astype(BF)
    code = dot(ncode.astype(BF), spread)
    col = iota((TOK, ROWS_N), 1)
    cn = div40(col)
    cp = col - 40 * cn
    cq = div5(cp)
    match = code == (cp - 5 * cq + 1).astype(F32)
    for q in range(7):
        pick = onehot(match & (cq == q)).astype(BF)
        dx_ref[:, 512 * q : 512 * (q + 1)] = dot(pick, a_ref[...]).astype(BF)
    total = b0_ref[...].astype(F32) + b1_ref[...].astype(F32)
    total = total + b2_ref[...].astype(F32) + b3_ref[...].astype(F32)
    dx_ref[:, 3584:] = total.astype(BF)
    last = match & (cq == 7)
    masks = jnp.concatenate(
        [onehot(last & (cn == (routes[:, k : k + 1] >> 2))) for k in range(8)], axis=0
    ).astype(BF)
    terms = dot(masks, a_ref[:, :EXT])
    lane = iota((TOK, EXT), 1)
    result = jnp.zeros((TOK, EXT), F32)
    for k in range(8):
        s = ((routes[:, k : k + 1] & 3) - y) & 3
        mine = jnp.where((lane >> 1) == s, terms[TOK * k : TOK * (k + 1)], 0.0)
        result = jnp.where(lane == k, jnp.sum(mine, axis=1, keepdims=True), result)
    gg_ref[...] = result[:, :8]


SMEM = pl.BlockSpec(memory_space=pltpu.SMEM)
VM = pl.BlockSpec(memory_space=pltpu.VMEM)
PARAMS = pltpu.CompilerParams(vmem_limit_bytes=VMEM_LIMIT)


def sds(shape, dtype=BF):
    return jax.ShapeDtypeStruct(shape, dtype)


def whole(kernel, out_shape, in_specs, name, scratch=()):
    multi = isinstance(out_shape, (list, tuple))
    return pl.pallas_call(
        kernel,
        out_shape=out_shape,
        in_specs=in_specs,
        out_specs=[VM] * len(out_shape) if multi else VM,
        scratch_shapes=list(scratch),
        compiler_params=PARAMS,
        name=name,
    )


def shift_y(v, s):
    return lax.ppermute(v, "local", [(i, (i + 2 * s) % 8) for i in range(8)])


def swap_core(v):
    return lax.ppermute(v, "local", [(i, i ^ 1) for i in range(8)])


def node_exchange(v):
    shape = v.shape
    v = v.reshape(N_NODE, shape[0] // N_NODE, shape[1])
    return lax.all_to_all(v, "node", split_axis=0, concat_axis=0, tiled=True).reshape(shape)


def on_device(tokens, out_grads, routes, gate_values, gate_weight, up_weight, down_weight):
    w_gate = gate_weight[0]
    w_up = up_weight[0]
    w_down = down_weight[0]
    place = jnp.stack([lax.axis_index("node"), lax.axis_index("local") // 2]).astype(I32)

    dy_send = whole(send_dy_kernel, sds((ROWS_N, 1024)), [VM] * 3, "send_dy")(
        routes, gate_values, out_grads
    )
    dy_send, tokens = lax.optimization_barrier((dy_send, tokens))
    dy_mid = node_exchange(dy_send)
    picks = jnp.concatenate([routes.astype(BF), gate_values.astype(BF)], axis=1)
    x_own = jnp.concatenate([tokens, jnp.pad(picks, ((0, 0), (0, EXT - 16)))], axis=1)
    x_near = [x_own] + [shift_y(x_own, s) for s in (1, 2, 3)]

    x_send = whole(send_x_kernel, sds((384, 3584)), [SMEM] + [VM] * 4, "send_x")(place, *x_near)
    *dy_out, table = whole(
        regroup_kernel,
        [sds((ROWS_Y, WIDTH))] * 4 + [sds((ROWS_N, 128), F32)],
        [SMEM, VM],
        "regroup",
    )(place, dy_mid)
    x_send, table = lax.optimization_barrier((x_send, table))
    x_mine = node_exchange(x_send)
    dy_mine = [dy_out[0]] + [shift_y(dy_out[s], s) for s in (1, 2, 3)]
    dy_other = [swap_core(v) for v in dy_mine]

    back = whole(back_kernel, sds((2 * SLOTS, HALF), F32), [VM] * 9, "back")(
        *dy_mine, *dy_other, w_down
    )
    x_mine, back = lax.optimization_barrier((x_mine, back))
    x_other = swap_core(x_mine)
    d_gate, d_up, ext = whole(
        forward_kernel,
        [sds((2 * SLOTS, HALF)), sds((2 * SLOTS, HALF)), sds((2 * SLOTS, EXT))],
        [VM] * 5,
        "forward",
        [pltpu.VMEM((2 * SLOTS, WIDTH), BF)],
    )(x_mine, x_other, w_gate, w_up, back)

    def dx(part, width):
        return whole(
            functools.partial(dx_kernel, part), [sds((SLOTS, width))] * 2, [VM] * 5, "dx"
        )(d_gate, d_up, w_gate, w_up, ext)

    own_a, other_a = dx(0, 3584 + EXT)
    own_b, other_b = dx(1, 3584)
    got_a = swap_core(other_a)
    got_b = swap_core(other_b)
    pieces = whole(add_kernel, [sds((ROWS_Y, 3584 + EXT))] * 4, [VM] * 2, "add_halves")(own_a, got_a)
    pieces = [pieces[0]] + [shift_y(pieces[s], -s) for s in (1, 2, 3)]
    sent_b = whole(add_to_nodes_kernel, sds((384, 1792)), [VM] * 2, "add_to_nodes")(own_b, got_b)
    back_b = node_exchange(sent_b)
    mixed = whole(combine_kernel, sds((ROWS_N, 512)), [VM] * 5, "combine")(table, *pieces)
    mixed, back_b = lax.optimization_barrier((mixed, back_b))
    back_a = node_exchange(mixed)
    near = whole(combine_near_kernel, [sds((TOK, 3584))] * 4, [SMEM] + [VM] * 5, "combine_near")(
        place, *x_near, back_b
    )
    near = [near[0]] + [shift_y(near[s], -s) for s in (1, 2, 3)]
    return tuple(
        whole(
            finish_kernel, [sds((TOK, WIDTH)), sds((TOK, 8), F32)], [SMEM] + [VM] * 6, "finish"
        )(place, routes, back_a, *near)
    )


def solution(mesh):
    row = P(("node", "local"), None)
    weight = P(("node", "local"), None, None)
    return jax.shard_map(
        on_device,
        mesh=mesh,
        in_specs=(row, row, row, row, weight, weight, weight),
        out_specs=(row, row),
        check_vma=False,
    )
```

```python
import functools

import jax
import jax.numpy as jnp
from jax import lax
from jax.experimental import pallas as pl
from jax.experimental.pallas import tpu as pltpu
from jax.sharding import PartitionSpec as P

BF = jnp.bfloat16
F32 = jnp.float32
I32 = jnp.int32

N_NODE = 16
N_Y = 4
TOK = 16
CAP_NODE = 5
CAP_EXP = 3
WIDTH = 7168
HALF = 512
ROWS_Y = N_NODE * CAP_EXP
SLOTS = N_Y * ROWS_Y
ROWS_N = N_NODE * 40
EXT = 128
MIB = 1024 * 1024
VMEM_LIMITS = {"back": 20, "forward_own": 30, "forward": 30, "dx": 24}


def iota(shape, dim):
    return lax.broadcasted_iota(I32, shape, dim)


def div3(v):
    return (v * 171) >> 9


def div5(v):
    return (v * 205) >> 10


def div40(v):
    return div5(v >> 3)


def dot(a, b):
    return jnp.dot(a, b, preferred_element_type=F32)


def dot_nt(a, b):
    return lax.dot_general(a, b, (((1,), (1,)), ((), ())), preferred_element_type=F32)


def dot_tn(a, b):
    return lax.dot_general(a, b, (((0,), (0,)), ((), ())), preferred_element_type=F32)


def onehot(mask):
    return jnp.where(mask, 1.0, 0.0)


def by_token(v):
    return dot_tn(v.astype(F32).astype(BF), onehot(iota((8, 128), 0) == iota((8, 128), 1)).astype(BF))


def route_tables(routes, width):
    lane = (iota((TOK, width), 1) & 63).astype(F32)
    hot = jnp.zeros((TOK, width), F32)
    for k in range(8):
        hot = hot + onehot(routes[:, k : k + 1] == lane)
    return hot


def node_codes(hot):
    width = hot.shape[1]
    row = iota((width, 128), 0)
    group = onehot((row < 64) & ((row >> 2) == iota((width, 128), 1))).astype(BF)
    used = jnp.minimum(dot(hot.astype(BF), group), 1.0)
    tri = onehot(iota((TOK, TOK), 1) < iota((TOK, TOK), 0)).astype(BF)
    return used * (dot(tri, used.astype(BF)) + 1.0)


def send_dy_kernel(routes_ref, gates_ref, dy_ref, out_ref):
    routes = by_token(routes_ref[...])
    gates = by_token(gates_ref[...])
    width = 256
    lane = iota((TOK, width), 1)
    expert = (lane & 63).astype(F32)
    hot = route_tables(routes, width)
    gate = jnp.zeros((TOK, width), F32)
    for k in range(8):
        gate = gate + jnp.where(routes[:, k : k + 1] == expert, gates[:, k : k + 1], 0.0)
    tri = onehot(iota((TOK, TOK), 1) < iota((TOK, TOK), 0)).astype(BF)
    code = hot * (dot(tri, hot.astype(BF)) + 1.0)
    section = lane >> 6
    meta = jnp.where(section == 0, code, jnp.where(section == 1, gate, 0.0)).astype(BF)
    meta = jnp.concatenate([meta, jnp.zeros((TOK, 1024 - width), BF)], axis=1)
    stack = jnp.concatenate([dy_ref[:, 1024 * q : 1024 * (q + 1)] for q in range(7)] + [meta], axis=0)
    ncode = node_codes(hot)
    spread = onehot((iota((TOK, 128), 1) & 15) == iota((TOK, 128), 0)).astype(BF)
    ncode_lane = dot_tn(ncode.astype(BF), spread)[:N_NODE]
    chunk = (iota((N_NODE, 128), 1) >> 4).astype(F32)
    key = jnp.where(ncode_lane > 0.0, 8.0 * chunk + ncode_lane, -1.0)
    row = iota((40, 128), 0)
    q = div5(row)
    row_key = (8 * q + (row - 5 * q) + 1).astype(F32)
    pick = jnp.concatenate([onehot(row_key == key[n : n + 1, :]) for n in range(N_NODE)], axis=0)
    out_ref[...] = dot(pick.astype(BF), stack).astype(BF)


def send_x_kernel(place_ref, x0_ref, x1_ref, x2_ref, x3_ref, out_ref):
    y = place_ref[1]
    xs = [x0_ref, x1_ref, x2_ref, x3_ref]
    code, _ = near_tables(y, xs)
    lane = iota((64, 128), 1)
    spread = onehot((lane & 63) == iota((64, 128), 0)).astype(BF)
    code_lane = dot_tn(code.astype(BF), spread)[:N_NODE]
    block = (iota((N_NODE, 128), 1) >> 4).astype(F32)
    key = jnp.where(code_lane > 0.0, 4.0 * block + code_lane, -1.0)
    row = iota((24, 128), 0)
    b = div3(row)
    row_key = (4 * b + (row - 3 * b) + 1).astype(F32)
    pick = jnp.concatenate([onehot(row_key == key[n : n + 1, :]) for n in range(N_NODE)], axis=0).astype(BF)
    for i in range(7):
        lo = 512 * i
        stack = jnp.concatenate(
            [r[:, lo : lo + 512] for r in xs] + [r[:, 3584 + lo : 3584 + lo + 512] for r in xs], axis=0
        )
        out_ref[:, lo : lo + 512] = dot(pick, stack).astype(BF)


def regroup_kernel(place_ref, rows_ref, out0_ref, out1_ref, out2_ref, out3_ref, table_ref, mark_ref):
    node = place_ref[0]
    y = place_ref[1]
    outs = [out0_ref, out1_ref, out2_ref, out3_ref]
    c = iota((256, 128), 1)
    want = ((c >> 2) << 6) + 4 * node + ((y + c) & 3)
    select = onehot((c < 8) & (iota((256, 128), 0) == want)).astype(BF)
    meta = rows_ref[:, :256]
    mark_ref[...] = jnp.zeros_like(mark_ref)
    code = lax.dot_general(select, meta, (((0,), (1,)), ((), ())), preferred_element_type=F32)[:8]
    col = iota((8, ROWS_N), 1)
    n = div40(col)
    key = jnp.where((col - 40 * n >= 35) & (code > 0.0), 4.0 * n.astype(F32) + code, -1.0)
    row = iota((ROWS_Y, ROWS_N), 0)
    rn = div3(row)
    row_key = (4 * rn + (row - 3 * rn) + 1).astype(F32)
    for q in range(7):
        key_q = pltpu.roll(key, ROWS_N - (35 - 5 * q), 1)
        pick = jnp.concatenate([onehot(row_key == key_q[s : s + 1, :]) for s in range(N_Y)], axis=0)
        moved = dot(pick.astype(BF), rows_ref[...]).astype(BF)
        for s in range(N_Y):
            outs[s][:, 1024 * q : 1024 * (q + 1)] = moved[ROWS_Y * s : ROWS_Y * (s + 1)]
    picked = dot(meta, select).astype(BF)
    r = iota((ROWS_N, ROWS_N), 0)
    rn = div40(r)
    rp = r - 40 * rn
    source = 40 * rn + 35 + (rp - 5 * div5(rp))
    table_ref[...] = dot(onehot(iota((ROWS_N, ROWS_N), 1) == source).astype(BF), picked)


def copy_parts(source, target, sems, first, rows):
    copies = []
    step = rows // sems.shape[0]
    for i in range(sems.shape[0]):
        at = pl.ds(first + step * i, step)
        copies.append(pltpu.make_async_copy(source.at[at], target.at[at], sems.at[i]))
        copies[-1].start()
    return copies


def wait_all(copies):
    for copy in copies:
        copy.wait()


def stage_kernel(source_ref, mark_ref, out_ref, sems):
    wait_all(copy_parts(source_ref, out_ref, sems, 0, source_ref.shape[0]))


def back_kernel(*refs):
    pieces, down_ref, out_ref = refs[:8], refs[8], refs[9]
    rows = jnp.concatenate([p[...] for p in pieces], axis=0)
    out_ref[...] = dot_nt(rows, down_ref[...])


def slot_order(h):
    row = iota((SLOTS, 384), 0)
    s = div3(row >> 4)
    rem = row - ROWS_Y * s
    n = div3(rem)
    r = rem - 3 * n
    return onehot(iota((SLOTS, 384), 1) == 24 * n + 12 * h + 3 * s + r).astype(BF)


def forward_own_kernel(x_ref, gate_hbm, up_hbm, mark_ref, pg_ref, pu_ref, gate_ref, up_ref, sems):
    loads = []
    for h in range(2):
        loads.append(copy_parts(gate_hbm, gate_ref, sems.at[2 * h], 3584 * h, 3584))
        loads.append(copy_parts(up_hbm, up_ref, sems.at[2 * h + 1], 3584 * h, 3584))
    for h in range(2):
        rows = dot(slot_order(h), x_ref[...]).astype(BF)
        at = slice(3584 * h, 3584 * (h + 1))
        wait_all(loads[2 * h])
        gate = dot(rows, gate_ref[at, :])
        wait_all(loads[2 * h + 1])
        up = dot(rows, up_ref[at, :])
        pg_ref[...] = gate if h == 0 else pg_ref[...] + gate
        pu_ref[...] = up if h == 0 else pu_ref[...] + up


def forward_kernel(
    x_ref, gate_ref, up_ref, back_ref, pg_ref, pu_ref, dgate_ref, dup_ref, ext_ref
):
    pre_gate = jnp.zeros((SLOTS, HALF), F32)
    pre_up = jnp.zeros((SLOTS, HALF), F32)
    for h in range(2):
        rows = dot(slot_order(h), x_ref[...]).astype(BF)
        at = slice(3584 * h, 3584 * (h + 1))
        pre_gate = pre_gate + dot(rows, gate_ref[at, :])
        pre_up = pre_up + dot(rows, up_ref[at, :])
    pre_gate = jnp.concatenate([pg_ref[...], pre_gate], axis=0)
    pre_up = jnp.concatenate([pu_ref[...], pre_up], axis=0)
    back = back_ref[...]
    sig = jax.nn.sigmoid(pre_gate)
    act = pre_gate * sig
    hidden = (act * pre_up).astype(BF)
    part = jnp.sum(hidden.astype(F32) * back, axis=1, keepdims=True)
    dgate_ref[...] = (back * pre_up * sig * (1.0 + pre_gate * (1.0 - sig))).astype(BF)
    dup_ref[...] = (back * act).astype(BF)
    high = part.astype(BF).astype(F32)
    low = part - high
    slot = iota((2 * SLOTS, EXT), 0)
    slot = jnp.where(slot >= SLOTS, slot - SLOTS, slot)
    at = 2 * div3(slot >> 4)
    lane = iota((2 * SLOTS, EXT), 1)
    ext_ref[...] = jnp.where(lane == at, high, jnp.where(lane == at + 1, low, 0.0)).astype(BF)


def dx_kernel(part, dgate_ref, dup_ref, gate_ref, up_ref, ext_ref, own_ref, other_ref):
    cols = slice(3584 * part, 3584 * (part + 1))
    out = (dot_nt(dgate_ref[...], gate_ref[cols, :]) + dot_nt(dup_ref[...], up_ref[cols, :])).astype(BF)
    own_ref[:, :3584] = out[:SLOTS]
    other_ref[:, :3584] = out[SLOTS:]
    if part == 0:
        own_ref[:, 3584:] = ext_ref[:SLOTS]
        other_ref[:, 3584:] = ext_ref[SLOTS:]


def add_kernel(own_ref, got_ref, *outs):
    outs[4][...] = jnp.zeros_like(outs[4])
    lane = iota((ROWS_Y, EXT), 1)
    for s in range(N_Y):
        rows = slice(ROWS_Y * s, ROWS_Y * (s + 1))
        total = own_ref[rows, :3584].astype(F32) + got_ref[rows, :3584].astype(F32)
        outs[s][:, :3584] = total.astype(BF)
        term = jnp.sum(
            own_ref[rows, 3584:].astype(F32) + got_ref[rows, 3584:].astype(F32), axis=1, keepdims=True
        )
        high = term.astype(BF).astype(F32)
        low = term - high
        outs[s][:, 3584:] = jnp.where(
            lane == 2 * s, high, jnp.where(lane == 2 * s + 1, low, 0.0)
        ).astype(BF)


def add_to_nodes_kernel(own_ref, got_ref, mark_ref, out_ref):
    row = iota((384, 384), 0)
    block = div3(row >> 3)
    rest = row - 24 * block
    h = jnp.where(rest >= 12, 1, 0)
    rest = rest - 12 * h
    s = div3(rest)
    source = SLOTS * h + ROWS_Y * s + 3 * block + (rest - 3 * s)
    perm = onehot(iota((384, 384), 1) == source).astype(BF)
    total = (own_ref[...].astype(F32) + got_ref[...].astype(F32)).astype(BF)
    out_ref[...] = dot(perm, jnp.concatenate([total[:, :1792], total[:, 1792:]], axis=0)).astype(BF)


def near_tables(y, xs):
    meta = jnp.concatenate([r[:, WIDTH : WIDTH + EXT] for r in xs], axis=0).astype(F32)
    lane = iota((64, 128), 1)
    wanted = jnp.where(lane < N_NODE, 4 * lane + y, -1).astype(F32)
    hot = jnp.zeros((64, 128), F32)
    gate = jnp.zeros((64, 128), F32)
    for k in range(8):
        here = meta[:, k : k + 1] == wanted
        hot = hot + onehot(here)
        gate = gate + jnp.where(here, meta[:, 8 + k : 9 + k], 0.0)
    r64 = iota((64, 64), 0)
    c64 = iota((64, 64), 1)
    tri = onehot((c64 < r64) & ((c64 >> 4) == (r64 >> 4))).astype(BF)
    return hot * (dot(tri, hot.astype(BF)) + 1.0), gate


def combine_near_kernel(place_ref, x0_ref, x1_ref, x2_ref, x3_ref, rows_ref, *outs):
    code, gate = near_tables(place_ref[1], [x0_ref, x1_ref, x2_ref, x3_ref])
    col = iota((128, 384), 1)
    spread = onehot(div3(col >> 3) == iota((128, 384), 0)).astype(BF)
    code = dot(code.astype(BF), spread)
    gate = dot(gate.astype(BF), spread)
    col = iota((64, 384), 1)
    rest = col - 24 * div3(col >> 3)
    half = jnp.where(rest >= 12, 1, 0)
    rest = rest - 12 * half
    s = div3(rest)
    match = (s == (iota((64, 384), 0) >> 4)) & (code == (rest - 3 * s + 1).astype(F32))
    for h in range(2):
        weight = jnp.where(match & (half == h), gate, 0.0).astype(BF)
        total = dot(weight, rows_ref[...]).astype(BF)
        for s in range(N_Y):
            outs[s][:, 1792 * h : 1792 * (h + 1)] = total[TOK * s : TOK * (s + 1)]


def combine_kernel(table_ref, p0_ref, p1_ref, p2_ref, p3_ref, out_ref):
    pieces = [p0_ref, p1_ref, p2_ref, p3_ref]
    lane = iota((ROWS_N, SLOTS), 1)
    ls = div3(lane >> 4)
    rem = lane - ROWS_Y * ls
    ln = div3(rem)
    lr = rem - 3 * ln
    row = iota((ROWS_N, SLOTS), 0)
    rn = div40(row)
    rq = div5(row - 40 * rn)
    table = table_ref[...]
    code = jnp.zeros((ROWS_N, SLOTS), F32)
    gate = jnp.zeros((ROWS_N, SLOTS), F32)
    for s in range(N_Y):
        code = jnp.where(ls == s, table[:, s : s + 1], code)
        gate = jnp.where(ls == s, table[:, 4 + s : 5 + s], gate)
    match = (rn == ln) & (code == (lr + 1).astype(F32))
    weight = jnp.where(match, gate, 0.0)
    total = jnp.zeros((ROWS_N, 512), F32)
    for q in range(7):
        rows = jnp.concatenate([p[:, 512 * q : 512 * (q + 1)] for p in pieces], axis=0)
        total = total + dot(jnp.where(rq == q, weight, 0.0).astype(BF), rows)
    ext = jnp.concatenate([p[:, 3584:] for p in pieces], axis=0)
    terms = dot(onehot(match & (rq == 7)).astype(BF), ext)
    out_ref[:, :EXT] = (total[:, :EXT] + terms).astype(BF)
    out_ref[:, EXT:] = total[:, EXT:].astype(BF)


def finish_kernel(place_ref, routes_ref, a_ref, b0_ref, b1_ref, b2_ref, b3_ref, dx_ref, gg_ref):
    y = place_ref[1]
    routes = by_token(routes_ref[...])
    ncode = node_codes(route_tables(routes, 128))
    col = iota((128, ROWS_N), 1)
    spread = onehot(div40(col) == iota((128, ROWS_N), 0)).astype(BF)
    code = dot(ncode.astype(BF), spread)
    col = iota((TOK, ROWS_N), 1)
    cn = div40(col)
    cp = col - 40 * cn
    cq = div5(cp)
    match = code == (cp - 5 * cq + 1).astype(F32)
    for q in range(7):
        pick = onehot(match & (cq == q)).astype(BF)
        dx_ref[:, 512 * q : 512 * (q + 1)] = dot(pick, a_ref[...]).astype(BF)
    total = b0_ref[...].astype(F32) + b1_ref[...].astype(F32)
    total = total + b2_ref[...].astype(F32) + b3_ref[...].astype(F32)
    dx_ref[:, 3584:] = total.astype(BF)
    last = match & (cq == 7)
    picks = routes.astype(I32)
    masks = jnp.concatenate(
        [onehot(last & (cn == (picks[:, k : k + 1] >> 2))) for k in range(8)], axis=0
    ).astype(BF)
    terms = dot(masks, a_ref[:, :EXT])
    lane = iota((TOK, EXT), 1)
    result = jnp.zeros((TOK, EXT), F32)
    for k in range(8):
        s = ((picks[:, k : k + 1] & 3) - y) & 3
        mine = jnp.where((lane >> 1) == s, terms[TOK * k : TOK * (k + 1)], 0.0)
        result = jnp.where(lane == k, jnp.sum(mine, axis=1, keepdims=True), result)
    gg_ref[...] = result.T[:8]


SMEM = pl.BlockSpec(memory_space=pltpu.SMEM)
VM = pl.BlockSpec(memory_space=pltpu.VMEM)


def sds(shape, dtype=BF):
    return jax.ShapeDtypeStruct(shape, dtype)


def whole(kernel, out_shape, in_specs, name, scratch=()):
    multi = isinstance(out_shape, (list, tuple))
    return pl.pallas_call(
        kernel,
        out_shape=out_shape,
        in_specs=in_specs,
        out_specs=[VM] * len(out_shape) if multi else VM,
        scratch_shapes=list(scratch),
        compiler_params=pltpu.CompilerParams(vmem_limit_bytes=VMEM_LIMITS.get(name, 14) * MIB),
        name=name,
    )


def shift_y(v, s):
    return lax.ppermute(v, "local", [(i, (i + 2 * s) % 8) for i in range(8)])


def swap_core(v):
    return lax.ppermute(v, "local", [(i, i ^ 1) for i in range(8)])


def node_exchange(v):
    shape = v.shape
    v = v.reshape(N_NODE, shape[0] // N_NODE, shape[1])
    return lax.all_to_all(v, "node", split_axis=0, concat_axis=0, tiled=True).reshape(shape)


def on_device(tokens, out_grads, routes, gate_values, gate_weight, up_weight, down_weight):
    w_gate = gate_weight[0]
    w_up = up_weight[0]
    w_down = down_weight[0]
    place = jnp.stack([lax.axis_index("node"), lax.axis_index("local") // 2]).astype(I32)

    dy_send = whole(send_dy_kernel, sds((ROWS_N, 1024)), [VM] * 3, "send_dy")(
        routes.T, gate_values.T, out_grads
    )
    dy_send, tokens = lax.optimization_barrier((dy_send, tokens))
    dy_mid = node_exchange(dy_send)
    picks = jnp.concatenate([routes.astype(BF), gate_values.astype(BF)], axis=1)
    x_own = jnp.concatenate([tokens, jnp.pad(picks, ((0, 0), (0, EXT - 16)))], axis=1)
    x_near = [x_own] + [shift_y(x_own, s) for s in (1, 2, 3)]

    x_send = whole(send_x_kernel, sds((384, 3584)), [SMEM] + [VM] * 4, "send_x")(place, *x_near)
    *dy_out, table, mark = whole(
        regroup_kernel,
        [sds((ROWS_Y, WIDTH))] * 4 + [sds((ROWS_N, 128), F32), sds((8, 128), F32)],
        [SMEM, VM],
        "regroup",
    )(place, dy_mid)
    x_mine = node_exchange(x_send)
    dy_mine = [dy_out[0]] + [shift_y(dy_out[s], s) for s in (1, 2, 3)]
    dy_other = [swap_core(v) for v in dy_mine]
    hbm = pl.BlockSpec(memory_space=pl.ANY)
    down_near = whole(
        stage_kernel,
        sds((HALF, WIDTH)),
        [hbm, VM],
        "stage",
        [pltpu.SemaphoreType.DMA((8,))],
    )(w_down, mark)
    back = whole(back_kernel, sds((2 * SLOTS, HALF), F32), [VM] * 9, "back")(
        *dy_mine, *dy_other, down_near
    )
    x_mine, back = lax.optimization_barrier((x_mine, back))
    x_other = swap_core(x_mine)
    pre_gate, pre_up, gate_near, up_near = whole(
        forward_own_kernel,
        [sds((SLOTS, HALF), F32)] * 2 + [sds((WIDTH, HALF))] * 2,
        [VM, hbm, hbm, hbm],
        "forward_own",
        [pltpu.SemaphoreType.DMA((4, 4))],
    )(x_mine, w_gate, w_up, back)
    d_gate, d_up, ext = whole(
        forward_kernel,
        [sds((2 * SLOTS, HALF)), sds((2 * SLOTS, HALF)), sds((2 * SLOTS, EXT))],
        [VM] * 6,
        "forward",
    )(x_other, gate_near, up_near, back, pre_gate, pre_up)

    def dx(part, width):
        return whole(
            functools.partial(dx_kernel, part),
            [sds((SLOTS, width))] * 2,
            [VM] * 5,
            "dx",
        )(d_gate, d_up, gate_near, up_near, ext)

    own_a, other_a = dx(0, 3584 + EXT)
    own_b, other_b = dx(1, 3584)
    got_a = swap_core(other_a)
    got_b = swap_core(other_b)
    *pieces, mark = whole(
        add_kernel,
        [sds((ROWS_Y, 3584 + EXT))] * 4 + [sds((8, 128), F32)],
        [VM] * 2,
        "add_halves",
    )(own_a, got_a)
    pieces = [pieces[0]] + [shift_y(pieces[s], -s) for s in (1, 2, 3)]
    sent_b = whole(add_to_nodes_kernel, sds((384, 1792)), [VM] * 3, "add_to_nodes")(
        own_b, got_b, mark
    )
    back_b = node_exchange(sent_b)
    mixed = whole(combine_kernel, sds((ROWS_N, 512)), [VM] * 5, "combine")(table, *pieces)
    mixed, back_b = lax.optimization_barrier((mixed, back_b))
    back_a = node_exchange(mixed)
    near = whole(combine_near_kernel, [sds((TOK, 3584))] * 4, [SMEM] + [VM] * 5, "combine_near")(
        place, *x_near, back_b
    )
    near = [near[0]] + [shift_y(near[s], -s) for s in (1, 2, 3)]
    input_grads, gate_grads = whole(
        finish_kernel, [sds((TOK, WIDTH)), sds((8, TOK), F32)], [SMEM] + [VM] * 6, "finish"
    )(place, routes.T, back_a, *near)
    return input_grads, gate_grads.T


def solution(mesh):
    row = P(("node", "local"), None)
    weight = P(("node", "local"), None, None)
    return jax.shard_map(
        on_device,
        mesh=mesh,
        in_specs=(row, row, row, row, weight, weight, weight),
        out_specs=(row, row),
        check_vma=False,
    )
```

```python
import functools

import jax
import jax.numpy as jnp
from jax import lax
from jax.experimental import pallas as pl
from jax.experimental.pallas import tpu as pltpu
from jax.sharding import PartitionSpec as P

BF = jnp.bfloat16
F32 = jnp.float32
I32 = jnp.int32

N_NODE = 16
N_Y = 4
TOK = 16
CAP_NODE = 5
CAP_EXP = 3
WIDTH = 7168
HALF = 512
ROWS_Y = N_NODE * CAP_EXP
SLOTS = N_Y * ROWS_Y
ROWS_N = N_NODE * 40
EXT = 128
MIB = 1024 * 1024
VMEM_LIMITS = {"send_dy": 60, "back": 20, "forward_own": 30, "forward": 30, "dx": 24}


def iota(shape, dim):
    return lax.broadcasted_iota(I32, shape, dim)


def div3(v):
    return (v * 171) >> 9


def div5(v):
    return (v * 205) >> 10


def div40(v):
    return div5(v >> 3)


def dot(a, b):
    return jnp.dot(a, b, preferred_element_type=F32)


def dot_nt(a, b):
    return lax.dot_general(a, b, (((1,), (1,)), ((), ())), preferred_element_type=F32)


def dot_tn(a, b):
    return lax.dot_general(a, b, (((0,), (0,)), ((), ())), preferred_element_type=F32)


def onehot(mask):
    return jnp.where(mask, 1.0, 0.0)


def by_token(v):
    return dot_tn(v.astype(F32).astype(BF), onehot(iota((8, 128), 0) == iota((8, 128), 1)).astype(BF))


def route_tables(routes, width):
    lane = (iota((TOK, width), 1) & 63).astype(F32)
    hot = jnp.zeros((TOK, width), F32)
    for k in range(8):
        hot = hot + onehot(routes[:, k : k + 1] == lane)
    return hot


def node_codes(hot):
    width = hot.shape[1]
    row = iota((width, 128), 0)
    group = onehot((row < 64) & ((row >> 2) == iota((width, 128), 1))).astype(BF)
    used = jnp.minimum(dot(hot.astype(BF), group), 1.0)
    tri = onehot(iota((TOK, TOK), 1) < iota((TOK, TOK), 0)).astype(BF)
    return used * (dot(tri, used.astype(BF)) + 1.0)


def send_dy_kernel(routes_ref, gates_ref, dy_ref, out_ref):
    routes = by_token(routes_ref[...])
    gates = by_token(gates_ref[...])
    width = 256
    lane = iota((TOK, width), 1)
    expert = (lane & 63).astype(F32)
    hot = route_tables(routes, width)
    gate = jnp.zeros((TOK, width), F32)
    for k in range(8):
        gate = gate + jnp.where(routes[:, k : k + 1] == expert, gates[:, k : k + 1], 0.0)
    tri = onehot(iota((TOK, TOK), 1) < iota((TOK, TOK), 0)).astype(BF)
    code = hot * (dot(tri, hot.astype(BF)) + 1.0)
    section = lane >> 6
    meta = jnp.where(section == 0, code, jnp.where(section == 1, gate, 0.0)).astype(BF)
    meta = jnp.concatenate([meta, jnp.zeros((TOK, 1024 - width), BF)], axis=1)
    stack = jnp.concatenate([dy_ref[:, 1024 * q : 1024 * (q + 1)] for q in range(7)] + [meta], axis=0)
    ncode = node_codes(hot)
    spread = onehot((iota((TOK, 128), 1) & 15) == iota((TOK, 128), 0)).astype(BF)
    ncode_lane = dot_tn(ncode.astype(BF), spread)[:N_NODE]
    chunk = (iota((N_NODE, 128), 1) >> 4).astype(F32)
    key = jnp.where(ncode_lane > 0.0, 8.0 * chunk + ncode_lane, -1.0)
    row = iota((40, 128), 0)
    q = div5(row)
    row_key = (8 * q + (row - 5 * q) + 1).astype(F32)
    pick = jnp.concatenate([onehot(row_key == key[n : n + 1, :]) for n in range(N_NODE)], axis=0)
    out_ref[...] = dot(pick.astype(BF), stack).astype(BF)


def send_x_kernel(place_ref, x0_ref, x1_ref, x2_ref, x3_ref, out_ref):
    y = place_ref[1]
    xs = [x0_ref, x1_ref, x2_ref, x3_ref]
    code, _ = near_tables(y, xs)
    lane = iota((64, 128), 1)
    spread = onehot((lane & 63) == iota((64, 128), 0)).astype(BF)
    code_lane = dot_tn(code.astype(BF), spread)[:N_NODE]
    block = (iota((N_NODE, 128), 1) >> 4).astype(F32)
    key = jnp.where(code_lane > 0.0, 4.0 * block + code_lane, -1.0)
    row = iota((24, 128), 0)
    b = div3(row)
    row_key = (4 * b + (row - 3 * b) + 1).astype(F32)
    pick = jnp.concatenate([onehot(row_key == key[n : n + 1, :]) for n in range(N_NODE)], axis=0).astype(BF)
    for i in range(7):
        lo = 512 * i
        stack = jnp.concatenate(
            [r[:, lo : lo + 512] for r in xs] + [r[:, 3584 + lo : 3584 + lo + 512] for r in xs], axis=0
        )
        out_ref[:, lo : lo + 512] = dot(pick, stack).astype(BF)


def regroup_kernel(place_ref, rows_ref, out0_ref, out1_ref, out2_ref, out3_ref, meta_ref, mark_ref):
    node = place_ref[0]
    y = place_ref[1]
    outs = [out0_ref, out1_ref, out2_ref, out3_ref]
    c = iota((256, 128), 1)
    want = ((c >> 2) << 6) + 4 * node + ((y + c) & 3)
    select = onehot((c < 8) & (iota((256, 128), 0) == want)).astype(BF)
    meta = rows_ref[:, :256]
    meta_ref[...] = meta
    mark_ref[...] = jnp.zeros_like(mark_ref)
    code = lax.dot_general(select, meta, (((0,), (1,)), ((), ())), preferred_element_type=F32)[:8]
    col = iota((8, ROWS_N), 1)
    n = div40(col)
    key = jnp.where((col - 40 * n >= 35) & (code > 0.0), 4.0 * n.astype(F32) + code, -1.0)
    row = iota((ROWS_Y, ROWS_N), 0)
    rn = div3(row)
    row_key = (4 * rn + (row - 3 * rn) + 1).astype(F32)
    for q in range(7):
        key_q = pltpu.roll(key, ROWS_N - (35 - 5 * q), 1)
        pick = jnp.concatenate([onehot(row_key == key_q[s : s + 1, :]) for s in range(N_Y)], axis=0)
        moved = dot(pick.astype(BF), rows_ref[...]).astype(BF)
        for s in range(N_Y):
            outs[s][:, 1024 * q : 1024 * (q + 1)] = moved[ROWS_Y * s : ROWS_Y * (s + 1)]


def table_kernel(place_ref, meta_ref, table_ref):
    c = iota((256, 128), 1)
    want = ((c >> 2) << 6) + 4 * place_ref[0] + ((place_ref[1] + c) & 3)
    select = onehot((c < 8) & (iota((256, 128), 0) == want)).astype(BF)
    picked = dot(meta_ref[...], select).astype(BF)
    r = iota((128, ROWS_N), 0)
    j = r & 7
    source = jnp.where(j < CAP_NODE, 40 * (r >> 3) + 35 + j, -1)
    table_ref[...] = dot(onehot(iota((128, ROWS_N), 1) == source).astype(BF), picked)


def copy_parts(source, target, sems, first, rows):
    copies = []
    step = rows // sems.shape[0]
    for i in range(sems.shape[0]):
        at = pl.ds(first + step * i, step)
        copies.append(pltpu.make_async_copy(source.at[at], target.at[at], sems.at[i]))
        copies[-1].start()
    return copies


def wait_all(copies):
    for copy in copies:
        copy.wait()


def stage_kernel(source_ref, mark_ref, out_ref, sems):
    wait_all(copy_parts(source_ref, out_ref, sems, 0, source_ref.shape[0]))


def back_kernel(*refs):
    pieces, down_ref, out_ref = refs[:8], refs[8], refs[9]
    rows = jnp.concatenate([p[...] for p in pieces], axis=0)
    out_ref[...] = dot_nt(rows, down_ref[...])


def slot_order(h):
    row = iota((SLOTS, 384), 0)
    s = div3(row >> 4)
    rem = row - ROWS_Y * s
    n = div3(rem)
    r = rem - 3 * n
    return onehot(iota((SLOTS, 384), 1) == 24 * n + 12 * h + 3 * s + r).astype(BF)


def forward_own_kernel(x_ref, gate_hbm, up_hbm, mark_ref, pg_ref, pu_ref, gate_ref, up_ref, sems):
    loads = []
    for h in range(2):
        loads.append(copy_parts(gate_hbm, gate_ref, sems.at[2 * h], 3584 * h, 3584))
        loads.append(copy_parts(up_hbm, up_ref, sems.at[2 * h + 1], 3584 * h, 3584))
    for h in range(2):
        rows = dot(slot_order(h), x_ref[...]).astype(BF)
        at = slice(3584 * h, 3584 * (h + 1))
        wait_all(loads[2 * h])
        gate = dot(rows, gate_ref[at, :])
        wait_all(loads[2 * h + 1])
        up = dot(rows, up_ref[at, :])
        pg_ref[...] = gate if h == 0 else pg_ref[...] + gate
        pu_ref[...] = up if h == 0 else pu_ref[...] + up


def forward_kernel(
    x_ref, gate_ref, up_ref, back_ref, pg_ref, pu_ref, dgate_ref, dup_ref, ext_ref
):
    pre_gate = jnp.zeros((SLOTS, HALF), F32)
    pre_up = jnp.zeros((SLOTS, HALF), F32)
    for h in range(2):
        rows = dot(slot_order(h), x_ref[...]).astype(BF)
        at = slice(3584 * h, 3584 * (h + 1))
        pre_gate = pre_gate + dot(rows, gate_ref[at, :])
        pre_up = pre_up + dot(rows, up_ref[at, :])
    pre_gate = jnp.concatenate([pg_ref[...], pre_gate], axis=0)
    pre_up = jnp.concatenate([pu_ref[...], pre_up], axis=0)
    back = back_ref[...]
    sig = jax.nn.sigmoid(pre_gate)
    act = pre_gate * sig
    hidden = (act * pre_up).astype(BF)
    part = jnp.sum(hidden.astype(F32) * back, axis=1, keepdims=True)
    dgate_ref[...] = (back * pre_up * sig * (1.0 + pre_gate * (1.0 - sig))).astype(BF)
    dup_ref[...] = (back * act).astype(BF)
    high = part.astype(BF).astype(F32)
    low = part - high
    slot = iota((2 * SLOTS, EXT), 0)
    slot = jnp.where(slot >= SLOTS, slot - SLOTS, slot)
    at = 2 * div3(slot >> 4)
    lane = iota((2 * SLOTS, EXT), 1)
    ext_ref[...] = jnp.where(lane == at, high, jnp.where(lane == at + 1, low, 0.0)).astype(BF)


def dx_kernel(part, dgate_ref, dup_ref, gate_ref, up_ref, ext_ref, own_ref, other_ref):
    cols = slice(3584 * part, 3584 * (part + 1))
    out = (dot_nt(dgate_ref[...], gate_ref[cols, :]) + dot_nt(dup_ref[...], up_ref[cols, :])).astype(BF)
    own_ref[:, :3584] = out[:SLOTS]
    other_ref[:, :3584] = out[SLOTS:]
    if part == 0:
        own_ref[:, 3584:] = ext_ref[:SLOTS]
        other_ref[:, 3584:] = ext_ref[SLOTS:]


def add_kernel(own_ref, got_ref, *outs):
    outs[4][...] = jnp.zeros_like(outs[4])
    lane = iota((ROWS_Y, EXT), 1)
    for s in range(N_Y):
        rows = slice(ROWS_Y * s, ROWS_Y * (s + 1))
        total = own_ref[rows, :3584].astype(F32) + got_ref[rows, :3584].astype(F32)
        outs[s][:, :3584] = total.astype(BF)
        term = jnp.sum(
            own_ref[rows, 3584:].astype(F32) + got_ref[rows, 3584:].astype(F32), axis=1, keepdims=True
        )
        high = term.astype(BF).astype(F32)
        low = term - high
        outs[s][:, 3584:] = jnp.where(
            lane == 2 * s, high, jnp.where(lane == 2 * s + 1, low, 0.0)
        ).astype(BF)


def add_to_nodes_kernel(own_ref, got_ref, mark_ref, out_ref):
    row = iota((384, 384), 0)
    block = div3(row >> 3)
    rest = row - 24 * block
    h = jnp.where(rest >= 12, 1, 0)
    rest = rest - 12 * h
    s = div3(rest)
    source = SLOTS * h + ROWS_Y * s + 3 * block + (rest - 3 * s)
    perm = onehot(iota((384, 384), 1) == source).astype(BF)
    total = (own_ref[...].astype(F32) + got_ref[...].astype(F32)).astype(BF)
    out_ref[...] = dot(perm, jnp.concatenate([total[:, :1792], total[:, 1792:]], axis=0)).astype(BF)


def near_tables(y, xs):
    meta = jnp.concatenate([r[:, WIDTH : WIDTH + EXT] for r in xs], axis=0).astype(F32)
    lane = iota((64, 128), 1)
    wanted = jnp.where(lane < N_NODE, 4 * lane + y, -1).astype(F32)
    hot = jnp.zeros((64, 128), F32)
    gate = jnp.zeros((64, 128), F32)
    for k in range(8):
        here = meta[:, k : k + 1] == wanted
        hot = hot + onehot(here)
        gate = gate + jnp.where(here, meta[:, 8 + k : 9 + k], 0.0)
    r64 = iota((64, 64), 0)
    c64 = iota((64, 64), 1)
    tri = onehot((c64 < r64) & ((c64 >> 4) == (r64 >> 4))).astype(BF)
    return hot * (dot(tri, hot.astype(BF)) + 1.0), gate


def combine_near_kernel(place_ref, x0_ref, x1_ref, x2_ref, x3_ref, rows_ref, *outs):
    code, gate = near_tables(place_ref[1], [x0_ref, x1_ref, x2_ref, x3_ref])
    col = iota((128, 384), 1)
    spread = onehot(div3(col >> 3) == iota((128, 384), 0)).astype(BF)
    code = dot(code.astype(BF), spread)
    gate = dot(gate.astype(BF), spread)
    col = iota((64, 384), 1)
    rest = col - 24 * div3(col >> 3)
    half = jnp.where(rest >= 12, 1, 0)
    rest = rest - 12 * half
    s = div3(rest)
    match = (s == (iota((64, 384), 0) >> 4)) & (code == (rest - 3 * s + 1).astype(F32))
    for h in range(2):
        weight = jnp.where(match & (half == h), gate, 0.0).astype(BF)
        total = dot(weight, rows_ref[...]).astype(BF)
        for s in range(N_Y):
            outs[s][:, 1792 * h : 1792 * (h + 1)] = total[TOK * s : TOK * (s + 1)]


def combine_kernel(table_ref, p0_ref, p1_ref, p2_ref, p3_ref, out_ref, rows_ref):
    pieces = [p0_ref, p1_ref, p2_ref, p3_ref]
    lane = iota((128, SLOTS), 1)
    ls = div3(lane >> 4)
    rem = lane - ROWS_Y * ls
    ln = div3(rem)
    lr = rem - 3 * ln
    table = table_ref[...]
    code = jnp.zeros((128, SLOTS), F32)
    gate = jnp.zeros((128, SLOTS), F32)
    for s in range(N_Y):
        code = jnp.where(ls == s, table[:, s : s + 1], code)
        gate = jnp.where(ls == s, table[:, 4 + s : 5 + s], gate)
    match = ((iota((128, SLOTS), 0) >> 3) == ln) & (code == (lr + 1).astype(F32))
    weight = jnp.where(match, gate, 0.0).astype(BF)
    ext = jnp.concatenate([p[:, 3584:] for p in pieces], axis=0)
    terms = dot(onehot(match).astype(BF), ext)
    terms = jnp.concatenate([terms, jnp.zeros((128, 512 - EXT), F32)], axis=1)
    for q in range(7):
        total = dot(weight, jnp.concatenate([p[:, 512 * q : 512 * (q + 1)] for p in pieces], axis=0))
        for n in range(N_NODE):
            at = 40 * n + 5 * q
            rows_ref[at : at + 8, :] = total[8 * n : 8 * n + 8]
    for n in range(N_NODE):
        rows_ref[40 * n + 35 : 40 * n + 40, :] = terms[8 * n : 8 * n + 5]
    out_ref[...] = rows_ref[...].astype(BF)


def finish_kernel(place_ref, routes_ref, a_ref, b0_ref, b1_ref, b2_ref, b3_ref, dx_ref, gg_ref):
    y = place_ref[1]
    routes = by_token(routes_ref[...])
    ncode = node_codes(route_tables(routes, 128))
    col = iota((128, ROWS_N), 1)
    spread = onehot(div40(col) == iota((128, ROWS_N), 0)).astype(BF)
    code = dot(ncode.astype(BF), spread)
    col = iota((TOK, ROWS_N), 1)
    cn = div40(col)
    cp = col - 40 * cn
    cq = div5(cp)
    match = code == (cp - 5 * cq + 1).astype(F32)
    pick = jnp.concatenate([onehot(match & (cq == q)) for q in range(7)], axis=0).astype(BF)
    total = dot(pick, a_ref[...]).astype(BF)
    for q in range(7):
        dx_ref[:, 512 * q : 512 * (q + 1)] = total[TOK * q : TOK * (q + 1)]
    total = b0_ref[...].astype(F32) + b1_ref[...].astype(F32)
    total = total + b2_ref[...].astype(F32) + b3_ref[...].astype(F32)
    dx_ref[:, 3584:] = total.astype(BF)
    last = match & (cq == 7)
    picks = routes.astype(I32)
    masks = jnp.concatenate(
        [onehot(last & (cn == (picks[:, k : k + 1] >> 2))) for k in range(8)], axis=0
    ).astype(BF)
    terms = dot(masks, a_ref[:, :EXT])
    lane = iota((TOK, EXT), 1)
    result = jnp.zeros((TOK, EXT), F32)
    for k in range(8):
        s = ((picks[:, k : k + 1] & 3) - y) & 3
        mine = jnp.where((lane >> 1) == s, terms[TOK * k : TOK * (k + 1)], 0.0)
        result = jnp.where(lane == k, jnp.sum(mine, axis=1, keepdims=True), result)
    gg_ref[...] = result.T[:8]


SMEM = pl.BlockSpec(memory_space=pltpu.SMEM)
VM = pl.BlockSpec(memory_space=pltpu.VMEM)


def sds(shape, dtype=BF):
    return jax.ShapeDtypeStruct(shape, dtype)


def whole(kernel, out_shape, in_specs, name, scratch=()):
    multi = isinstance(out_shape, (list, tuple))
    return pl.pallas_call(
        kernel,
        out_shape=out_shape,
        in_specs=in_specs,
        out_specs=[VM] * len(out_shape) if multi else VM,
        scratch_shapes=list(scratch),
        compiler_params=pltpu.CompilerParams(vmem_limit_bytes=VMEM_LIMITS.get(name, 14) * MIB),
        name=name,
    )


def shift_y(v, s):
    return lax.ppermute(v, "local", [(i, (i + 2 * s) % 8) for i in range(8)])


def swap_core(v):
    return lax.ppermute(v, "local", [(i, i ^ 1) for i in range(8)])


def node_exchange(v):
    shape = v.shape
    v = v.reshape(N_NODE, shape[0] // N_NODE, shape[1])
    return lax.all_to_all(v, "node", split_axis=0, concat_axis=0, tiled=True).reshape(shape)


def on_device(tokens, out_grads, routes, gate_values, gate_weight, up_weight, down_weight):
    w_gate = gate_weight[0]
    w_up = up_weight[0]
    w_down = down_weight[0]
    place = jnp.stack([lax.axis_index("node"), lax.axis_index("local") // 2]).astype(I32)

    dy_send = whole(send_dy_kernel, sds((ROWS_N, 1024)), [VM] * 3, "send_dy")(
        routes.T, gate_values.T, out_grads
    )
    dy_send, tokens = lax.optimization_barrier((dy_send, tokens))
    dy_mid = node_exchange(dy_send)
    picks = jnp.concatenate([routes.astype(BF), gate_values.astype(BF)], axis=1)
    x_own = jnp.concatenate([tokens, jnp.pad(picks, ((0, 0), (0, EXT - 16)))], axis=1)
    x_near = [x_own] + [shift_y(x_own, s) for s in (1, 2, 3)]

    x_send = whole(send_x_kernel, sds((384, 3584)), [SMEM] + [VM] * 4, "send_x")(place, *x_near)
    *dy_out, meta, mark = whole(
        regroup_kernel,
        [sds((ROWS_Y, WIDTH))] * 4 + [sds((ROWS_N, 256)), sds((8, 128), F32)],
        [SMEM, VM],
        "regroup",
    )(place, dy_mid)
    x_mine = node_exchange(x_send)
    dy_mine = [dy_out[0]] + [shift_y(dy_out[s], s) for s in (1, 2, 3)]
    dy_other = [swap_core(v) for v in dy_mine]
    hbm = pl.BlockSpec(memory_space=pl.ANY)
    down_near = whole(
        stage_kernel,
        sds((HALF, WIDTH)),
        [hbm, VM],
        "stage",
        [pltpu.SemaphoreType.DMA((8,))],
    )(w_down, mark)
    table = whole(table_kernel, sds((128, 128), F32), [SMEM, VM], "table")(place, meta)
    back = whole(back_kernel, sds((2 * SLOTS, HALF), F32), [VM] * 9, "back")(
        *dy_mine, *dy_other, down_near
    )
    x_mine, back = lax.optimization_barrier((x_mine, back))
    x_other = swap_core(x_mine)
    pre_gate, pre_up, gate_near, up_near = whole(
        forward_own_kernel,
        [sds((SLOTS, HALF), F32)] * 2 + [sds((WIDTH, HALF))] * 2,
        [VM, hbm, hbm, hbm],
        "forward_own",
        [pltpu.SemaphoreType.DMA((4, 4))],
    )(x_mine, w_gate, w_up, back)
    d_gate, d_up, ext = whole(
        forward_kernel,
        [sds((2 * SLOTS, HALF)), sds((2 * SLOTS, HALF)), sds((2 * SLOTS, EXT))],
        [VM] * 6,
        "forward",
    )(x_other, gate_near, up_near, back, pre_gate, pre_up)

    def dx(part, width):
        return whole(
            functools.partial(dx_kernel, part),
            [sds((SLOTS, width))] * 2,
            [VM] * 5,
            "dx",
        )(d_gate, d_up, gate_near, up_near, ext)

    own_a, other_a = dx(0, 3584 + EXT)
    own_b, other_b = dx(1, 3584)
    got_a = swap_core(other_a)
    got_b = swap_core(other_b)
    *pieces, mark = whole(
        add_kernel,
        [sds((ROWS_Y, 3584 + EXT))] * 4 + [sds((8, 128), F32)],
        [VM] * 2,
        "add_halves",
    )(own_a, got_a)
    pieces = [pieces[0]] + [shift_y(pieces[s], -s) for s in (1, 2, 3)]
    sent_b = whole(add_to_nodes_kernel, sds((384, 1792)), [VM] * 3, "add_to_nodes")(
        own_b, got_b, mark
    )
    back_b = node_exchange(sent_b)
    mixed = whole(
        combine_kernel,
        sds((ROWS_N, 512)),
        [VM] * 5,
        "combine",
        [pltpu.VMEM((ROWS_N, 512), F32)],
    )(table, *pieces)
    mixed, back_b = lax.optimization_barrier((mixed, back_b))
    back_a = node_exchange(mixed)
    near = whole(combine_near_kernel, [sds((TOK, 3584))] * 4, [SMEM] + [VM] * 5, "combine_near")(
        place, *x_near, back_b
    )
    near = [near[0]] + [shift_y(near[s], -s) for s in (1, 2, 3)]
    input_grads, gate_grads = whole(
        finish_kernel, [sds((TOK, WIDTH)), sds((8, TOK), F32)], [SMEM] + [VM] * 6, "finish"
    )(place, routes.T, back_a, *near)
    return input_grads, gate_grads.T


def solution(mesh):
    row = P(("node", "local"), None)
    weight = P(("node", "local"), None, None)
    return jax.shard_map(
        on_device,
        mesh=mesh,
        in_specs=(row, row, row, row, weight, weight, weight),
        out_specs=(row, row),
        check_vma=False,
    )
```

```python
import functools

import jax
import jax.numpy as jnp
from jax import lax
from jax.experimental import pallas as pl
from jax.experimental.pallas import tpu as pltpu
from jax.sharding import PartitionSpec as P

BF = jnp.bfloat16
F32 = jnp.float32
I32 = jnp.int32

N_NODE = 16
N_Y = 4
TOK = 16
CAP_NODE = 5
CAP_EXP = 3
WIDTH = 7168
HALF = 512
ROWS_Y = N_NODE * CAP_EXP
SLOTS = N_Y * ROWS_Y
ROWS_N = N_NODE * 40
EXT = 128
MIB = 1024 * 1024
VMEM_LIMITS = {"send_dy": 60, "regroup_own": 24, "back": 20, "forward_own": 30, "forward": 30, "dx": 24}


def iota(shape, dim):
    return lax.broadcasted_iota(I32, shape, dim)


def div3(v):
    return (v * 171) >> 9


def div5(v):
    return (v * 205) >> 10


def div40(v):
    return div5(v >> 3)


def dot(a, b):
    return jnp.dot(a, b, preferred_element_type=F32)


def dot_nt(a, b):
    return lax.dot_general(a, b, (((1,), (1,)), ((), ())), preferred_element_type=F32)


def dot_tn(a, b):
    return lax.dot_general(a, b, (((0,), (0,)), ((), ())), preferred_element_type=F32)


def onehot(mask):
    return jnp.where(mask, 1.0, 0.0)


def by_token(v):
    return dot_tn(v.astype(F32).astype(BF), onehot(iota((8, 128), 0) == iota((8, 128), 1)).astype(BF))


def route_tables(routes, width):
    lane = (iota((TOK, width), 1) & 63).astype(F32)
    hot = jnp.zeros((TOK, width), F32)
    for k in range(8):
        hot = hot + onehot(routes[:, k : k + 1] == lane)
    return hot


def node_codes(hot):
    width = hot.shape[1]
    row = iota((width, 128), 0)
    group = onehot((row < 64) & ((row >> 2) == iota((width, 128), 1))).astype(BF)
    used = jnp.minimum(dot(hot.astype(BF), group), 1.0)
    tri = onehot(iota((TOK, TOK), 1) < iota((TOK, TOK), 0)).astype(BF)
    return used * (dot(tri, used.astype(BF)) + 1.0)


def send_dy_kernel(routes_ref, gates_ref, dy_ref, out_ref):
    routes = by_token(routes_ref[...])
    gates = by_token(gates_ref[...])
    width = 256
    lane = iota((TOK, width), 1)
    expert = (lane & 63).astype(F32)
    hot = route_tables(routes, width)
    gate = jnp.zeros((TOK, width), F32)
    for k in range(8):
        gate = gate + jnp.where(routes[:, k : k + 1] == expert, gates[:, k : k + 1], 0.0)
    tri = onehot(iota((TOK, TOK), 1) < iota((TOK, TOK), 0)).astype(BF)
    code = hot * (dot(tri, hot.astype(BF)) + 1.0)
    section = lane >> 6
    meta = jnp.where(section == 0, code, jnp.where(section == 1, gate, 0.0)).astype(BF)
    meta = jnp.concatenate([meta, jnp.zeros((TOK, 1024 - width), BF)], axis=1)
    stack = jnp.concatenate([dy_ref[:, 1024 * q : 1024 * (q + 1)] for q in range(7)] + [meta], axis=0)
    ncode = node_codes(hot)
    spread = onehot((iota((TOK, 128), 1) & 15) == iota((TOK, 128), 0)).astype(BF)
    ncode_lane = dot_tn(ncode.astype(BF), spread)[:N_NODE]
    chunk = (iota((N_NODE, 128), 1) >> 4).astype(F32)
    key = jnp.where(ncode_lane > 0.0, 8.0 * chunk + ncode_lane, -1.0)
    row = iota((40, 128), 0)
    q = div5(row)
    row_key = (8 * q + (row - 5 * q) + 1).astype(F32)
    pick = jnp.concatenate([onehot(row_key == key[n : n + 1, :]) for n in range(N_NODE)], axis=0)
    out_ref[...] = dot(pick.astype(BF), stack).astype(BF)


def send_x_kernel(place_ref, x0_ref, x1_ref, x2_ref, x3_ref, out_ref):
    y = place_ref[1]
    xs = [x0_ref, x1_ref, x2_ref, x3_ref]
    code, _ = near_tables(y, xs)
    lane = iota((64, 128), 1)
    spread = onehot((lane & 63) == iota((64, 128), 0)).astype(BF)
    code_lane = dot_tn(code.astype(BF), spread)[:N_NODE]
    block = (iota((N_NODE, 128), 1) >> 4).astype(F32)
    key = jnp.where(code_lane > 0.0, 4.0 * block + code_lane, -1.0)
    row = iota((24, 128), 0)
    b = div3(row)
    row_key = (4 * b + (row - 3 * b) + 1).astype(F32)
    pick = jnp.concatenate([onehot(row_key == key[n : n + 1, :]) for n in range(N_NODE)], axis=0).astype(BF)
    for i in range(7):
        lo = 512 * i
        stack = jnp.concatenate(
            [r[:, lo : lo + 512] for r in xs] + [r[:, 3584 + lo : 3584 + lo + 512] for r in xs], axis=0
        )
        out_ref[:, lo : lo + 512] = dot(pick, stack).astype(BF)


def copy_parts(source, target, sems, first, rows):
    copies = []
    step = rows // sems.shape[0]
    for i in range(sems.shape[0]):
        at = pl.ds(first + step * i, step)
        copies.append(pltpu.make_async_copy(source.at[at], target.at[at], sems.at[i]))
        copies[-1].start()
    return copies


def wait_all(copies):
    for copy in copies:
        copy.wait()


def regroup(shifts, place_ref, rows_ref, outs):
    c = iota((256, 128), 1)
    want = ((c >> 2) << 6) + 4 * place_ref[0] + ((place_ref[1] + c) & 3)
    select = onehot((c < 8) & (iota((256, 128), 0) == want)).astype(BF)
    code = lax.dot_general(
        select, rows_ref[:, :256], (((0,), (1,)), ((), ())), preferred_element_type=F32
    )[:8]
    col = iota((8, ROWS_N), 1)
    n = div40(col)
    key = jnp.where((col - 40 * n >= 35) & (code > 0.0), 4.0 * n.astype(F32) + code, -1.0)
    row = iota((ROWS_Y, ROWS_N), 0)
    rn = div3(row)
    row_key = (4 * rn + (row - 3 * rn) + 1).astype(F32)
    for q in range(7):
        key_q = pltpu.roll(key, ROWS_N - (35 - 5 * q), 1)
        pick = jnp.concatenate([onehot(row_key == key_q[s : s + 1, :]) for s in shifts], axis=0)
        moved = dot(pick.astype(BF), rows_ref[...]).astype(BF)
        for i, out in enumerate(outs):
            out[:, 1024 * q : 1024 * (q + 1)] = moved[ROWS_Y * i : ROWS_Y * (i + 1)]


def regroup_far_kernel(place_ref, rows_ref, out1_ref, out2_ref, out3_ref, meta_ref):
    meta_ref[...] = rows_ref[:, :256]
    regroup((1, 2, 3), place_ref, rows_ref, [out1_ref, out2_ref, out3_ref])


def regroup_own_kernel(place_ref, rows_ref, down_hbm, out_ref, down_ref, sems):
    loads = copy_parts(down_hbm, down_ref, sems, 0, HALF)
    regroup((0,), place_ref, rows_ref, [out_ref])
    wait_all(loads)


def table_kernel(place_ref, meta_ref, table_ref):
    c = iota((256, 128), 1)
    want = ((c >> 2) << 6) + 4 * place_ref[0] + ((place_ref[1] + c) & 3)
    select = onehot((c < 8) & (iota((256, 128), 0) == want)).astype(BF)
    picked = dot(meta_ref[...], select).astype(BF)
    r = iota((128, ROWS_N), 0)
    j = r & 7
    source = jnp.where(j < CAP_NODE, 40 * (r >> 3) + 35 + j, -1)
    table_ref[...] = dot(onehot(iota((128, ROWS_N), 1) == source).astype(BF), picked)


def back_kernel(*refs):
    pieces, down_ref, out_ref = refs[:8], refs[8], refs[9]
    rows = jnp.concatenate([p[...] for p in pieces], axis=0)
    out_ref[...] = dot_nt(rows, down_ref[...])


def slot_order(h):
    row = iota((SLOTS, 384), 0)
    s = div3(row >> 4)
    rem = row - ROWS_Y * s
    n = div3(rem)
    r = rem - 3 * n
    return onehot(iota((SLOTS, 384), 1) == 24 * n + 12 * h + 3 * s + r).astype(BF)


def forward_own_kernel(x_ref, gate_hbm, up_hbm, mark_ref, pg_ref, pu_ref, gate_ref, up_ref, sems):
    loads = []
    for h in range(2):
        loads.append(copy_parts(gate_hbm, gate_ref, sems.at[2 * h], 3584 * h, 3584))
        loads.append(copy_parts(up_hbm, up_ref, sems.at[2 * h + 1], 3584 * h, 3584))
    for h in range(2):
        rows = dot(slot_order(h), x_ref[...]).astype(BF)
        at = slice(3584 * h, 3584 * (h + 1))
        wait_all(loads[2 * h])
        gate = dot(rows, gate_ref[at, :])
        wait_all(loads[2 * h + 1])
        up = dot(rows, up_ref[at, :])
        pg_ref[...] = gate if h == 0 else pg_ref[...] + gate
        pu_ref[...] = up if h == 0 else pu_ref[...] + up


def forward_kernel(
    x_ref, gate_ref, up_ref, back_ref, pg_ref, pu_ref, dgate_ref, dup_ref, ext_ref
):
    pre_gate = jnp.zeros((SLOTS, HALF), F32)
    pre_up = jnp.zeros((SLOTS, HALF), F32)
    for h in range(2):
        rows = dot(slot_order(h), x_ref[...]).astype(BF)
        at = slice(3584 * h, 3584 * (h + 1))
        pre_gate = pre_gate + dot(rows, gate_ref[at, :])
        pre_up = pre_up + dot(rows, up_ref[at, :])
    pre_gate = jnp.concatenate([pg_ref[...], pre_gate], axis=0)
    pre_up = jnp.concatenate([pu_ref[...], pre_up], axis=0)
    back = back_ref[...]
    sig = jax.nn.sigmoid(pre_gate)
    act = pre_gate * sig
    hidden = (act * pre_up).astype(BF)
    part = jnp.sum(hidden.astype(F32) * back, axis=1, keepdims=True)
    dgate_ref[...] = (back * pre_up * sig * (1.0 + pre_gate * (1.0 - sig))).astype(BF)
    dup_ref[...] = (back * act).astype(BF)
    high = part.astype(BF).astype(F32)
    low = part - high
    slot = iota((2 * SLOTS, EXT), 0)
    slot = jnp.where(slot >= SLOTS, slot - SLOTS, slot)
    at = 2 * div3(slot >> 4)
    lane = iota((2 * SLOTS, EXT), 1)
    ext_ref[...] = jnp.where(lane == at, high, jnp.where(lane == at + 1, low, 0.0)).astype(BF)


def dx_kernel(part, dgate_ref, dup_ref, gate_ref, up_ref, ext_ref, own_ref, other_ref):
    cols = slice(3584 * part, 3584 * (part + 1))
    out = (dot_nt(dgate_ref[...], gate_ref[cols, :]) + dot_nt(dup_ref[...], up_ref[cols, :])).astype(BF)
    own_ref[:, :3584] = out[:SLOTS]
    other_ref[:, :3584] = out[SLOTS:]
    if part == 0:
        own_ref[:, 3584:] = ext_ref[:SLOTS]
        other_ref[:, 3584:] = ext_ref[SLOTS:]


def add_kernel(own_ref, got_ref, *outs):
    outs[4][...] = jnp.zeros_like(outs[4])
    lane = iota((ROWS_Y, EXT), 1)
    for s in range(N_Y):
        rows = slice(ROWS_Y * s, ROWS_Y * (s + 1))
        total = own_ref[rows, :3584].astype(F32) + got_ref[rows, :3584].astype(F32)
        outs[s][:, :3584] = total.astype(BF)
        term = jnp.sum(
            own_ref[rows, 3584:].astype(F32) + got_ref[rows, 3584:].astype(F32), axis=1, keepdims=True
        )
        high = term.astype(BF).astype(F32)
        low = term - high
        outs[s][:, 3584:] = jnp.where(
            lane == 2 * s, high, jnp.where(lane == 2 * s + 1, low, 0.0)
        ).astype(BF)


def add_to_nodes_kernel(own_ref, got_ref, mark_ref, out_ref):
    row = iota((384, 384), 0)
    block = div3(row >> 3)
    rest = row - 24 * block
    h = jnp.where(rest >= 12, 1, 0)
    rest = rest - 12 * h
    s = div3(rest)
    source = SLOTS * h + ROWS_Y * s + 3 * block + (rest - 3 * s)
    perm = onehot(iota((384, 384), 1) == source).astype(BF)
    total = (own_ref[...].astype(F32) + got_ref[...].astype(F32)).astype(BF)
    out_ref[...] = dot(perm, jnp.concatenate([total[:, :1792], total[:, 1792:]], axis=0)).astype(BF)


def near_tables(y, xs):
    meta = jnp.concatenate([r[:, WIDTH : WIDTH + EXT] for r in xs], axis=0).astype(F32)
    lane = iota((64, 128), 1)
    wanted = jnp.where(lane < N_NODE, 4 * lane + y, -1).astype(F32)
    hot = jnp.zeros((64, 128), F32)
    gate = jnp.zeros((64, 128), F32)
    for k in range(8):
        here = meta[:, k : k + 1] == wanted
        hot = hot + onehot(here)
        gate = gate + jnp.where(here, meta[:, 8 + k : 9 + k], 0.0)
    r64 = iota((64, 64), 0)
    c64 = iota((64, 64), 1)
    tri = onehot((c64 < r64) & ((c64 >> 4) == (r64 >> 4))).astype(BF)
    return hot * (dot(tri, hot.astype(BF)) + 1.0), gate


def combine_near_kernel(place_ref, x0_ref, x1_ref, x2_ref, x3_ref, rows_ref, *outs):
    code, gate = near_tables(place_ref[1], [x0_ref, x1_ref, x2_ref, x3_ref])
    col = iota((128, 384), 1)
    spread = onehot(div3(col >> 3) == iota((128, 384), 0)).astype(BF)
    code = dot(code.astype(BF), spread)
    gate = dot(gate.astype(BF), spread)
    col = iota((64, 384), 1)
    rest = col - 24 * div3(col >> 3)
    half = jnp.where(rest >= 12, 1, 0)
    rest = rest - 12 * half
    s = div3(rest)
    match = (s == (iota((64, 384), 0) >> 4)) & (code == (rest - 3 * s + 1).astype(F32))
    for h in range(2):
        weight = jnp.where(match & (half == h), gate, 0.0).astype(BF)
        total = dot(weight, rows_ref[...]).astype(BF)
        for s in range(N_Y):
            outs[s][:, 1792 * h : 1792 * (h + 1)] = total[TOK * s : TOK * (s + 1)]


def combine_kernel(table_ref, p0_ref, p1_ref, p2_ref, p3_ref, out_ref, rows_ref):
    pieces = [p0_ref, p1_ref, p2_ref, p3_ref]
    lane = iota((128, SLOTS), 1)
    ls = div3(lane >> 4)
    rem = lane - ROWS_Y * ls
    ln = div3(rem)
    lr = rem - 3 * ln
    table = table_ref[...]
    code = jnp.zeros((128, SLOTS), F32)
    gate = jnp.zeros((128, SLOTS), F32)
    for s in range(N_Y):
        code = jnp.where(ls == s, table[:, s : s + 1], code)
        gate = jnp.where(ls == s, table[:, 4 + s : 5 + s], gate)
    match = ((iota((128, SLOTS), 0) >> 3) == ln) & (code == (lr + 1).astype(F32))
    weight = jnp.where(match, gate, 0.0).astype(BF)
    ext = jnp.concatenate([p[:, 3584:] for p in pieces], axis=0)
    terms = dot(onehot(match).astype(BF), ext)
    terms = jnp.concatenate([terms, jnp.zeros((128, 512 - EXT), F32)], axis=1)
    for q in range(7):
        total = dot(weight, jnp.concatenate([p[:, 512 * q : 512 * (q + 1)] for p in pieces], axis=0))
        for n in range(N_NODE):
            at = 40 * n + 5 * q
            rows_ref[at : at + 8, :] = total[8 * n : 8 * n + 8]
    for n in range(N_NODE):
        rows_ref[40 * n + 35 : 40 * n + 40, :] = terms[8 * n : 8 * n + 5]
    out_ref[...] = rows_ref[...].astype(BF)


def finish_kernel(place_ref, routes_ref, a_ref, b0_ref, b1_ref, b2_ref, b3_ref, dx_ref, gg_ref):
    y = place_ref[1]
    routes = by_token(routes_ref[...])
    ncode = node_codes(route_tables(routes, 128))
    col = iota((128, ROWS_N), 1)
    spread = onehot(div40(col) == iota((128, ROWS_N), 0)).astype(BF)
    code = dot(ncode.astype(BF), spread)
    col = iota((TOK, ROWS_N), 1)
    cn = div40(col)
    cp = col - 40 * cn
    cq = div5(cp)
    match = code == (cp - 5 * cq + 1).astype(F32)
    pick = jnp.concatenate([onehot(match & (cq == q)) for q in range(7)], axis=0).astype(BF)
    total = dot(pick, a_ref[...]).astype(BF)
    for q in range(7):
        dx_ref[:, 512 * q : 512 * (q + 1)] = total[TOK * q : TOK * (q + 1)]
    total = b0_ref[...].astype(F32) + b1_ref[...].astype(F32)
    total = total + b2_ref[...].astype(F32) + b3_ref[...].astype(F32)
    dx_ref[:, 3584:] = total.astype(BF)
    last = match & (cq == 7)
    picks = routes.astype(I32)
    masks = jnp.concatenate(
        [onehot(last & (cn == (picks[:, k : k + 1] >> 2))) for k in range(8)], axis=0
    ).astype(BF)
    terms = dot(masks, a_ref[:, :EXT])
    lane = iota((TOK, EXT), 1)
    result = jnp.zeros((TOK, EXT), F32)
    for k in range(8):
        s = ((picks[:, k : k + 1] & 3) - y) & 3
        mine = jnp.where((lane >> 1) == s, terms[TOK * k : TOK * (k + 1)], 0.0)
        result = jnp.where(lane == k, jnp.sum(mine, axis=1, keepdims=True), result)
    gg_ref[...] = result.T[:8]


SMEM = pl.BlockSpec(memory_space=pltpu.SMEM)
VM = pl.BlockSpec(memory_space=pltpu.VMEM)


def sds(shape, dtype=BF):
    return jax.ShapeDtypeStruct(shape, dtype)


def whole(kernel, out_shape, in_specs, name, scratch=()):
    multi = isinstance(out_shape, (list, tuple))
    return pl.pallas_call(
        kernel,
        out_shape=out_shape,
        in_specs=in_specs,
        out_specs=[VM] * len(out_shape) if multi else VM,
        scratch_shapes=list(scratch),
        compiler_params=pltpu.CompilerParams(vmem_limit_bytes=VMEM_LIMITS.get(name, 14) * MIB),
        name=name,
    )


def shift_y(v, s):
    return lax.ppermute(v, "local", [(i, (i + 2 * s) % 8) for i in range(8)])


def swap_core(v):
    return lax.ppermute(v, "local", [(i, i ^ 1) for i in range(8)])


def node_exchange(v):
    shape = v.shape
    v = v.reshape(N_NODE, shape[0] // N_NODE, shape[1])
    return lax.all_to_all(v, "node", split_axis=0, concat_axis=0, tiled=True).reshape(shape)


def on_device(tokens, out_grads, routes, gate_values, gate_weight, up_weight, down_weight):
    w_gate = gate_weight[0]
    w_up = up_weight[0]
    w_down = down_weight[0]
    place = jnp.stack([lax.axis_index("node"), lax.axis_index("local") // 2]).astype(I32)

    dy_send = whole(send_dy_kernel, sds((ROWS_N, 1024)), [VM] * 3, "send_dy")(
        routes.T, gate_values.T, out_grads
    )
    dy_send, tokens = lax.optimization_barrier((dy_send, tokens))
    dy_mid = node_exchange(dy_send)
    picks = jnp.concatenate([routes.astype(BF), gate_values.astype(BF)], axis=1)
    x_own = jnp.concatenate([tokens, jnp.pad(picks, ((0, 0), (0, EXT - 16)))], axis=1)
    x_near = [x_own] + [shift_y(x_own, s) for s in (1, 2, 3)]

    x_send = whole(send_x_kernel, sds((384, 3584)), [SMEM] + [VM] * 4, "send_x")(place, *x_near)
    hbm = pl.BlockSpec(memory_space=pl.ANY)
    *dy_far, meta = whole(
        regroup_far_kernel,
        [sds((ROWS_Y, WIDTH))] * 3 + [sds((ROWS_N, 256))],
        [SMEM, VM],
        "regroup",
    )(place, dy_mid)
    dy_own, down_near = whole(
        regroup_own_kernel,
        [sds((ROWS_Y, WIDTH)), sds((HALF, WIDTH))],
        [SMEM, VM, hbm],
        "regroup_own",
        [pltpu.SemaphoreType.DMA((8,))],
    )(place, dy_mid, w_down)
    x_mine = node_exchange(x_send)
    dy_mine = [dy_own] + [shift_y(dy_far[s - 1], s) for s in (1, 2, 3)]
    dy_other = [swap_core(v) for v in dy_mine]
    table = whole(table_kernel, sds((128, 128), F32), [SMEM, VM], "table")(place, meta)
    back = whole(back_kernel, sds((2 * SLOTS, HALF), F32), [VM] * 9, "back")(
        *dy_mine, *dy_other, down_near
    )
    x_mine, back = lax.optimization_barrier((x_mine, back))
    x_other = swap_core(x_mine)
    pre_gate, pre_up, gate_near, up_near = whole(
        forward_own_kernel,
        [sds((SLOTS, HALF), F32)] * 2 + [sds((WIDTH, HALF))] * 2,
        [VM, hbm, hbm, hbm],
        "forward_own",
        [pltpu.SemaphoreType.DMA((4, 4))],
    )(x_mine, w_gate, w_up, back)
    d_gate, d_up, ext = whole(
        forward_kernel,
        [sds((2 * SLOTS, HALF)), sds((2 * SLOTS, HALF)), sds((2 * SLOTS, EXT))],
        [VM] * 6,
        "forward",
    )(x_other, gate_near, up_near, back, pre_gate, pre_up)

    def dx(part, width):
        return whole(
            functools.partial(dx_kernel, part),
            [sds((SLOTS, width))] * 2,
            [VM] * 5,
            "dx",
        )(d_gate, d_up, gate_near, up_near, ext)

    own_a, other_a = dx(0, 3584 + EXT)
    own_b, other_b = dx(1, 3584)
    got_a = swap_core(other_a)
    got_b = swap_core(other_b)
    *pieces, mark = whole(
        add_kernel,
        [sds((ROWS_Y, 3584 + EXT))] * 4 + [sds((8, 128), F32)],
        [VM] * 2,
        "add_halves",
    )(own_a, got_a)
    pieces = [pieces[0]] + [shift_y(pieces[s], -s) for s in (1, 2, 3)]
    sent_b = whole(add_to_nodes_kernel, sds((384, 1792)), [VM] * 3, "add_to_nodes")(
        own_b, got_b, mark
    )
    back_b = node_exchange(sent_b)
    mixed = whole(
        combine_kernel,
        sds((ROWS_N, 512)),
        [VM] * 5,
        "combine",
        [pltpu.VMEM((ROWS_N, 512), F32)],
    )(table, *pieces)
    mixed, back_b = lax.optimization_barrier((mixed, back_b))
    back_a = node_exchange(mixed)
    near = whole(combine_near_kernel, [sds((TOK, 3584))] * 4, [SMEM] + [VM] * 5, "combine_near")(
        place, *x_near, back_b
    )
    near = [near[0]] + [shift_y(near[s], -s) for s in (1, 2, 3)]
    input_grads, gate_grads = whole(
        finish_kernel, [sds((TOK, WIDTH)), sds((8, TOK), F32)], [SMEM] + [VM] * 6, "finish"
    )(place, routes.T, back_a, *near)
    return input_grads, gate_grads.T


def solution(mesh):
    row = P(("node", "local"), None)
    weight = P(("node", "local"), None, None)
    return jax.shard_map(
        on_device,
        mesh=mesh,
        in_specs=(row, row, row, row, weight, weight, weight),
        out_specs=(row, row),
        check_vma=False,
    )
```

```python
import functools

import jax
import jax.numpy as jnp
from jax import lax
from jax.experimental import pallas as pl
from jax.experimental.pallas import tpu as pltpu
from jax.sharding import PartitionSpec as P

BF = jnp.bfloat16
F32 = jnp.float32
I32 = jnp.int32

N_NODE = 16
N_Y = 4
TOK = 16
CAP_NODE = 5
CAP_EXP = 3
WIDTH = 7168
HALF = 512
ROWS_Y = N_NODE * CAP_EXP
SLOTS = N_Y * ROWS_Y
ROWS_N = N_NODE * 40
EXT = 128
MIB = 1024 * 1024
VMEM_LIMITS = {"send_dy": 60, "regroup_own": 24, "back": 20, "forward_own": 30, "forward": 30, "dx": 24}


def iota(shape, dim):
    return lax.broadcasted_iota(I32, shape, dim)


def div3(v):
    return (v * 171) >> 9


def div5(v):
    return (v * 205) >> 10


def div40(v):
    return div5(v >> 3)


def dot(a, b):
    return jnp.dot(a, b, preferred_element_type=F32)


def dot_nt(a, b):
    return lax.dot_general(a, b, (((1,), (1,)), ((), ())), preferred_element_type=F32)


def dot_tn(a, b):
    return lax.dot_general(a, b, (((0,), (0,)), ((), ())), preferred_element_type=F32)


def onehot(mask):
    return jnp.where(mask, 1.0, 0.0)


def by_token(v):
    return dot_tn(v.astype(F32).astype(BF), onehot(iota((8, 128), 0) == iota((8, 128), 1)).astype(BF))


def route_tables(routes, width):
    lane = (iota((TOK, width), 1) & 63).astype(F32)
    hot = jnp.zeros((TOK, width), F32)
    for k in range(8):
        hot = hot + onehot(routes[:, k : k + 1] == lane)
    return hot


def node_codes(hot):
    width = hot.shape[1]
    row = iota((width, 128), 0)
    group = onehot((row < 64) & ((row >> 2) == iota((width, 128), 1))).astype(BF)
    used = jnp.minimum(dot(hot.astype(BF), group), 1.0)
    tri = onehot(iota((TOK, TOK), 1) < iota((TOK, TOK), 0)).astype(BF)
    return used * (dot(tri, used.astype(BF)) + 1.0)


def send_dy_kernel(routes_ref, gates_ref, dy_ref, out_ref):
    routes = by_token(routes_ref[...])
    gates = by_token(gates_ref[...])
    width = 256
    lane = iota((TOK, width), 1)
    expert = (lane & 63).astype(F32)
    hot = route_tables(routes, width)
    gate = jnp.zeros((TOK, width), F32)
    for k in range(8):
        gate = gate + jnp.where(routes[:, k : k + 1] == expert, gates[:, k : k + 1], 0.0)
    tri = onehot(iota((TOK, TOK), 1) < iota((TOK, TOK), 0)).astype(BF)
    code = hot * (dot(tri, hot.astype(BF)) + 1.0)
    section = lane >> 6
    meta = jnp.where(section == 0, code, jnp.where(section == 1, gate, 0.0)).astype(BF)
    meta = jnp.concatenate([meta, jnp.zeros((TOK, 1024 - width), BF)], axis=1)
    stack = jnp.concatenate([dy_ref[:, 1024 * q : 1024 * (q + 1)] for q in range(7)] + [meta], axis=0)
    ncode = node_codes(hot)
    spread = onehot((iota((TOK, 128), 1) & 15) == iota((TOK, 128), 0)).astype(BF)
    ncode_lane = dot_tn(ncode.astype(BF), spread)[:N_NODE]
    chunk = (iota((N_NODE, 128), 1) >> 4).astype(F32)
    key = jnp.where(ncode_lane > 0.0, 8.0 * chunk + ncode_lane, -1.0)
    row = iota((40, 128), 0)
    q = div5(row)
    row_key = (8 * q + (row - 5 * q) + 1).astype(F32)
    pick = jnp.concatenate([onehot(row_key == key[n : n + 1, :]) for n in range(N_NODE)], axis=0)
    out_ref[...] = dot(pick.astype(BF), stack).astype(BF)


def send_x_kernel(place_ref, x0_ref, x1_ref, x2_ref, x3_ref, out_ref):
    y = place_ref[1]
    xs = [x0_ref, x1_ref, x2_ref, x3_ref]
    code, _ = near_tables(y, xs)
    lane = iota((64, 128), 1)
    spread = onehot((lane & 63) == iota((64, 128), 0)).astype(BF)
    code_lane = dot_tn(code.astype(BF), spread)[:N_NODE]
    block = (iota((N_NODE, 128), 1) >> 4).astype(F32)
    key = jnp.where(code_lane > 0.0, 4.0 * block + code_lane, -1.0)
    row = iota((24, 128), 0)
    b = div3(row)
    row_key = (4 * b + (row - 3 * b) + 1).astype(F32)
    pick = jnp.concatenate([onehot(row_key == key[n : n + 1, :]) for n in range(N_NODE)], axis=0).astype(BF)
    for i in range(7):
        lo = 512 * i
        stack = jnp.concatenate(
            [r[:, lo : lo + 512] for r in xs] + [r[:, 3584 + lo : 3584 + lo + 512] for r in xs], axis=0
        )
        out_ref[:, lo : lo + 512] = dot(pick, stack).astype(BF)


def copy_parts(source, target, sems, first, rows):
    copies = []
    step = rows // sems.shape[0]
    for i in range(sems.shape[0]):
        at = pl.ds(first + step * i, step)
        copies.append(pltpu.make_async_copy(source.at[at], target.at[at], sems.at[i]))
        copies[-1].start()
    return copies


def wait_all(copies):
    for copy in copies:
        copy.wait()


def regroup(shifts, place_ref, rows_ref, outs):
    c = iota((256, 128), 1)
    want = ((c >> 2) << 6) + 4 * place_ref[0] + ((place_ref[1] + c) & 3)
    select = onehot((c < 8) & (iota((256, 128), 0) == want)).astype(BF)
    code = lax.dot_general(
        select, rows_ref[:, :256], (((0,), (1,)), ((), ())), preferred_element_type=F32
    )[:8]
    col = iota((8, ROWS_N), 1)
    n = div40(col)
    key = jnp.where((col - 40 * n >= 35) & (code > 0.0), 4.0 * n.astype(F32) + code, -1.0)
    row = iota((ROWS_Y, ROWS_N), 0)
    rn = div3(row)
    row_key = (4 * rn + (row - 3 * rn) + 1).astype(F32)
    for q in range(7):
        key_q = pltpu.roll(key, ROWS_N - (35 - 5 * q), 1)
        pick = jnp.concatenate([onehot(row_key == key_q[s : s + 1, :]) for s in shifts], axis=0)
        moved = dot(pick.astype(BF), rows_ref[...]).astype(BF)
        for i, out in enumerate(outs):
            out[:, 1024 * q : 1024 * (q + 1)] = moved[ROWS_Y * i : ROWS_Y * (i + 1)]


def regroup_far_kernel(place_ref, rows_ref, out1_ref, out2_ref, out3_ref, meta_ref):
    meta_ref[...] = rows_ref[:, :256]
    regroup((1, 2, 3), place_ref, rows_ref, [out1_ref, out2_ref, out3_ref])


def regroup_own_kernel(place_ref, rows_ref, down_hbm, out_ref, down_ref, sems):
    loads = copy_parts(down_hbm, down_ref, sems, 0, HALF)
    regroup((0,), place_ref, rows_ref, [out_ref])
    wait_all(loads)


def table_kernel(place_ref, meta_ref, table_ref):
    c = iota((256, 128), 1)
    want = ((c >> 2) << 6) + 4 * place_ref[0] + ((place_ref[1] + c) & 3)
    select = onehot((c < 8) & (iota((256, 128), 0) == want)).astype(BF)
    picked = dot(meta_ref[...], select).astype(BF)
    r = iota((128, ROWS_N), 0)
    j = r & 7
    source = jnp.where(j < CAP_NODE, 40 * (r >> 3) + 35 + j, -1)
    table_ref[...] = dot(onehot(iota((128, ROWS_N), 1) == source).astype(BF), picked)


def back_kernel(*refs):
    pieces, down_ref, out_ref = refs[:8], refs[8], refs[9]
    rows = jnp.concatenate([p[...] for p in pieces], axis=0)
    out_ref[...] = dot_nt(rows, down_ref[...])


def slot_order(h):
    row = iota((SLOTS, 384), 0)
    s = div3(row >> 4)
    rem = row - ROWS_Y * s
    n = div3(rem)
    r = rem - 3 * n
    return onehot(iota((SLOTS, 384), 1) == 24 * n + 12 * h + 3 * s + r).astype(BF)


def forward_own_kernel(x_ref, gate_hbm, up_hbm, mark_ref, pg_ref, pu_ref, gate_ref, up_ref, sems):
    loads = []
    for h in range(2):
        loads.append(copy_parts(gate_hbm, gate_ref, sems.at[2 * h], 3584 * h, 3584))
        loads.append(copy_parts(up_hbm, up_ref, sems.at[2 * h + 1], 3584 * h, 3584))
    for h in range(2):
        rows = dot(slot_order(h), x_ref[...]).astype(BF)
        at = slice(3584 * h, 3584 * (h + 1))
        wait_all(loads[2 * h])
        gate = dot(rows, gate_ref[at, :])
        wait_all(loads[2 * h + 1])
        up = dot(rows, up_ref[at, :])
        pg_ref[...] = gate if h == 0 else pg_ref[...] + gate
        pu_ref[...] = up if h == 0 else pu_ref[...] + up


def forward_kernel(
    x_ref, gate_ref, up_ref, back_ref, pg_ref, pu_ref, dgate_ref, dup_ref, ext_ref
):
    pre_gate = jnp.zeros((SLOTS, HALF), F32)
    pre_up = jnp.zeros((SLOTS, HALF), F32)
    for h in range(2):
        rows = dot(slot_order(h), x_ref[...]).astype(BF)
        at = slice(3584 * h, 3584 * (h + 1))
        pre_gate = pre_gate + dot(rows, gate_ref[at, :])
        pre_up = pre_up + dot(rows, up_ref[at, :])
    pre_gate = jnp.concatenate([pg_ref[...], pre_gate], axis=0)
    pre_up = jnp.concatenate([pu_ref[...], pre_up], axis=0)
    back = back_ref[...]
    sig = jax.nn.sigmoid(pre_gate)
    act = pre_gate * sig
    hidden = (act * pre_up).astype(BF)
    part = jnp.sum(hidden.astype(F32) * back, axis=1, keepdims=True)
    dgate_ref[...] = (back * pre_up * sig * (1.0 + pre_gate * (1.0 - sig))).astype(BF)
    dup_ref[...] = (back * act).astype(BF)
    high = part.astype(BF).astype(F32)
    low = part - high
    slot = iota((2 * SLOTS, EXT), 0)
    slot = jnp.where(slot >= SLOTS, slot - SLOTS, slot)
    at = 2 * div3(slot >> 4)
    lane = iota((2 * SLOTS, EXT), 1)
    ext_ref[...] = jnp.where(lane == at, high, jnp.where(lane == at + 1, low, 0.0)).astype(BF)


def dx_kernel(part, dgate_ref, dup_ref, gate_ref, up_ref, ext_ref, own_ref, other_ref):
    cols = slice(3584 * part, 3584 * (part + 1))
    out = (dot_nt(dgate_ref[...], gate_ref[cols, :]) + dot_nt(dup_ref[...], up_ref[cols, :])).astype(BF)
    own_ref[:, :3584] = out[:SLOTS]
    other_ref[:, :3584] = out[SLOTS:]
    if part == 0:
        own_ref[:, 3584:] = ext_ref[:SLOTS]
        other_ref[:, 3584:] = ext_ref[SLOTS:]


def add_kernel(own_ref, got_ref, *outs):
    outs[4][...] = jnp.zeros_like(outs[4])
    lane = iota((ROWS_Y, EXT), 1)
    for s in range(N_Y):
        rows = slice(ROWS_Y * s, ROWS_Y * (s + 1))
        total = own_ref[rows, :3584].astype(F32) + got_ref[rows, :3584].astype(F32)
        outs[s][:, :3584] = total.astype(BF)
        term = jnp.sum(
            own_ref[rows, 3584:].astype(F32) + got_ref[rows, 3584:].astype(F32), axis=1, keepdims=True
        )
        high = term.astype(BF).astype(F32)
        low = term - high
        outs[s][:, 3584:] = jnp.where(
            lane == 2 * s, high, jnp.where(lane == 2 * s + 1, low, 0.0)
        ).astype(BF)


def add_to_nodes_kernel(own_ref, got_ref, mark_ref, out_ref):
    row = iota((384, 384), 0)
    block = div3(row >> 3)
    rest = row - 24 * block
    h = jnp.where(rest >= 12, 1, 0)
    rest = rest - 12 * h
    s = div3(rest)
    source = SLOTS * h + ROWS_Y * s + 3 * block + (rest - 3 * s)
    perm = onehot(iota((384, 384), 1) == source).astype(BF)
    total = (own_ref[...].astype(F32) + got_ref[...].astype(F32)).astype(BF)
    out_ref[...] = dot(perm, jnp.concatenate([total[:, :1792], total[:, 1792:]], axis=0)).astype(BF)


def near_tables(y, xs):
    meta = jnp.concatenate([r[:, WIDTH : WIDTH + EXT] for r in xs], axis=0).astype(F32)
    lane = iota((64, 128), 1)
    wanted = jnp.where(lane < N_NODE, 4 * lane + y, -1).astype(F32)
    hot = jnp.zeros((64, 128), F32)
    gate = jnp.zeros((64, 128), F32)
    for k in range(8):
        here = meta[:, k : k + 1] == wanted
        hot = hot + onehot(here)
        gate = gate + jnp.where(here, meta[:, 8 + k : 9 + k], 0.0)
    r64 = iota((64, 64), 0)
    c64 = iota((64, 64), 1)
    tri = onehot((c64 < r64) & ((c64 >> 4) == (r64 >> 4))).astype(BF)
    return hot * (dot(tri, hot.astype(BF)) + 1.0), gate


def combine_near_kernel(place_ref, x0_ref, x1_ref, x2_ref, x3_ref, rows_ref, *outs):
    code, gate = near_tables(place_ref[1], [x0_ref, x1_ref, x2_ref, x3_ref])
    col = iota((128, 384), 1)
    spread = onehot(div3(col >> 3) == iota((128, 384), 0)).astype(BF)
    code = dot(code.astype(BF), spread)
    gate = dot(gate.astype(BF), spread)
    col = iota((64, 384), 1)
    rest = col - 24 * div3(col >> 3)
    half = jnp.where(rest >= 12, 1, 0)
    rest = rest - 12 * half
    s = div3(rest)
    match = (s == (iota((64, 384), 0) >> 4)) & (code == (rest - 3 * s + 1).astype(F32))
    for h in range(2):
        weight = jnp.where(match & (half == h), gate, 0.0).astype(BF)
        total = dot(weight, rows_ref[...]).astype(BF)
        for s in range(N_Y):
            outs[s][:, 1792 * h : 1792 * (h + 1)] = total[TOK * s : TOK * (s + 1)]


def combine_kernel(table_ref, p0_ref, p1_ref, p2_ref, p3_ref, out_ref, rows_ref):
    pieces = [p0_ref, p1_ref, p2_ref, p3_ref]
    lane = iota((128, SLOTS), 1)
    ls = div3(lane >> 4)
    rem = lane - ROWS_Y * ls
    ln = div3(rem)
    lr = rem - 3 * ln
    table = table_ref[...]
    code = jnp.zeros((128, SLOTS), F32)
    gate = jnp.zeros((128, SLOTS), F32)
    for s in range(N_Y):
        code = jnp.where(ls == s, table[:, s : s + 1], code)
        gate = jnp.where(ls == s, table[:, 4 + s : 5 + s], gate)
    match = ((iota((128, SLOTS), 0) >> 3) == ln) & (code == (lr + 1).astype(F32))
    weight = jnp.where(match, gate, 0.0).astype(BF)
    ext = jnp.concatenate([p[:, 3584:] for p in pieces], axis=0)
    terms = dot(onehot(match).astype(BF), ext)
    terms = jnp.concatenate([terms, jnp.zeros((128, 512 - EXT), F32)], axis=1)
    for q in range(7):
        total = dot(weight, jnp.concatenate([p[:, 512 * q : 512 * (q + 1)] for p in pieces], axis=0))
        for n in range(N_NODE):
            at = 40 * n + 5 * q
            rows_ref[at : at + 8, :] = total[8 * n : 8 * n + 8]
    for n in range(N_NODE):
        rows_ref[40 * n + 35 : 40 * n + 40, :] = terms[8 * n : 8 * n + 5]
    out_ref[...] = rows_ref[...].astype(BF)


def finish_kernel(place_ref, routes_ref, a_ref, b0_ref, b1_ref, b2_ref, b3_ref, dx_ref, gg_ref):
    y = place_ref[1]
    routes = by_token(routes_ref[...])
    ncode = node_codes(route_tables(routes, 128))
    col = iota((128, ROWS_N), 1)
    spread = onehot(div40(col) == iota((128, ROWS_N), 0)).astype(BF)
    code = dot(ncode.astype(BF), spread)
    col = iota((TOK, ROWS_N), 1)
    cn = div40(col)
    cp = col - 40 * cn
    cq = div5(cp)
    match = code == (cp - 5 * cq + 1).astype(F32)
    pick = jnp.concatenate([onehot(match & (cq == q)) for q in range(7)], axis=0).astype(BF)
    total = dot(pick, a_ref[...]).astype(BF)
    for q in range(7):
        dx_ref[:, 512 * q : 512 * (q + 1)] = total[TOK * q : TOK * (q + 1)]
    total = b0_ref[...].astype(F32) + b1_ref[...].astype(F32)
    total = total + b2_ref[...].astype(F32) + b3_ref[...].astype(F32)
    dx_ref[:, 3584:] = total.astype(BF)
    last = match & (cq == 7)
    picks = routes.astype(I32)
    masks = jnp.concatenate(
        [onehot(last & (cn == (picks[:, k : k + 1] >> 2))) for k in range(8)], axis=0
    ).astype(BF)
    terms = dot(masks, a_ref[:, :EXT])
    lane = iota((TOK, EXT), 1)
    result = jnp.zeros((TOK, EXT), F32)
    for k in range(8):
        s = ((picks[:, k : k + 1] & 3) - y) & 3
        mine = jnp.where((lane >> 1) == s, terms[TOK * k : TOK * (k + 1)], 0.0)
        result = jnp.where(lane == k, jnp.sum(mine, axis=1, keepdims=True), result)
    gg_ref[...] = result.T[:8]


SMEM = pl.BlockSpec(memory_space=pltpu.SMEM)
VM = pl.BlockSpec(memory_space=pltpu.VMEM)


def sds(shape, dtype=BF):
    return jax.ShapeDtypeStruct(shape, dtype)


def whole(kernel, out_shape, in_specs, name, scratch=(), cost=None):
    multi = isinstance(out_shape, (list, tuple))
    return pl.pallas_call(
        kernel,
        out_shape=out_shape,
        in_specs=in_specs,
        out_specs=[VM] * len(out_shape) if multi else VM,
        scratch_shapes=list(scratch),
        compiler_params=pltpu.CompilerParams(vmem_limit_bytes=VMEM_LIMITS.get(name, 14) * MIB),
        cost_estimate=cost,
        name=name,
    )


def shift_y(v, s):
    return lax.ppermute(v, "local", [(i, (i + 2 * s) % 8) for i in range(8)])


def swap_core(v):
    return lax.ppermute(v, "local", [(i, i ^ 1) for i in range(8)])


def node_exchange(v):
    shape = v.shape
    v = v.reshape(N_NODE, shape[0] // N_NODE, shape[1])
    return lax.all_to_all(v, "node", split_axis=0, concat_axis=0, tiled=True).reshape(shape)


def on_device(tokens, out_grads, routes, gate_values, gate_weight, up_weight, down_weight):
    w_gate = gate_weight[0]
    w_up = up_weight[0]
    w_down = down_weight[0]
    place = jnp.stack([lax.axis_index("node"), lax.axis_index("local") // 2]).astype(I32)

    dy_send = whole(send_dy_kernel, sds((ROWS_N, 1024)), [VM] * 3, "send_dy")(
        routes.T, gate_values.T, out_grads
    )
    dy_send, tokens = lax.optimization_barrier((dy_send, tokens))
    dy_mid = node_exchange(dy_send)
    picks = jnp.concatenate([routes.astype(BF), gate_values.astype(BF)], axis=1)
    x_own = jnp.concatenate([tokens, jnp.pad(picks, ((0, 0), (0, EXT - 16)))], axis=1)
    x_near = [x_own] + [shift_y(x_own, s) for s in (1, 2, 3)]

    x_send = whole(send_x_kernel, sds((384, 3584)), [SMEM] + [VM] * 4, "send_x")(place, *x_near)
    hbm = pl.BlockSpec(memory_space=pl.ANY)
    *dy_far, meta = whole(
        regroup_far_kernel,
        [sds((ROWS_Y, WIDTH))] * 3 + [sds((ROWS_N, 256))],
        [SMEM, VM],
        "regroup",
    )(place, dy_mid)
    dy_own, down_near = whole(
        regroup_own_kernel,
        [sds((ROWS_Y, WIDTH)), sds((HALF, WIDTH))],
        [SMEM, VM, hbm],
        "regroup_own",
        [pltpu.SemaphoreType.DMA((8,))],
    )(place, dy_mid, w_down)
    x_mine = node_exchange(x_send)
    dy_mine = [dy_own] + [shift_y(dy_far[s - 1], s) for s in (1, 2, 3)]
    dy_other = [swap_core(v) for v in dy_mine]
    table = whole(table_kernel, sds((128, 128), F32), [SMEM, VM], "table")(place, meta)
    back = whole(back_kernel, sds((2 * SLOTS, HALF), F32), [VM] * 9, "back")(
        *dy_mine, *dy_other, down_near
    )
    x_mine, back = lax.optimization_barrier((x_mine, back))
    x_other = swap_core(x_mine)
    pre_gate, pre_up, gate_near, up_near = whole(
        forward_own_kernel,
        [sds((SLOTS, HALF), F32)] * 2 + [sds((WIDTH, HALF))] * 2,
        [VM, hbm, hbm, hbm],
        "forward_own",
        [pltpu.SemaphoreType.DMA((4, 4))],
    )(x_mine, w_gate, w_up, back)
    d_gate, d_up, ext = whole(
        forward_kernel,
        [sds((2 * SLOTS, HALF)), sds((2 * SLOTS, HALF)), sds((2 * SLOTS, EXT))],
        [VM] * 6,
        "forward",
    )(x_other, gate_near, up_near, back, pre_gate, pre_up)

    def dx(part, width):
        return whole(
            functools.partial(dx_kernel, part),
            [sds((SLOTS, width))] * 2,
            [VM] * 5,
            "dx",
        )(d_gate, d_up, gate_near, up_near, ext)

    own_a, other_a = dx(0, 3584 + EXT)
    own_b, other_b = dx(1, 3584)
    got_a = swap_core(other_a)
    got_b = swap_core(other_b)
    *pieces, mark = whole(
        add_kernel,
        [sds((ROWS_Y, 3584 + EXT))] * 4 + [sds((8, 128), F32)],
        [VM] * 2,
        "add_halves",
    )(own_a, got_a)
    pieces = [pieces[0]] + [shift_y(pieces[s], -s) for s in (1, 2, 3)]
    sent_b = whole(add_to_nodes_kernel, sds((384, 1792)), [VM] * 3, "add_to_nodes")(
        own_b, got_b, mark
    )
    back_b = node_exchange(sent_b)
    mixed = whole(
        combine_kernel,
        sds((ROWS_N, 512)),
        [VM] * 5,
        "combine",
        [pltpu.VMEM((ROWS_N, 512), F32)],
        pl.CostEstimate(flops=20_000_000_000, bytes_accessed=70_000_000, transcendentals=0),
    )(table, *pieces)
    mixed, back_b = lax.optimization_barrier((mixed, back_b))
    back_a = node_exchange(mixed)
    near = whole(combine_near_kernel, [sds((TOK, 3584))] * 4, [SMEM] + [VM] * 5, "combine_near")(
        place, *x_near, back_b
    )
    near = [near[0]] + [shift_y(near[s], -s) for s in (1, 2, 3)]
    input_grads, gate_grads = whole(
        finish_kernel, [sds((TOK, WIDTH)), sds((8, TOK), F32)], [SMEM] + [VM] * 6, "finish"
    )(place, routes.T, back_a, *near)
    return input_grads, gate_grads.T


def solution(mesh):
    row = P(("node", "local"), None)
    weight = P(("node", "local"), None, None)
    return jax.shard_map(
        on_device,
        mesh=mesh,
        in_specs=(row, row, row, row, weight, weight, weight),
        out_specs=(row, row),
        check_vma=False,
    )
```

```python
import functools

import jax
import jax.numpy as jnp
from jax import lax
from jax.experimental import pallas as pl
from jax.experimental.pallas import tpu as pltpu
from jax.sharding import PartitionSpec as P

BF = jnp.bfloat16
F32 = jnp.float32
I32 = jnp.int32

N_NODE = 16
N_Y = 4
TOK = 16
CAP_NODE = 5
CAP_EXP = 3
WIDTH = 7168
HALF = 512
ROWS_Y = N_NODE * CAP_EXP
SLOTS = N_Y * ROWS_Y
ROWS_N = N_NODE * 40
EXT = 128
MIB = 1024 * 1024
VMEM_LIMITS = {"send_dy": 60, "regroup_own": 24, "back": 20, "forward_own": 30, "forward": 30, "dx": 24}


def iota(shape, dim):
    return lax.broadcasted_iota(I32, shape, dim)


def div3(v):
    return (v * 171) >> 9


def div5(v):
    return (v * 205) >> 10


def div40(v):
    return div5(v >> 3)


def dot(a, b):
    return jnp.dot(a, b, preferred_element_type=F32)


def dot_nt(a, b):
    return lax.dot_general(a, b, (((1,), (1,)), ((), ())), preferred_element_type=F32)


def dot_tn(a, b):
    return lax.dot_general(a, b, (((0,), (0,)), ((), ())), preferred_element_type=F32)


def onehot(mask):
    return jnp.where(mask, 1.0, 0.0)


def by_token(v):
    return dot_tn(v.astype(F32).astype(BF), onehot(iota((8, 128), 0) == iota((8, 128), 1)).astype(BF))


def route_tables(routes, width):
    lane = (iota((TOK, width), 1) & 63).astype(F32)
    hot = jnp.zeros((TOK, width), F32)
    for k in range(8):
        hot = hot + onehot(routes[:, k : k + 1] == lane)
    return hot


def node_codes(hot):
    width = hot.shape[1]
    row = iota((width, 128), 0)
    group = onehot((row < 64) & ((row >> 2) == iota((width, 128), 1))).astype(BF)
    used = jnp.minimum(dot(hot.astype(BF), group), 1.0)
    tri = onehot(iota((TOK, TOK), 1) < iota((TOK, TOK), 0)).astype(BF)
    return used * (dot(tri, used.astype(BF)) + 1.0)


def send_dy_kernel(routes_ref, gates_ref, dy_ref, out_ref):
    routes = by_token(routes_ref[...])
    gates = by_token(gates_ref[...])
    width = 256
    lane = iota((TOK, width), 1)
    expert = (lane & 63).astype(F32)
    hot = route_tables(routes, width)
    gate = jnp.zeros((TOK, width), F32)
    for k in range(8):
        gate = gate + jnp.where(routes[:, k : k + 1] == expert, gates[:, k : k + 1], 0.0)
    tri = onehot(iota((TOK, TOK), 1) < iota((TOK, TOK), 0)).astype(BF)
    code = hot * (dot(tri, hot.astype(BF)) + 1.0)
    section = lane >> 6
    meta = jnp.where(section == 0, code, jnp.where(section == 1, gate, 0.0)).astype(BF)
    meta = jnp.concatenate([meta, jnp.zeros((TOK, 1024 - width), BF)], axis=1)
    stack = jnp.concatenate([dy_ref[:, 1024 * q : 1024 * (q + 1)] for q in range(7)] + [meta], axis=0)
    ncode = node_codes(hot)
    spread = onehot((iota((TOK, 128), 1) & 15) == iota((TOK, 128), 0)).astype(BF)
    ncode_lane = dot_tn(ncode.astype(BF), spread)[:N_NODE]
    chunk = (iota((N_NODE, 128), 1) >> 4).astype(F32)
    key = jnp.where(ncode_lane > 0.0, 8.0 * chunk + ncode_lane, -1.0)
    row = iota((40, 128), 0)
    q = div5(row)
    row_key = (8 * q + (row - 5 * q) + 1).astype(F32)
    pick = jnp.concatenate([onehot(row_key == key[n : n + 1, :]) for n in range(N_NODE)], axis=0)
    out_ref[...] = dot(pick.astype(BF), stack).astype(BF)


def send_x_kernel(place_ref, x0_ref, x1_ref, x2_ref, x3_ref, out_ref):
    y = place_ref[1]
    xs = [x0_ref, x1_ref, x2_ref, x3_ref]
    code, _ = near_tables(y, xs)
    lane = iota((64, 128), 1)
    spread = onehot((lane & 63) == iota((64, 128), 0)).astype(BF)
    code_lane = dot_tn(code.astype(BF), spread)[:N_NODE]
    block = (iota((N_NODE, 128), 1) >> 4).astype(F32)
    key = jnp.where(code_lane > 0.0, 4.0 * block + code_lane, -1.0)
    row = iota((24, 128), 0)
    b = div3(row)
    row_key = (4 * b + (row - 3 * b) + 1).astype(F32)
    pick = jnp.concatenate([onehot(row_key == key[n : n + 1, :]) for n in range(N_NODE)], axis=0).astype(BF)
    for i in range(7):
        lo = 512 * i
        stack = jnp.concatenate(
            [r[:, lo : lo + 512] for r in xs] + [r[:, 3584 + lo : 3584 + lo + 512] for r in xs], axis=0
        )
        out_ref[:, lo : lo + 512] = dot(pick, stack).astype(BF)


def copy_parts(source, target, sems, first, rows):
    copies = []
    step = rows // sems.shape[0]
    for i in range(sems.shape[0]):
        at = pl.ds(first + step * i, step)
        copies.append(pltpu.make_async_copy(source.at[at], target.at[at], sems.at[i]))
        copies[-1].start()
    return copies


def wait_all(copies):
    for copy in copies:
        copy.wait()


def regroup(shifts, place_ref, rows_ref, outs):
    c = iota((256, 128), 1)
    want = ((c >> 2) << 6) + 4 * place_ref[0] + ((place_ref[1] + c) & 3)
    select = onehot((c < 8) & (iota((256, 128), 0) == want)).astype(BF)
    code = lax.dot_general(
        select, rows_ref[:, :256], (((0,), (1,)), ((), ())), preferred_element_type=F32
    )[:8]
    col = iota((8, ROWS_N), 1)
    n = div40(col)
    key = jnp.where((col - 40 * n >= 35) & (code > 0.0), 4.0 * n.astype(F32) + code, -1.0)
    row = iota((ROWS_Y, ROWS_N), 0)
    rn = div3(row)
    row_key = (4 * rn + (row - 3 * rn) + 1).astype(F32)
    for q in range(7):
        key_q = pltpu.roll(key, ROWS_N - (35 - 5 * q), 1)
        pick = jnp.concatenate([onehot(row_key == key_q[s : s + 1, :]) for s in shifts], axis=0)
        moved = dot(pick.astype(BF), rows_ref[...]).astype(BF)
        for i, out in enumerate(outs):
            out[:, 1024 * q : 1024 * (q + 1)] = moved[ROWS_Y * i : ROWS_Y * (i + 1)]


def regroup_far_kernel(place_ref, rows_ref, out1_ref, out2_ref, out3_ref, meta_ref):
    meta_ref[...] = rows_ref[:, :256]
    regroup((1, 2, 3), place_ref, rows_ref, [out1_ref, out2_ref, out3_ref])


def regroup_own_kernel(place_ref, rows_ref, down_hbm, out_ref, down_ref, sems):
    loads = copy_parts(down_hbm, down_ref, sems, 0, HALF)
    regroup((0,), place_ref, rows_ref, [out_ref])
    wait_all(loads)


def table_kernel(place_ref, meta_ref, mark_ref, table_ref):
    c = iota((256, 128), 1)
    want = ((c >> 2) << 6) + 4 * place_ref[0] + ((place_ref[1] + c) & 3)
    select = onehot((c < 8) & (iota((256, 128), 0) == want)).astype(BF)
    picked = dot(meta_ref[...], select).astype(BF)
    r = iota((128, ROWS_N), 0)
    j = r & 7
    source = jnp.where(j < CAP_NODE, 40 * (r >> 3) + 35 + j, -1)
    table_ref[...] = dot(onehot(iota((128, ROWS_N), 1) == source).astype(BF), picked)


def back_kernel(*refs):
    pieces, down_ref, out_ref = refs[:8], refs[8], refs[9]
    rows = jnp.concatenate([p[...] for p in pieces], axis=0)
    out_ref[...] = dot_nt(rows, down_ref[...])


def slot_order(h):
    row = iota((SLOTS, 384), 0)
    s = div3(row >> 4)
    rem = row - ROWS_Y * s
    n = div3(rem)
    r = rem - 3 * n
    return onehot(iota((SLOTS, 384), 1) == 24 * n + 12 * h + 3 * s + r).astype(BF)


def forward_own_kernel(x_ref, gate_hbm, up_hbm, mark_ref, pg_ref, pu_ref, gate_ref, up_ref, sems):
    loads = []
    for h in range(2):
        loads.append(copy_parts(gate_hbm, gate_ref, sems.at[2 * h], 3584 * h, 3584))
        loads.append(copy_parts(up_hbm, up_ref, sems.at[2 * h + 1], 3584 * h, 3584))
    for h in range(2):
        rows = dot(slot_order(h), x_ref[...]).astype(BF)
        at = slice(3584 * h, 3584 * (h + 1))
        wait_all(loads[2 * h])
        gate = dot(rows, gate_ref[at, :])
        wait_all(loads[2 * h + 1])
        up = dot(rows, up_ref[at, :])
        pg_ref[...] = gate if h == 0 else pg_ref[...] + gate
        pu_ref[...] = up if h == 0 else pu_ref[...] + up


def forward_kernel(
    x_ref, gate_ref, up_ref, back_ref, pg_ref, pu_ref, dgate_ref, dup_ref, ext_ref
):
    pre_gate = jnp.zeros((SLOTS, HALF), F32)
    pre_up = jnp.zeros((SLOTS, HALF), F32)
    for h in range(2):
        rows = dot(slot_order(h), x_ref[...]).astype(BF)
        at = slice(3584 * h, 3584 * (h + 1))
        pre_gate = pre_gate + dot(rows, gate_ref[at, :])
        pre_up = pre_up + dot(rows, up_ref[at, :])
    pre_gate = jnp.concatenate([pg_ref[...], pre_gate], axis=0)
    pre_up = jnp.concatenate([pu_ref[...], pre_up], axis=0)
    back = back_ref[...]
    sig = jax.nn.sigmoid(pre_gate)
    act = pre_gate * sig
    hidden = (act * pre_up).astype(BF)
    part = jnp.sum(hidden.astype(F32) * back, axis=1, keepdims=True)
    dgate_ref[...] = (back * pre_up * sig * (1.0 + pre_gate * (1.0 - sig))).astype(BF)
    dup_ref[...] = (back * act).astype(BF)
    high = part.astype(BF).astype(F32)
    low = part - high
    slot = iota((2 * SLOTS, EXT), 0)
    slot = jnp.where(slot >= SLOTS, slot - SLOTS, slot)
    at = 2 * div3(slot >> 4)
    lane = iota((2 * SLOTS, EXT), 1)
    ext_ref[...] = jnp.where(lane == at, high, jnp.where(lane == at + 1, low, 0.0)).astype(BF)


def dx_kernel(part, dgate_ref, dup_ref, gate_ref, up_ref, ext_ref, own_ref, other_ref):
    cols = slice(3584 * part, 3584 * (part + 1))
    out = (dot_nt(dgate_ref[...], gate_ref[cols, :]) + dot_nt(dup_ref[...], up_ref[cols, :])).astype(BF)
    own_ref[:, :3584] = out[:SLOTS]
    other_ref[:, :3584] = out[SLOTS:]
    if part == 0:
        own_ref[:, 3584:] = ext_ref[:SLOTS]
        other_ref[:, 3584:] = ext_ref[SLOTS:]


def add_kernel(own_ref, got_ref, *outs):
    outs[4][...] = jnp.zeros_like(outs[4])
    lane = iota((ROWS_Y, EXT), 1)
    for s in range(N_Y):
        rows = slice(ROWS_Y * s, ROWS_Y * (s + 1))
        total = own_ref[rows, :3584].astype(F32) + got_ref[rows, :3584].astype(F32)
        outs[s][:, :3584] = total.astype(BF)
        term = jnp.sum(
            own_ref[rows, 3584:].astype(F32) + got_ref[rows, 3584:].astype(F32), axis=1, keepdims=True
        )
        high = term.astype(BF).astype(F32)
        low = term - high
        outs[s][:, 3584:] = jnp.where(
            lane == 2 * s, high, jnp.where(lane == 2 * s + 1, low, 0.0)
        ).astype(BF)


def add_to_nodes_kernel(own_ref, got_ref, mark_ref, out_ref, mark_out):
    mark_out[...] = mark_ref[...]
    row = iota((384, 384), 0)
    block = div3(row >> 3)
    rest = row - 24 * block
    h = jnp.where(rest >= 12, 1, 0)
    rest = rest - 12 * h
    s = div3(rest)
    source = SLOTS * h + ROWS_Y * s + 3 * block + (rest - 3 * s)
    perm = onehot(iota((384, 384), 1) == source).astype(BF)
    total = (own_ref[...].astype(F32) + got_ref[...].astype(F32)).astype(BF)
    out_ref[...] = dot(perm, jnp.concatenate([total[:, :1792], total[:, 1792:]], axis=0)).astype(BF)


def near_tables(y, xs):
    meta = jnp.concatenate([r[:, WIDTH : WIDTH + EXT] for r in xs], axis=0).astype(F32)
    lane = iota((64, 128), 1)
    wanted = jnp.where(lane < N_NODE, 4 * lane + y, -1).astype(F32)
    hot = jnp.zeros((64, 128), F32)
    gate = jnp.zeros((64, 128), F32)
    for k in range(8):
        here = meta[:, k : k + 1] == wanted
        hot = hot + onehot(here)
        gate = gate + jnp.where(here, meta[:, 8 + k : 9 + k], 0.0)
    r64 = iota((64, 64), 0)
    c64 = iota((64, 64), 1)
    tri = onehot((c64 < r64) & ((c64 >> 4) == (r64 >> 4))).astype(BF)
    return hot * (dot(tri, hot.astype(BF)) + 1.0), gate


def combine_near_kernel(place_ref, x0_ref, x1_ref, x2_ref, x3_ref, rows_ref, *outs):
    code, gate = near_tables(place_ref[1], [x0_ref, x1_ref, x2_ref, x3_ref])
    col = iota((128, 384), 1)
    spread = onehot(div3(col >> 3) == iota((128, 384), 0)).astype(BF)
    code = dot(code.astype(BF), spread)
    gate = dot(gate.astype(BF), spread)
    col = iota((64, 384), 1)
    rest = col - 24 * div3(col >> 3)
    half = jnp.where(rest >= 12, 1, 0)
    rest = rest - 12 * half
    s = div3(rest)
    match = (s == (iota((64, 384), 0) >> 4)) & (code == (rest - 3 * s + 1).astype(F32))
    for h in range(2):
        weight = jnp.where(match & (half == h), gate, 0.0).astype(BF)
        total = dot(weight, rows_ref[...]).astype(BF)
        for s in range(N_Y):
            outs[s][:, 1792 * h : 1792 * (h + 1)] = total[TOK * s : TOK * (s + 1)]


def combine_kernel(table_ref, p0_ref, p1_ref, p2_ref, p3_ref, out_ref, rows_ref):
    pieces = [p0_ref, p1_ref, p2_ref, p3_ref]
    lane = iota((128, SLOTS), 1)
    ls = div3(lane >> 4)
    rem = lane - ROWS_Y * ls
    ln = div3(rem)
    lr = rem - 3 * ln
    table = table_ref[...]
    code = jnp.zeros((128, SLOTS), F32)
    gate = jnp.zeros((128, SLOTS), F32)
    for s in range(N_Y):
        code = jnp.where(ls == s, table[:, s : s + 1], code)
        gate = jnp.where(ls == s, table[:, 4 + s : 5 + s], gate)
    match = ((iota((128, SLOTS), 0) >> 3) == ln) & (code == (lr + 1).astype(F32))
    weight = jnp.where(match, gate, 0.0).astype(BF)
    ext = jnp.concatenate([p[:, 3584:] for p in pieces], axis=0)
    terms = dot(onehot(match).astype(BF), ext)
    terms = jnp.concatenate([terms, jnp.zeros((128, 512 - EXT), F32)], axis=1)
    for q in range(7):
        total = dot(weight, jnp.concatenate([p[:, 512 * q : 512 * (q + 1)] for p in pieces], axis=0))
        for n in range(N_NODE):
            at = 40 * n + 5 * q
            rows_ref[at : at + 8, :] = total[8 * n : 8 * n + 8]
    for n in range(N_NODE):
        rows_ref[40 * n + 35 : 40 * n + 40, :] = terms[8 * n : 8 * n + 5]
    out_ref[...] = rows_ref[...].astype(BF)


def finish_kernel(place_ref, routes_ref, a_ref, b0_ref, b1_ref, b2_ref, b3_ref, dx_ref, gg_ref):
    y = place_ref[1]
    routes = by_token(routes_ref[...])
    ncode = node_codes(route_tables(routes, 128))
    col = iota((128, ROWS_N), 1)
    spread = onehot(div40(col) == iota((128, ROWS_N), 0)).astype(BF)
    code = dot(ncode.astype(BF), spread)
    col = iota((TOK, ROWS_N), 1)
    cn = div40(col)
    cp = col - 40 * cn
    cq = div5(cp)
    match = code == (cp - 5 * cq + 1).astype(F32)
    pick = jnp.concatenate([onehot(match & (cq == q)) for q in range(7)], axis=0).astype(BF)
    total = dot(pick, a_ref[...]).astype(BF)
    for q in range(7):
        dx_ref[:, 512 * q : 512 * (q + 1)] = total[TOK * q : TOK * (q + 1)]
    total = b0_ref[...].astype(F32) + b1_ref[...].astype(F32)
    total = total + b2_ref[...].astype(F32) + b3_ref[...].astype(F32)
    dx_ref[:, 3584:] = total.astype(BF)
    last = match & (cq == 7)
    picks = routes.astype(I32)
    masks = jnp.concatenate(
        [onehot(last & (cn == (picks[:, k : k + 1] >> 2))) for k in range(8)], axis=0
    ).astype(BF)
    terms = dot(masks, a_ref[:, :EXT])
    lane = iota((TOK, EXT), 1)
    result = jnp.zeros((TOK, EXT), F32)
    for k in range(8):
        s = ((picks[:, k : k + 1] & 3) - y) & 3
        mine = jnp.where((lane >> 1) == s, terms[TOK * k : TOK * (k + 1)], 0.0)
        result = jnp.where(lane == k, jnp.sum(mine, axis=1, keepdims=True), result)
    gg_ref[...] = result.T[:8]


SMEM = pl.BlockSpec(memory_space=pltpu.SMEM)
VM = pl.BlockSpec(memory_space=pltpu.VMEM)


def sds(shape, dtype=BF):
    return jax.ShapeDtypeStruct(shape, dtype)


def whole(kernel, out_shape, in_specs, name, scratch=(), cost=None):
    multi = isinstance(out_shape, (list, tuple))
    return pl.pallas_call(
        kernel,
        out_shape=out_shape,
        in_specs=in_specs,
        out_specs=[VM] * len(out_shape) if multi else VM,
        scratch_shapes=list(scratch),
        compiler_params=pltpu.CompilerParams(vmem_limit_bytes=VMEM_LIMITS.get(name, 14) * MIB),
        cost_estimate=cost,
        name=name,
    )


def shift_y(v, s):
    return lax.ppermute(v, "local", [(i, (i + 2 * s) % 8) for i in range(8)])


def swap_core(v):
    return lax.ppermute(v, "local", [(i, i ^ 1) for i in range(8)])


def node_exchange(v):
    shape = v.shape
    v = v.reshape(N_NODE, shape[0] // N_NODE, shape[1])
    return lax.all_to_all(v, "node", split_axis=0, concat_axis=0, tiled=True).reshape(shape)


def on_device(tokens, out_grads, routes, gate_values, gate_weight, up_weight, down_weight):
    w_gate = gate_weight[0]
    w_up = up_weight[0]
    w_down = down_weight[0]
    place = jnp.stack([lax.axis_index("node"), lax.axis_index("local") // 2]).astype(I32)

    dy_send = whole(send_dy_kernel, sds((ROWS_N, 1024)), [VM] * 3, "send_dy")(
        routes.T, gate_values.T, out_grads
    )
    dy_send, tokens = lax.optimization_barrier((dy_send, tokens))
    dy_mid = node_exchange(dy_send)
    picks = jnp.concatenate([routes.astype(BF), gate_values.astype(BF)], axis=1)
    x_own = jnp.concatenate([tokens, jnp.pad(picks, ((0, 0), (0, EXT - 16)))], axis=1)
    x_near = [x_own] + [shift_y(x_own, s) for s in (1, 2, 3)]

    x_send = whole(send_x_kernel, sds((384, 3584)), [SMEM] + [VM] * 4, "send_x")(place, *x_near)
    hbm = pl.BlockSpec(memory_space=pl.ANY)
    *dy_far, meta = whole(
        regroup_far_kernel,
        [sds((ROWS_Y, WIDTH))] * 3 + [sds((ROWS_N, 256))],
        [SMEM, VM],
        "regroup",
    )(place, dy_mid)
    dy_own, down_near = whole(
        regroup_own_kernel,
        [sds((ROWS_Y, WIDTH)), sds((HALF, WIDTH))],
        [SMEM, VM, hbm],
        "regroup_own",
        [pltpu.SemaphoreType.DMA((8,))],
    )(place, dy_mid, w_down)
    x_mine = node_exchange(x_send)
    dy_mine = [dy_own] + [shift_y(dy_far[s - 1], s) for s in (1, 2, 3)]
    dy_other = [swap_core(v) for v in dy_mine]
    back = whole(back_kernel, sds((2 * SLOTS, HALF), F32), [VM] * 9, "back")(
        *dy_mine, *dy_other, down_near
    )
    x_mine, back = lax.optimization_barrier((x_mine, back))
    x_other = swap_core(x_mine)
    pre_gate, pre_up, gate_near, up_near = whole(
        forward_own_kernel,
        [sds((SLOTS, HALF), F32)] * 2 + [sds((WIDTH, HALF))] * 2,
        [VM, hbm, hbm, hbm],
        "forward_own",
        [pltpu.SemaphoreType.DMA((4, 4))],
    )(x_mine, w_gate, w_up, back)
    d_gate, d_up, ext = whole(
        forward_kernel,
        [sds((2 * SLOTS, HALF)), sds((2 * SLOTS, HALF)), sds((2 * SLOTS, EXT))],
        [VM] * 6,
        "forward",
    )(x_other, gate_near, up_near, back, pre_gate, pre_up)

    def dx(part, width):
        return whole(
            functools.partial(dx_kernel, part),
            [sds((SLOTS, width))] * 2,
            [VM] * 5,
            "dx",
        )(d_gate, d_up, gate_near, up_near, ext)

    own_a, other_a = dx(0, 3584 + EXT)
    own_b, other_b = dx(1, 3584)
    got_a = swap_core(other_a)
    got_b = swap_core(other_b)
    *pieces, mark = whole(
        add_kernel,
        [sds((ROWS_Y, 3584 + EXT))] * 4 + [sds((8, 128), F32)],
        [VM] * 2,
        "add_halves",
    )(own_a, got_a)
    pieces = [pieces[0]] + [shift_y(pieces[s], -s) for s in (1, 2, 3)]
    sent_b, mark = whole(
        add_to_nodes_kernel, [sds((384, 1792)), sds((8, 128), F32)], [VM] * 3, "add_to_nodes"
    )(own_b, got_b, mark)
    table = whole(table_kernel, sds((128, 128), F32), [SMEM, VM, VM], "table")(place, meta, mark)
    back_b = node_exchange(sent_b)
    mixed = whole(
        combine_kernel,
        sds((ROWS_N, 512)),
        [VM] * 5,
        "combine",
        [pltpu.VMEM((ROWS_N, 512), F32)],
        pl.CostEstimate(flops=20_000_000_000, bytes_accessed=70_000_000, transcendentals=0),
    )(table, *pieces)
    mixed, back_b = lax.optimization_barrier((mixed, back_b))
    back_a = node_exchange(mixed)
    near = whole(combine_near_kernel, [sds((TOK, 3584))] * 4, [SMEM] + [VM] * 5, "combine_near")(
        place, *x_near, back_b
    )
    near = [near[0]] + [shift_y(near[s], -s) for s in (1, 2, 3)]
    input_grads, gate_grads = whole(
        finish_kernel, [sds((TOK, WIDTH)), sds((8, TOK), F32)], [SMEM] + [VM] * 6, "finish"
    )(place, routes.T, back_a, *near)
    return input_grads, gate_grads.T


def solution(mesh):
    row = P(("node", "local"), None)
    weight = P(("node", "local"), None, None)
    return jax.shard_map(
        on_device,
        mesh=mesh,
        in_specs=(row, row, row, row, weight, weight, weight),
        out_specs=(row, row),
        check_vma=False,
    )
```

```python
import functools

import jax
import jax.numpy as jnp
from jax import lax
from jax.experimental import pallas as pl
from jax.experimental.pallas import tpu as pltpu
from jax.sharding import PartitionSpec as P

BF = jnp.bfloat16
F32 = jnp.float32
I32 = jnp.int32

N_NODE = 16
N_Y = 4
TOK = 16
CAP_NODE = 5
CAP_EXP = 3
WIDTH = 7168
HALF = 512
ROWS_Y = N_NODE * CAP_EXP
SLOTS = N_Y * ROWS_Y
ROWS_N = N_NODE * 40
EXT = 128
A_PARTS = 15
A_CHUNK = 256
A_WIDTH = A_PARTS * A_CHUNK
A_BLOCK = 5 * (A_PARTS + 1)
ROWS_A = N_NODE * A_BLOCK
B_WIDTH = WIDTH - A_WIDTH
B_HALF = B_WIDTH // 2
MIB = 1024 * 1024
VMEM_LIMITS = {"send_dy": 60, "regroup_own": 24, "back": 20, "forward_own": 30, "forward": 30, "dx": 24}


def iota(shape, dim):
    return lax.broadcasted_iota(I32, shape, dim)


def div3(v):
    return (v * 171) >> 9


def div5(v):
    return (v * 205) >> 10


def div40(v):
    return div5(v >> 3)


def dot(a, b):
    return jnp.dot(a, b, preferred_element_type=F32)


def dot_nt(a, b):
    return lax.dot_general(a, b, (((1,), (1,)), ((), ())), preferred_element_type=F32)


def dot_tn(a, b):
    return lax.dot_general(a, b, (((0,), (0,)), ((), ())), preferred_element_type=F32)


def onehot(mask):
    return jnp.where(mask, 1.0, 0.0)


def by_token(v):
    return dot_tn(v.astype(F32).astype(BF), onehot(iota((8, 128), 0) == iota((8, 128), 1)).astype(BF))


def route_tables(routes, width):
    lane = (iota((TOK, width), 1) & 63).astype(F32)
    hot = jnp.zeros((TOK, width), F32)
    for k in range(8):
        hot = hot + onehot(routes[:, k : k + 1] == lane)
    return hot


def node_codes(hot):
    width = hot.shape[1]
    row = iota((width, 128), 0)
    group = onehot((row < 64) & ((row >> 2) == iota((width, 128), 1))).astype(BF)
    used = jnp.minimum(dot(hot.astype(BF), group), 1.0)
    tri = onehot(iota((TOK, TOK), 1) < iota((TOK, TOK), 0)).astype(BF)
    return used * (dot(tri, used.astype(BF)) + 1.0)


def send_dy_kernel(routes_ref, gates_ref, dy_ref, out_ref):
    routes = by_token(routes_ref[...])
    gates = by_token(gates_ref[...])
    width = 256
    lane = iota((TOK, width), 1)
    expert = (lane & 63).astype(F32)
    hot = route_tables(routes, width)
    gate = jnp.zeros((TOK, width), F32)
    for k in range(8):
        gate = gate + jnp.where(routes[:, k : k + 1] == expert, gates[:, k : k + 1], 0.0)
    tri = onehot(iota((TOK, TOK), 1) < iota((TOK, TOK), 0)).astype(BF)
    code = hot * (dot(tri, hot.astype(BF)) + 1.0)
    section = lane >> 6
    meta = jnp.where(section == 0, code, jnp.where(section == 1, gate, 0.0)).astype(BF)
    meta = jnp.concatenate([meta, jnp.zeros((TOK, 1024 - width), BF)], axis=1)
    stack = jnp.concatenate([dy_ref[:, 1024 * q : 1024 * (q + 1)] for q in range(7)] + [meta], axis=0)
    ncode = node_codes(hot)
    spread = onehot((iota((TOK, 128), 1) & 15) == iota((TOK, 128), 0)).astype(BF)
    ncode_lane = dot_tn(ncode.astype(BF), spread)[:N_NODE]
    chunk = (iota((N_NODE, 128), 1) >> 4).astype(F32)
    key = jnp.where(ncode_lane > 0.0, 8.0 * chunk + ncode_lane, -1.0)
    row = iota((40, 128), 0)
    q = div5(row)
    row_key = (8 * q + (row - 5 * q) + 1).astype(F32)
    pick = jnp.concatenate([onehot(row_key == key[n : n + 1, :]) for n in range(N_NODE)], axis=0)
    out_ref[...] = dot(pick.astype(BF), stack).astype(BF)


def send_x_kernel(place_ref, x0_ref, x1_ref, x2_ref, x3_ref, out_ref):
    y = place_ref[1]
    xs = [x0_ref, x1_ref, x2_ref, x3_ref]
    code, _ = near_tables(y, xs)
    lane = iota((64, 128), 1)
    spread = onehot((lane & 63) == iota((64, 128), 0)).astype(BF)
    code_lane = dot_tn(code.astype(BF), spread)[:N_NODE]
    block = (iota((N_NODE, 128), 1) >> 4).astype(F32)
    key = jnp.where(code_lane > 0.0, 4.0 * block + code_lane, -1.0)
    row = iota((24, 128), 0)
    b = div3(row)
    row_key = (4 * b + (row - 3 * b) + 1).astype(F32)
    pick = jnp.concatenate([onehot(row_key == key[n : n + 1, :]) for n in range(N_NODE)], axis=0).astype(BF)
    for i in range(7):
        lo = 512 * i
        stack = jnp.concatenate(
            [r[:, lo : lo + 512] for r in xs] + [r[:, 3584 + lo : 3584 + lo + 512] for r in xs], axis=0
        )
        out_ref[:, lo : lo + 512] = dot(pick, stack).astype(BF)


def copy_parts(source, target, sems, first, rows):
    copies = []
    step = rows // sems.shape[0]
    for i in range(sems.shape[0]):
        at = pl.ds(first + step * i, step)
        copies.append(pltpu.make_async_copy(source.at[at], target.at[at], sems.at[i]))
        copies[-1].start()
    return copies


def wait_all(copies):
    for copy in copies:
        copy.wait()


def regroup(shifts, place_ref, rows_ref, outs):
    c = iota((256, 128), 1)
    want = ((c >> 2) << 6) + 4 * place_ref[0] + ((place_ref[1] + c) & 3)
    select = onehot((c < 8) & (iota((256, 128), 0) == want)).astype(BF)
    code = lax.dot_general(
        select, rows_ref[:, :256], (((0,), (1,)), ((), ())), preferred_element_type=F32
    )[:8]
    col = iota((8, ROWS_N), 1)
    n = div40(col)
    key = jnp.where((col - 40 * n >= 35) & (code > 0.0), 4.0 * n.astype(F32) + code, -1.0)
    row = iota((ROWS_Y, ROWS_N), 0)
    rn = div3(row)
    row_key = (4 * rn + (row - 3 * rn) + 1).astype(F32)
    for q in range(7):
        key_q = pltpu.roll(key, ROWS_N - (35 - 5 * q), 1)
        pick = jnp.concatenate([onehot(row_key == key_q[s : s + 1, :]) for s in shifts], axis=0)
        moved = dot(pick.astype(BF), rows_ref[...]).astype(BF)
        for i, out in enumerate(outs):
            out[:, 1024 * q : 1024 * (q + 1)] = moved[ROWS_Y * i : ROWS_Y * (i + 1)]


def regroup_far_kernel(place_ref, rows_ref, out1_ref, out2_ref, out3_ref, meta_ref):
    meta_ref[...] = rows_ref[:, :256]
    regroup((1, 2, 3), place_ref, rows_ref, [out1_ref, out2_ref, out3_ref])


def regroup_own_kernel(place_ref, rows_ref, down_hbm, out_ref, down_ref, sems):
    loads = copy_parts(down_hbm, down_ref, sems, 0, HALF)
    regroup((0,), place_ref, rows_ref, [out_ref])
    wait_all(loads)


def table_kernel(place_ref, meta_ref, mark_ref, table_ref):
    c = iota((256, 128), 1)
    want = ((c >> 2) << 6) + 4 * place_ref[0] + ((place_ref[1] + c) & 3)
    select = onehot((c < 8) & (iota((256, 128), 0) == want)).astype(BF)
    picked = dot(meta_ref[...], select).astype(BF)
    r = iota((128, ROWS_N), 0)
    j = r & 7
    source = jnp.where(j < CAP_NODE, 40 * (r >> 3) + 35 + j, -1)
    table_ref[...] = dot(onehot(iota((128, ROWS_N), 1) == source).astype(BF), picked)


def back_kernel(*refs):
    pieces, down_ref, out_ref = refs[:8], refs[8], refs[9]
    rows = jnp.concatenate([p[...] for p in pieces], axis=0)
    out_ref[...] = dot_nt(rows, down_ref[...])


def slot_order(h):
    row = iota((SLOTS, 384), 0)
    s = div3(row >> 4)
    rem = row - ROWS_Y * s
    n = div3(rem)
    r = rem - 3 * n
    return onehot(iota((SLOTS, 384), 1) == 24 * n + 12 * h + 3 * s + r).astype(BF)


def forward_own_kernel(x_ref, gate_hbm, up_hbm, mark_ref, pg_ref, pu_ref, gate_ref, up_ref, sems):
    loads = []
    for h in range(2):
        loads.append(copy_parts(gate_hbm, gate_ref, sems.at[2 * h], 3584 * h, 3584))
        loads.append(copy_parts(up_hbm, up_ref, sems.at[2 * h + 1], 3584 * h, 3584))
    for h in range(2):
        rows = dot(slot_order(h), x_ref[...]).astype(BF)
        at = slice(3584 * h, 3584 * (h + 1))
        wait_all(loads[2 * h])
        gate = dot(rows, gate_ref[at, :])
        wait_all(loads[2 * h + 1])
        up = dot(rows, up_ref[at, :])
        pg_ref[...] = gate if h == 0 else pg_ref[...] + gate
        pu_ref[...] = up if h == 0 else pu_ref[...] + up


def forward_kernel(
    x_ref, gate_ref, up_ref, back_ref, pg_ref, pu_ref, dgate_ref, dup_ref, ext_ref
):
    pre_gate = jnp.zeros((SLOTS, HALF), F32)
    pre_up = jnp.zeros((SLOTS, HALF), F32)
    for h in range(2):
        rows = dot(slot_order(h), x_ref[...]).astype(BF)
        at = slice(3584 * h, 3584 * (h + 1))
        pre_gate = pre_gate + dot(rows, gate_ref[at, :])
        pre_up = pre_up + dot(rows, up_ref[at, :])
    pre_gate = jnp.concatenate([pg_ref[...], pre_gate], axis=0)
    pre_up = jnp.concatenate([pu_ref[...], pre_up], axis=0)
    back = back_ref[...]
    sig = jax.nn.sigmoid(pre_gate)
    act = pre_gate * sig
    hidden = (act * pre_up).astype(BF)
    part = jnp.sum(hidden.astype(F32) * back, axis=1, keepdims=True)
    dgate_ref[...] = (back * pre_up * sig * (1.0 + pre_gate * (1.0 - sig))).astype(BF)
    dup_ref[...] = (back * act).astype(BF)
    high = part.astype(BF).astype(F32)
    low = part - high
    slot = iota((2 * SLOTS, EXT), 0)
    slot = jnp.where(slot >= SLOTS, slot - SLOTS, slot)
    at = 2 * div3(slot >> 4)
    lane = iota((2 * SLOTS, EXT), 1)
    ext_ref[...] = jnp.where(lane == at, high, jnp.where(lane == at + 1, low, 0.0)).astype(BF)


def dx_kernel(part, dgate_ref, dup_ref, gate_ref, up_ref, ext_ref, own_ref, other_ref):
    cols = slice(A_WIDTH, WIDTH) if part else slice(0, A_WIDTH)
    width = cols.stop - cols.start
    out = (dot_nt(dgate_ref[...], gate_ref[cols, :]) + dot_nt(dup_ref[...], up_ref[cols, :])).astype(BF)
    own_ref[:, :width] = out[:SLOTS]
    other_ref[:, :width] = out[SLOTS:]
    if part == 0:
        own_ref[:, A_WIDTH:] = ext_ref[:SLOTS]
        other_ref[:, A_WIDTH:] = ext_ref[SLOTS:]


def add_kernel(own_ref, got_ref, *outs):
    outs[4][...] = jnp.zeros_like(outs[4])
    lane = iota((ROWS_Y, EXT), 1)
    for s in range(N_Y):
        rows = slice(ROWS_Y * s, ROWS_Y * (s + 1))
        total = own_ref[rows, :A_WIDTH].astype(F32) + got_ref[rows, :A_WIDTH].astype(F32)
        outs[s][:, :A_WIDTH] = total.astype(BF)
        term = jnp.sum(
            own_ref[rows, A_WIDTH:].astype(F32) + got_ref[rows, A_WIDTH:].astype(F32), axis=1, keepdims=True
        )
        high = term.astype(BF).astype(F32)
        low = term - high
        outs[s][:, A_WIDTH:] = jnp.where(
            lane == 2 * s, high, jnp.where(lane == 2 * s + 1, low, 0.0)
        ).astype(BF)


def add_to_nodes_kernel(own_ref, got_ref, mark_ref, out_ref, mark_out):
    mark_out[...] = mark_ref[...]
    row = iota((384, 384), 0)
    block = div3(row >> 3)
    rest = row - 24 * block
    h = jnp.where(rest >= 12, 1, 0)
    rest = rest - 12 * h
    s = div3(rest)
    source = SLOTS * h + ROWS_Y * s + 3 * block + (rest - 3 * s)
    perm = onehot(iota((384, 384), 1) == source).astype(BF)
    total = (own_ref[...].astype(F32) + got_ref[...].astype(F32)).astype(BF)
    out_ref[...] = dot(perm, jnp.concatenate([total[:, :B_HALF], total[:, B_HALF:]], axis=0)).astype(BF)


def near_tables(y, xs):
    meta = jnp.concatenate([r[:, WIDTH : WIDTH + EXT] for r in xs], axis=0).astype(F32)
    lane = iota((64, 128), 1)
    wanted = jnp.where(lane < N_NODE, 4 * lane + y, -1).astype(F32)
    hot = jnp.zeros((64, 128), F32)
    gate = jnp.zeros((64, 128), F32)
    for k in range(8):
        here = meta[:, k : k + 1] == wanted
        hot = hot + onehot(here)
        gate = gate + jnp.where(here, meta[:, 8 + k : 9 + k], 0.0)
    r64 = iota((64, 64), 0)
    c64 = iota((64, 64), 1)
    tri = onehot((c64 < r64) & ((c64 >> 4) == (r64 >> 4))).astype(BF)
    return hot * (dot(tri, hot.astype(BF)) + 1.0), gate


def combine_near_kernel(place_ref, x0_ref, x1_ref, x2_ref, x3_ref, rows_ref, *outs):
    code, gate = near_tables(place_ref[1], [x0_ref, x1_ref, x2_ref, x3_ref])
    col = iota((128, 384), 1)
    spread = onehot(div3(col >> 3) == iota((128, 384), 0)).astype(BF)
    code = dot(code.astype(BF), spread)
    gate = dot(gate.astype(BF), spread)
    col = iota((64, 384), 1)
    rest = col - 24 * div3(col >> 3)
    half = jnp.where(rest >= 12, 1, 0)
    rest = rest - 12 * half
    s = div3(rest)
    match = (s == (iota((64, 384), 0) >> 4)) & (code == (rest - 3 * s + 1).astype(F32))
    for h in range(2):
        weight = jnp.where(match & (half == h), gate, 0.0).astype(BF)
        total = dot(weight, rows_ref[...]).astype(BF)
        for s in range(N_Y):
            outs[s][:, B_HALF * h : B_HALF * (h + 1)] = total[TOK * s : TOK * (s + 1)]


def combine_kernel(table_ref, p0_ref, p1_ref, p2_ref, p3_ref, out_ref, rows_ref):
    pieces = [p0_ref, p1_ref, p2_ref, p3_ref]
    lane = iota((128, SLOTS), 1)
    ls = div3(lane >> 4)
    rem = lane - ROWS_Y * ls
    ln = div3(rem)
    lr = rem - 3 * ln
    table = table_ref[...]
    code = jnp.zeros((128, SLOTS), F32)
    gate = jnp.zeros((128, SLOTS), F32)
    for s in range(N_Y):
        code = jnp.where(ls == s, table[:, s : s + 1], code)
        gate = jnp.where(ls == s, table[:, 4 + s : 5 + s], gate)
    match = ((iota((128, SLOTS), 0) >> 3) == ln) & (code == (lr + 1).astype(F32))
    weight = jnp.where(match, gate, 0.0).astype(BF)
    ext = jnp.concatenate([p[:, A_WIDTH:] for p in pieces], axis=0)
    terms = dot(onehot(match).astype(BF), ext)
    terms = jnp.concatenate([terms, jnp.zeros((128, A_CHUNK - EXT), F32)], axis=1)
    for q in range(A_PARTS):
        total = dot(weight, jnp.concatenate([p[:, A_CHUNK * q : A_CHUNK * (q + 1)] for p in pieces], axis=0))
        for n in range(N_NODE):
            at = A_BLOCK * n + 5 * q
            rows_ref[at : at + 8, :] = total[8 * n : 8 * n + 8]
    for n in range(N_NODE):
        rows_ref[A_BLOCK * (n + 1) - 5 : A_BLOCK * (n + 1), :] = terms[8 * n : 8 * n + 5]
    out_ref[...] = rows_ref[...].astype(BF)


def finish_kernel(place_ref, routes_ref, a_ref, b0_ref, b1_ref, b2_ref, b3_ref, dx_ref, gg_ref):
    y = place_ref[1]
    routes = by_token(routes_ref[...])
    ncode = node_codes(route_tables(routes, 128))
    col = iota((128, ROWS_A), 1)
    spread = onehot(div5(col >> 4) == iota((128, ROWS_A), 0)).astype(BF)
    code = dot(ncode.astype(BF), spread)
    col = iota((TOK, ROWS_A), 1)
    cn = div5(col >> 4)
    cp = col - A_BLOCK * cn
    cq = div5(cp)
    match = code == (cp - 5 * cq + 1).astype(F32)
    pick = jnp.concatenate([onehot(match & (cq == q)) for q in range(A_PARTS)], axis=0).astype(BF)
    total = dot(pick, a_ref[...]).astype(BF)
    for q in range(A_PARTS):
        dx_ref[:, A_CHUNK * q : A_CHUNK * (q + 1)] = total[TOK * q : TOK * (q + 1)]
    total = b0_ref[...].astype(F32) + b1_ref[...].astype(F32)
    total = total + b2_ref[...].astype(F32) + b3_ref[...].astype(F32)
    dx_ref[:, A_WIDTH:] = total.astype(BF)
    last = match & (cq == A_PARTS)
    picks = routes.astype(I32)
    masks = jnp.concatenate(
        [onehot(last & (cn == (picks[:, k : k + 1] >> 2))) for k in range(8)], axis=0
    ).astype(BF)
    terms = dot(masks, a_ref[:, :EXT])
    lane = iota((TOK, EXT), 1)
    result = jnp.zeros((TOK, EXT), F32)
    for k in range(8):
        s = ((picks[:, k : k + 1] & 3) - y) & 3
        mine = jnp.where((lane >> 1) == s, terms[TOK * k : TOK * (k + 1)], 0.0)
        result = jnp.where(lane == k, jnp.sum(mine, axis=1, keepdims=True), result)
    gg_ref[...] = result.T[:8]


SMEM = pl.BlockSpec(memory_space=pltpu.SMEM)
VM = pl.BlockSpec(memory_space=pltpu.VMEM)


def sds(shape, dtype=BF):
    return jax.ShapeDtypeStruct(shape, dtype)


def whole(kernel, out_shape, in_specs, name, scratch=(), cost=None):
    multi = isinstance(out_shape, (list, tuple))
    return pl.pallas_call(
        kernel,
        out_shape=out_shape,
        in_specs=in_specs,
        out_specs=[VM] * len(out_shape) if multi else VM,
        scratch_shapes=list(scratch),
        compiler_params=pltpu.CompilerParams(vmem_limit_bytes=VMEM_LIMITS.get(name, 14) * MIB),
        cost_estimate=cost,
        name=name,
    )


def shift_y(v, s):
    return lax.ppermute(v, "local", [(i, (i + 2 * s) % 8) for i in range(8)])


def swap_core(v):
    return lax.ppermute(v, "local", [(i, i ^ 1) for i in range(8)])


def node_exchange(v):
    shape = v.shape
    v = v.reshape(N_NODE, shape[0] // N_NODE, shape[1])
    return lax.all_to_all(v, "node", split_axis=0, concat_axis=0, tiled=True).reshape(shape)


def on_device(tokens, out_grads, routes, gate_values, gate_weight, up_weight, down_weight):
    w_gate = gate_weight[0]
    w_up = up_weight[0]
    w_down = down_weight[0]
    place = jnp.stack([lax.axis_index("node"), lax.axis_index("local") // 2]).astype(I32)

    dy_send = whole(send_dy_kernel, sds((ROWS_N, 1024)), [VM] * 3, "send_dy")(
        routes.T, gate_values.T, out_grads
    )
    dy_send, tokens = lax.optimization_barrier((dy_send, tokens))
    dy_mid = node_exchange(dy_send)
    picks = jnp.concatenate([routes.astype(BF), gate_values.astype(BF)], axis=1)
    x_own = jnp.concatenate([tokens, jnp.pad(picks, ((0, 0), (0, EXT - 16)))], axis=1)
    x_near = [x_own] + [shift_y(x_own, s) for s in (1, 2, 3)]

    x_send = whole(send_x_kernel, sds((384, 3584)), [SMEM] + [VM] * 4, "send_x")(place, *x_near)
    hbm = pl.BlockSpec(memory_space=pl.ANY)
    *dy_far, meta = whole(
        regroup_far_kernel,
        [sds((ROWS_Y, WIDTH))] * 3 + [sds((ROWS_N, 256))],
        [SMEM, VM],
        "regroup",
    )(place, dy_mid)
    dy_own, down_near = whole(
        regroup_own_kernel,
        [sds((ROWS_Y, WIDTH)), sds((HALF, WIDTH))],
        [SMEM, VM, hbm],
        "regroup_own",
        [pltpu.SemaphoreType.DMA((8,))],
    )(place, dy_mid, w_down)
    x_mine = node_exchange(x_send)
    dy_mine = [dy_own] + [shift_y(dy_far[s - 1], s) for s in (1, 2, 3)]
    dy_other = [swap_core(v) for v in dy_mine]
    back = whole(back_kernel, sds((2 * SLOTS, HALF), F32), [VM] * 9, "back")(
        *dy_mine, *dy_other, down_near
    )
    x_mine, back = lax.optimization_barrier((x_mine, back))
    x_other = swap_core(x_mine)
    pre_gate, pre_up, gate_near, up_near = whole(
        forward_own_kernel,
        [sds((SLOTS, HALF), F32)] * 2 + [sds((WIDTH, HALF))] * 2,
        [VM, hbm, hbm, hbm],
        "forward_own",
        [pltpu.SemaphoreType.DMA((4, 4))],
    )(x_mine, w_gate, w_up, back)
    d_gate, d_up, ext = whole(
        forward_kernel,
        [sds((2 * SLOTS, HALF)), sds((2 * SLOTS, HALF)), sds((2 * SLOTS, EXT))],
        [VM] * 6,
        "forward",
    )(x_other, gate_near, up_near, back, pre_gate, pre_up)

    def dx(part, width):
        return whole(
            functools.partial(dx_kernel, part),
            [sds((SLOTS, width))] * 2,
            [VM] * 5,
            "dx",
        )(d_gate, d_up, gate_near, up_near, ext)

    own_a, other_a = dx(0, A_WIDTH + EXT)
    own_b, other_b = dx(1, B_WIDTH)
    got_a = swap_core(other_a)
    got_b = swap_core(other_b)
    *pieces, mark = whole(
        add_kernel,
        [sds((ROWS_Y, A_WIDTH + EXT))] * 4 + [sds((8, 128), F32)],
        [VM] * 2,
        "add_halves",
    )(own_a, got_a)
    pieces = [pieces[0]] + [shift_y(pieces[s], -s) for s in (1, 2, 3)]
    sent_b, mark = whole(
        add_to_nodes_kernel, [sds((384, B_HALF)), sds((8, 128), F32)], [VM] * 3, "add_to_nodes"
    )(own_b, got_b, mark)
    table = whole(table_kernel, sds((128, 128), F32), [SMEM, VM, VM], "table")(place, meta, mark)
    back_b = node_exchange(sent_b)
    mixed = whole(
        combine_kernel,
        sds((ROWS_A, A_CHUNK)),
        [VM] * 5,
        "combine",
        [pltpu.VMEM((ROWS_A, A_CHUNK), F32)],
        pl.CostEstimate(flops=20_000_000_000, bytes_accessed=70_000_000, transcendentals=0),
    )(table, *pieces)
    mixed, back_b = lax.optimization_barrier((mixed, back_b))
    back_a = node_exchange(mixed)
    near = whole(combine_near_kernel, [sds((TOK, B_WIDTH))] * 4, [SMEM] + [VM] * 5, "combine_near")(
        place, *x_near, back_b
    )
    near = [near[0]] + [shift_y(near[s], -s) for s in (1, 2, 3)]
    input_grads, gate_grads = whole(
        finish_kernel, [sds((TOK, WIDTH)), sds((8, TOK), F32)], [SMEM] + [VM] * 6, "finish"
    )(place, routes.T, back_a, *near)
    return input_grads, gate_grads.T


def solution(mesh):
    row = P(("node", "local"), None)
    weight = P(("node", "local"), None, None)
    return jax.shard_map(
        on_device,
        mesh=mesh,
        in_specs=(row, row, row, row, weight, weight, weight),
        out_specs=(row, row),
        check_vma=False,
    )
```

```python
import functools

import jax
import jax.numpy as jnp
from jax import lax
from jax.experimental import pallas as pl
from jax.experimental.pallas import tpu as pltpu
from jax.sharding import PartitionSpec as P

BF = jnp.bfloat16
F32 = jnp.float32
I32 = jnp.int32

N_NODE = 16
N_Y = 4
TOK = 16
CAP_NODE = 5
CAP_EXP = 3
WIDTH = 7168
HALF = 512
ROWS_Y = N_NODE * CAP_EXP
SLOTS = N_Y * ROWS_Y
ROWS_N = N_NODE * 40
EXT = 128
A_PARTS = 15
A_CHUNK = 256
A_WIDTH = A_PARTS * A_CHUNK
A_BLOCK = 5 * (A_PARTS + 1)
ROWS_A = N_NODE * A_BLOCK
B_WIDTH = WIDTH - A_WIDTH
B_HALF = B_WIDTH // 2
MIB = 1024 * 1024
VMEM_LIMITS = {"send_dy": 60, "regroup_own": 24, "back": 20, "forward_own": 30, "forward": 30, "dx": 24}


def iota(shape, dim):
    return lax.broadcasted_iota(I32, shape, dim)


def div3(v):
    return (v * 171) >> 9


def div5(v):
    return (v * 205) >> 10


def div40(v):
    return div5(v >> 3)


def dot(a, b):
    return jnp.dot(a, b, preferred_element_type=F32)


def dot_nt(a, b):
    return lax.dot_general(a, b, (((1,), (1,)), ((), ())), preferred_element_type=F32)


def dot_tn(a, b):
    return lax.dot_general(a, b, (((0,), (0,)), ((), ())), preferred_element_type=F32)


def onehot(mask):
    return jnp.where(mask, 1.0, 0.0)


def by_token(v):
    return dot_tn(v.astype(F32).astype(BF), onehot(iota((8, 128), 0) == iota((8, 128), 1)).astype(BF))


def route_tables(routes, width):
    lane = (iota((TOK, width), 1) & 63).astype(F32)
    hot = jnp.zeros((TOK, width), F32)
    for k in range(8):
        hot = hot + onehot(routes[:, k : k + 1] == lane)
    return hot


def node_codes(hot):
    width = hot.shape[1]
    row = iota((width, 128), 0)
    group = onehot((row < 64) & ((row >> 2) == iota((width, 128), 1))).astype(BF)
    used = jnp.minimum(dot(hot.astype(BF), group), 1.0)
    tri = onehot(iota((TOK, TOK), 1) < iota((TOK, TOK), 0)).astype(BF)
    return used * (dot(tri, used.astype(BF)) + 1.0)


def send_dy_kernel(routes_ref, gates_ref, dy_ref, out_ref):
    routes = by_token(routes_ref[...])
    gates = by_token(gates_ref[...])
    width = 256
    lane = iota((TOK, width), 1)
    expert = (lane & 63).astype(F32)
    hot = route_tables(routes, width)
    gate = jnp.zeros((TOK, width), F32)
    for k in range(8):
        gate = gate + jnp.where(routes[:, k : k + 1] == expert, gates[:, k : k + 1], 0.0)
    tri = onehot(iota((TOK, TOK), 1) < iota((TOK, TOK), 0)).astype(BF)
    code = hot * (dot(tri, hot.astype(BF)) + 1.0)
    section = lane >> 6
    meta = jnp.where(section == 0, code, jnp.where(section == 1, gate, 0.0)).astype(BF)
    meta = jnp.concatenate([meta, jnp.zeros((TOK, 1024 - width), BF)], axis=1)
    stack = jnp.concatenate([dy_ref[:, 1024 * q : 1024 * (q + 1)] for q in range(7)] + [meta], axis=0)
    ncode = node_codes(hot)
    spread = onehot((iota((TOK, 128), 1) & 15) == iota((TOK, 128), 0)).astype(BF)
    ncode_lane = dot_tn(ncode.astype(BF), spread)[:N_NODE]
    chunk = (iota((N_NODE, 128), 1) >> 4).astype(F32)
    key = jnp.where(ncode_lane > 0.0, 8.0 * chunk + ncode_lane, -1.0)
    row = iota((40, 128), 0)
    q = div5(row)
    row_key = (8 * q + (row - 5 * q) + 1).astype(F32)
    pick = jnp.concatenate([onehot(row_key == key[n : n + 1, :]) for n in range(N_NODE)], axis=0)
    out_ref[...] = dot(pick.astype(BF), stack).astype(BF)


def send_x_kernel(place_ref, x0_ref, x1_ref, x2_ref, x3_ref, out_ref):
    y = place_ref[1]
    xs = [x0_ref, x1_ref, x2_ref, x3_ref]
    code, _ = near_tables(y, xs)
    lane = iota((64, 128), 1)
    spread = onehot((lane & 63) == iota((64, 128), 0)).astype(BF)
    code_lane = dot_tn(code.astype(BF), spread)[:N_NODE]
    block = (iota((N_NODE, 128), 1) >> 4).astype(F32)
    key = jnp.where(code_lane > 0.0, 4.0 * block + code_lane, -1.0)
    row = iota((24, 128), 0)
    b = div3(row)
    row_key = (4 * b + (row - 3 * b) + 1).astype(F32)
    pick = jnp.concatenate([onehot(row_key == key[n : n + 1, :]) for n in range(N_NODE)], axis=0).astype(BF)
    for i in range(7):
        lo = 512 * i
        stack = jnp.concatenate(
            [r[:, lo : lo + 512] for r in xs] + [r[:, 3584 + lo : 3584 + lo + 512] for r in xs], axis=0
        )
        out_ref[:, lo : lo + 512] = dot(pick, stack).astype(BF)


def copy_parts(source, target, sems, first, rows):
    copies = []
    step = rows // sems.shape[0]
    for i in range(sems.shape[0]):
        at = pl.ds(first + step * i, step)
        copies.append(pltpu.make_async_copy(source.at[at], target.at[at], sems.at[i]))
        copies[-1].start()
    return copies


def wait_all(copies):
    for copy in copies:
        copy.wait()


def regroup(shifts, place_ref, rows_ref, outs):
    c = iota((256, 128), 1)
    want = ((c >> 2) << 6) + 4 * place_ref[0] + ((place_ref[1] + c) & 3)
    select = onehot((c < 8) & (iota((256, 128), 0) == want)).astype(BF)
    code = lax.dot_general(
        select, rows_ref[:, :256], (((0,), (1,)), ((), ())), preferred_element_type=F32
    )[:8]
    col = iota((8, ROWS_N), 1)
    n = div40(col)
    key = jnp.where((col - 40 * n >= 35) & (code > 0.0), 4.0 * n.astype(F32) + code, -1.0)
    row = iota((ROWS_Y, ROWS_N), 0)
    rn = div3(row)
    row_key = (4 * rn + (row - 3 * rn) + 1).astype(F32)
    for q in range(7):
        key_q = pltpu.roll(key, ROWS_N - (35 - 5 * q), 1)
        pick = jnp.concatenate([onehot(row_key == key_q[s : s + 1, :]) for s in shifts], axis=0)
        moved = dot(pick.astype(BF), rows_ref[...]).astype(BF)
        for i, out in enumerate(outs):
            out[:, 1024 * q : 1024 * (q + 1)] = moved[ROWS_Y * i : ROWS_Y * (i + 1)]


def regroup_far_kernel(place_ref, rows_ref, out1_ref, out2_ref, out3_ref, meta_ref):
    meta_ref[...] = rows_ref[:, :256]
    regroup((1, 2, 3), place_ref, rows_ref, [out1_ref, out2_ref, out3_ref])


def regroup_own_kernel(place_ref, rows_ref, down_hbm, out_ref, down_ref, sems):
    loads = copy_parts(down_hbm, down_ref, sems, 0, HALF)
    regroup((0,), place_ref, rows_ref, [out_ref])
    wait_all(loads)


def table_kernel(place_ref, meta_ref, mark_ref, table_ref):
    c = iota((256, 128), 1)
    want = ((c >> 2) << 6) + 4 * place_ref[0] + ((place_ref[1] + c) & 3)
    select = onehot((c < 8) & (iota((256, 128), 0) == want)).astype(BF)
    picked = dot(meta_ref[...], select).astype(BF)
    r = iota((128, ROWS_N), 0)
    j = r & 7
    source = jnp.where(j < CAP_NODE, 40 * (r >> 3) + 35 + j, -1)
    table_ref[...] = dot(onehot(iota((128, ROWS_N), 1) == source).astype(BF), picked)


def back_kernel(*refs):
    pieces, down_ref, out_ref = refs[:4], refs[4], refs[5]
    rows = jnp.concatenate([p[...] for p in pieces], axis=0)
    out_ref[...] = dot_nt(rows, down_ref[...])


def slot_order(h):
    row = iota((SLOTS, 384), 0)
    s = div3(row >> 4)
    rem = row - ROWS_Y * s
    n = div3(rem)
    r = rem - 3 * n
    return onehot(iota((SLOTS, 384), 1) == 24 * n + 12 * h + 3 * s + r).astype(BF)


def forward_own_kernel(x_ref, gate_hbm, up_hbm, mark_ref, pg_ref, pu_ref, gate_ref, up_ref, sems):
    loads = []
    for h in range(2):
        loads.append(copy_parts(gate_hbm, gate_ref, sems.at[2 * h], 3584 * h, 3584))
        loads.append(copy_parts(up_hbm, up_ref, sems.at[2 * h + 1], 3584 * h, 3584))
    for h in range(2):
        rows = dot(slot_order(h), x_ref[...]).astype(BF)
        at = slice(3584 * h, 3584 * (h + 1))
        wait_all(loads[2 * h])
        gate = dot(rows, gate_ref[at, :])
        wait_all(loads[2 * h + 1])
        up = dot(rows, up_ref[at, :])
        pg_ref[...] = gate if h == 0 else pg_ref[...] + gate
        pu_ref[...] = up if h == 0 else pu_ref[...] + up


def forward_kernel(
    x_ref, gate_ref, up_ref, back_ref, back2_ref, pg_ref, pu_ref, dgate_ref, dup_ref, ext_ref
):
    pre_gate = jnp.zeros((SLOTS, HALF), F32)
    pre_up = jnp.zeros((SLOTS, HALF), F32)
    for h in range(2):
        rows = dot(slot_order(h), x_ref[...]).astype(BF)
        at = slice(3584 * h, 3584 * (h + 1))
        pre_gate = pre_gate + dot(rows, gate_ref[at, :])
        pre_up = pre_up + dot(rows, up_ref[at, :])
    pre_gate = jnp.concatenate([pg_ref[...], pre_gate], axis=0)
    pre_up = jnp.concatenate([pu_ref[...], pre_up], axis=0)
    back = jnp.concatenate([back_ref[...], back2_ref[...]], axis=0)
    sig = jax.nn.sigmoid(pre_gate)
    act = pre_gate * sig
    hidden = (act * pre_up).astype(BF)
    part = jnp.sum(hidden.astype(F32) * back, axis=1, keepdims=True)
    dgate_ref[...] = (back * pre_up * sig * (1.0 + pre_gate * (1.0 - sig))).astype(BF)
    dup_ref[...] = (back * act).astype(BF)
    high = part.astype(BF).astype(F32)
    low = part - high
    slot = iota((2 * SLOTS, EXT), 0)
    slot = jnp.where(slot >= SLOTS, slot - SLOTS, slot)
    at = 2 * div3(slot >> 4)
    lane = iota((2 * SLOTS, EXT), 1)
    ext_ref[...] = jnp.where(lane == at, high, jnp.where(lane == at + 1, low, 0.0)).astype(BF)


def dx_kernel(part, dgate_ref, dup_ref, gate_ref, up_ref, ext_ref, own_ref, other_ref):
    cols = slice(A_WIDTH, WIDTH) if part else slice(0, A_WIDTH)
    width = cols.stop - cols.start
    out = (dot_nt(dgate_ref[...], gate_ref[cols, :]) + dot_nt(dup_ref[...], up_ref[cols, :])).astype(BF)
    own_ref[:, :width] = out[:SLOTS]
    other_ref[:, :width] = out[SLOTS:]
    if part == 0:
        own_ref[:, A_WIDTH:] = ext_ref[:SLOTS]
        other_ref[:, A_WIDTH:] = ext_ref[SLOTS:]


def add_kernel(own_ref, got_ref, *outs):
    outs[4][...] = jnp.zeros_like(outs[4])
    lane = iota((ROWS_Y, EXT), 1)
    for s in range(N_Y):
        rows = slice(ROWS_Y * s, ROWS_Y * (s + 1))
        total = own_ref[rows, :A_WIDTH].astype(F32) + got_ref[rows, :A_WIDTH].astype(F32)
        outs[s][:, :A_WIDTH] = total.astype(BF)
        term = jnp.sum(
            own_ref[rows, A_WIDTH:].astype(F32) + got_ref[rows, A_WIDTH:].astype(F32), axis=1, keepdims=True
        )
        high = term.astype(BF).astype(F32)
        low = term - high
        outs[s][:, A_WIDTH:] = jnp.where(
            lane == 2 * s, high, jnp.where(lane == 2 * s + 1, low, 0.0)
        ).astype(BF)


def add_to_nodes_kernel(own_ref, got_ref, mark_ref, out_ref, mark_out):
    mark_out[...] = mark_ref[...]
    row = iota((384, 384), 0)
    block = div3(row >> 3)
    rest = row - 24 * block
    h = jnp.where(rest >= 12, 1, 0)
    rest = rest - 12 * h
    s = div3(rest)
    source = SLOTS * h + ROWS_Y * s + 3 * block + (rest - 3 * s)
    perm = onehot(iota((384, 384), 1) == source).astype(BF)
    total = (own_ref[...].astype(F32) + got_ref[...].astype(F32)).astype(BF)
    out_ref[...] = dot(perm, jnp.concatenate([total[:, :B_HALF], total[:, B_HALF:]], axis=0)).astype(BF)


def near_tables(y, xs):
    meta = jnp.concatenate([r[:, WIDTH : WIDTH + EXT] for r in xs], axis=0).astype(F32)
    lane = iota((64, 128), 1)
    wanted = jnp.where(lane < N_NODE, 4 * lane + y, -1).astype(F32)
    hot = jnp.zeros((64, 128), F32)
    gate = jnp.zeros((64, 128), F32)
    for k in range(8):
        here = meta[:, k : k + 1] == wanted
        hot = hot + onehot(here)
        gate = gate + jnp.where(here, meta[:, 8 + k : 9 + k], 0.0)
    r64 = iota((64, 64), 0)
    c64 = iota((64, 64), 1)
    tri = onehot((c64 < r64) & ((c64 >> 4) == (r64 >> 4))).astype(BF)
    return hot * (dot(tri, hot.astype(BF)) + 1.0), gate


def combine_near_kernel(place_ref, x0_ref, x1_ref, x2_ref, x3_ref, rows_ref, *outs):
    code, gate = near_tables(place_ref[1], [x0_ref, x1_ref, x2_ref, x3_ref])
    col = iota((128, 384), 1)
    spread = onehot(div3(col >> 3) == iota((128, 384), 0)).astype(BF)
    code = dot(code.astype(BF), spread)
    gate = dot(gate.astype(BF), spread)
    col = iota((64, 384), 1)
    rest = col - 24 * div3(col >> 3)
    half = jnp.where(rest >= 12, 1, 0)
    rest = rest - 12 * half
    s = div3(rest)
    match = (s == (iota((64, 384), 0) >> 4)) & (code == (rest - 3 * s + 1).astype(F32))
    for h in range(2):
        weight = jnp.where(match & (half == h), gate, 0.0).astype(BF)
        total = dot(weight, rows_ref[...]).astype(BF)
        for s in range(N_Y):
            outs[s][:, B_HALF * h : B_HALF * (h + 1)] = total[TOK * s : TOK * (s + 1)]


def combine_kernel(table_ref, p0_ref, p1_ref, p2_ref, p3_ref, out_ref, rows_ref):
    pieces = [p0_ref, p1_ref, p2_ref, p3_ref]
    lane = iota((128, SLOTS), 1)
    ls = div3(lane >> 4)
    rem = lane - ROWS_Y * ls
    ln = div3(rem)
    lr = rem - 3 * ln
    table = table_ref[...]
    code = jnp.zeros((128, SLOTS), F32)
    gate = jnp.zeros((128, SLOTS), F32)
    for s in range(N_Y):
        code = jnp.where(ls == s, table[:, s : s + 1], code)
        gate = jnp.where(ls == s, table[:, 4 + s : 5 + s], gate)
    match = ((iota((128, SLOTS), 0) >> 3) == ln) & (code == (lr + 1).astype(F32))
    weight = jnp.where(match, gate, 0.0).astype(BF)
    ext = jnp.concatenate([p[:, A_WIDTH:] for p in pieces], axis=0)
    terms = dot(onehot(match).astype(BF), ext)
    terms = jnp.concatenate([terms, jnp.zeros((128, A_CHUNK - EXT), F32)], axis=1)
    for q in range(A_PARTS):
        total = dot(weight, jnp.concatenate([p[:, A_CHUNK * q : A_CHUNK * (q + 1)] for p in pieces], axis=0))
        for n in range(N_NODE):
            at = A_BLOCK * n + 5 * q
            rows_ref[at : at + 8, :] = total[8 * n : 8 * n + 8]
    for n in range(N_NODE):
        rows_ref[A_BLOCK * (n + 1) - 5 : A_BLOCK * (n + 1), :] = terms[8 * n : 8 * n + 5]
    out_ref[...] = rows_ref[...].astype(BF)


def finish_kernel(place_ref, routes_ref, a_ref, b0_ref, b1_ref, b2_ref, b3_ref, dx_ref, gg_ref):
    y = place_ref[1]
    routes = by_token(routes_ref[...])
    ncode = node_codes(route_tables(routes, 128))
    col = iota((128, ROWS_A), 1)
    spread = onehot(div5(col >> 4) == iota((128, ROWS_A), 0)).astype(BF)
    code = dot(ncode.astype(BF), spread)
    col = iota((TOK, ROWS_A), 1)
    cn = div5(col >> 4)
    cp = col - A_BLOCK * cn
    cq = div5(cp)
    match = code == (cp - 5 * cq + 1).astype(F32)
    pick = jnp.concatenate([onehot(match & (cq == q)) for q in range(A_PARTS)], axis=0).astype(BF)
    total = dot(pick, a_ref[...]).astype(BF)
    for q in range(A_PARTS):
        dx_ref[:, A_CHUNK * q : A_CHUNK * (q + 1)] = total[TOK * q : TOK * (q + 1)]
    total = b0_ref[...].astype(F32) + b1_ref[...].astype(F32)
    total = total + b2_ref[...].astype(F32) + b3_ref[...].astype(F32)
    dx_ref[:, A_WIDTH:] = total.astype(BF)
    last = match & (cq == A_PARTS)
    picks = routes.astype(I32)
    masks = jnp.concatenate(
        [onehot(last & (cn == (picks[:, k : k + 1] >> 2))) for k in range(8)], axis=0
    ).astype(BF)
    terms = dot(masks, a_ref[:, :EXT])
    lane = iota((TOK, EXT), 1)
    result = jnp.zeros((TOK, EXT), F32)
    for k in range(8):
        s = ((picks[:, k : k + 1] & 3) - y) & 3
        mine = jnp.where((lane >> 1) == s, terms[TOK * k : TOK * (k + 1)], 0.0)
        result = jnp.where(lane == k, jnp.sum(mine, axis=1, keepdims=True), result)
    gg_ref[...] = result.T[:8]


SMEM = pl.BlockSpec(memory_space=pltpu.SMEM)
VM = pl.BlockSpec(memory_space=pltpu.VMEM)


def sds(shape, dtype=BF):
    return jax.ShapeDtypeStruct(shape, dtype)


def whole(kernel, out_shape, in_specs, name, scratch=(), cost=None):
    multi = isinstance(out_shape, (list, tuple))
    return pl.pallas_call(
        kernel,
        out_shape=out_shape,
        in_specs=in_specs,
        out_specs=[VM] * len(out_shape) if multi else VM,
        scratch_shapes=list(scratch),
        compiler_params=pltpu.CompilerParams(vmem_limit_bytes=VMEM_LIMITS.get(name, 14) * MIB),
        cost_estimate=cost,
        name=name,
    )


def shift_y(v, s):
    return lax.ppermute(v, "local", [(i, (i + 2 * s) % 8) for i in range(8)])


def swap_core(v):
    return lax.ppermute(v, "local", [(i, i ^ 1) for i in range(8)])


def node_exchange(v):
    shape = v.shape
    v = v.reshape(N_NODE, shape[0] // N_NODE, shape[1])
    return lax.all_to_all(v, "node", split_axis=0, concat_axis=0, tiled=True).reshape(shape)


def on_device(tokens, out_grads, routes, gate_values, gate_weight, up_weight, down_weight):
    w_gate = gate_weight[0]
    w_up = up_weight[0]
    w_down = down_weight[0]
    place = jnp.stack([lax.axis_index("node"), lax.axis_index("local") // 2]).astype(I32)

    dy_send = whole(send_dy_kernel, sds((ROWS_N, 1024)), [VM] * 3, "send_dy")(
        routes.T, gate_values.T, out_grads
    )
    dy_send, tokens = lax.optimization_barrier((dy_send, tokens))
    dy_mid = node_exchange(dy_send)
    picks = jnp.concatenate([routes.astype(BF), gate_values.astype(BF)], axis=1)
    x_own = jnp.concatenate([tokens, jnp.pad(picks, ((0, 0), (0, EXT - 16)))], axis=1)
    x_near = [x_own] + [shift_y(x_own, s) for s in (1, 2, 3)]

    x_send = whole(send_x_kernel, sds((384, 3584)), [SMEM] + [VM] * 4, "send_x")(place, *x_near)
    hbm = pl.BlockSpec(memory_space=pl.ANY)
    *dy_far, meta = whole(
        regroup_far_kernel,
        [sds((ROWS_Y, WIDTH))] * 3 + [sds((ROWS_N, 256))],
        [SMEM, VM],
        "regroup",
    )(place, dy_mid)
    dy_own, down_near = whole(
        regroup_own_kernel,
        [sds((ROWS_Y, WIDTH)), sds((HALF, WIDTH))],
        [SMEM, VM, hbm],
        "regroup_own",
        [pltpu.SemaphoreType.DMA((8,))],
    )(place, dy_mid, w_down)
    x_mine = node_exchange(x_send)
    dy_mine = [dy_own] + [shift_y(dy_far[s - 1], s) for s in (1, 2, 3)]
    dy_other = [swap_core(v) for v in dy_mine]
    back = whole(back_kernel, sds((SLOTS, HALF), F32), [VM] * 5, "back")
    back_own = back(*dy_mine, down_near)
    back_other = back(*dy_other, down_near)
    x_mine, back_own, back_other = lax.optimization_barrier((x_mine, back_own, back_other))
    x_other = swap_core(x_mine)
    pre_gate, pre_up, gate_near, up_near = whole(
        forward_own_kernel,
        [sds((SLOTS, HALF), F32)] * 2 + [sds((WIDTH, HALF))] * 2,
        [VM, hbm, hbm, hbm],
        "forward_own",
        [pltpu.SemaphoreType.DMA((4, 4))],
    )(x_mine, w_gate, w_up, back_other)
    d_gate, d_up, ext = whole(
        forward_kernel,
        [sds((2 * SLOTS, HALF)), sds((2 * SLOTS, HALF)), sds((2 * SLOTS, EXT))],
        [VM] * 7,
        "forward",
    )(x_other, gate_near, up_near, back_own, back_other, pre_gate, pre_up)

    def dx(part, width):
        return whole(
            functools.partial(dx_kernel, part),
            [sds((SLOTS, width))] * 2,
            [VM] * 5,
            "dx",
        )(d_gate, d_up, gate_near, up_near, ext)

    own_a, other_a = dx(0, A_WIDTH + EXT)
    own_b, other_b = dx(1, B_WIDTH)
    got_a = swap_core(other_a)
    got_b = swap_core(other_b)
    *pieces, mark = whole(
        add_kernel,
        [sds((ROWS_Y, A_WIDTH + EXT))] * 4 + [sds((8, 128), F32)],
        [VM] * 2,
        "add_halves",
    )(own_a, got_a)
    pieces = [pieces[0]] + [shift_y(pieces[s], -s) for s in (1, 2, 3)]
    sent_b, mark = whole(
        add_to_nodes_kernel, [sds((384, B_HALF)), sds((8, 128), F32)], [VM] * 3, "add_to_nodes"
    )(own_b, got_b, mark)
    table = whole(table_kernel, sds((128, 128), F32), [SMEM, VM, VM], "table")(place, meta, mark)
    back_b = node_exchange(sent_b)
    mixed = whole(
        combine_kernel,
        sds((ROWS_A, A_CHUNK)),
        [VM] * 5,
        "combine",
        [pltpu.VMEM((ROWS_A, A_CHUNK), F32)],
        pl.CostEstimate(flops=20_000_000_000, bytes_accessed=70_000_000, transcendentals=0),
    )(table, *pieces)
    mixed, back_b = lax.optimization_barrier((mixed, back_b))
    back_a = node_exchange(mixed)
    near = whole(combine_near_kernel, [sds((TOK, B_WIDTH))] * 4, [SMEM] + [VM] * 5, "combine_near")(
        place, *x_near, back_b
    )
    near = [near[0]] + [shift_y(near[s], -s) for s in (1, 2, 3)]
    input_grads, gate_grads = whole(
        finish_kernel, [sds((TOK, WIDTH)), sds((8, TOK), F32)], [SMEM] + [VM] * 6, "finish"
    )(place, routes.T, back_a, *near)
    return input_grads, gate_grads.T


def solution(mesh):
    row = P(("node", "local"), None)
    weight = P(("node", "local"), None, None)
    return jax.shard_map(
        on_device,
        mesh=mesh,
        in_specs=(row, row, row, row, weight, weight, weight),
        out_specs=(row, row),
        check_vma=False,
    )
```
